32 devices in a mesh: dp: 2 (over x), context: 4 (over z), tensor: 4 (over y, core).
Axes of the slice: x: 2, y: 2, z: 4, core: 2. Of those that a mesh axis runs over, the one named last changes fastest.
Arguments:
- streams: bfloat16 [2048, 3, 8192], P(('dp', 'context'), None, 'tensor'), parts along dimension 0, may hold values from -6 to 6
- short_filter: float32 [3, 3, 8192], P(None, None, 'tensor'), may hold values from -3 to 3
- decay_rate: float32 [8192, 16], P('tensor'), as said below
- residue: float32 [8192, 16], P('tensor'), may hold values from -0.26 to 0.26
- bias: float32 [8192], P('tensor'), may hold values from -4 to 4
Outputs:
- gated: bfloat16 [2048, 8192], P(('dp', 'context'), 'tensor'), parts along dimension 0
The draws below stay inside these ranges and needn't reach their ends.
There are 2 independent parts, one for each index of `dp`. The reference program is written for one: setup_inputs(seed, part) draws one part's arguments, and reference() takes and returns one part's arrays. A program takes and returns all parts, laid end to end along the dimension named above; an argument that names none is the same for every part. Nothing has to cross between parts.
Inputs may be any that keep to these rules, and one draw needn't show every extreme that they name: `decay_rate`: positive.
All inputs are finite; a program needn't handle non-finite values.
Results may differ from the reference program's by a relative error of at most 0.0058.
Values may be sent and summed in bfloat16 or wider, within the bound.
No kernel may reach another device: no remote copies, remote signals or barrier semaphores. Data moves between devices by JAX's collectives and lax.ppermute only.
A program may use at most 384 MiB of HBM per device.

```python
import jax
import jax.numpy as jnp
from jax import lax

D = 8192
MODES = 16
SEQ = 1024


def mode_table(key):
    rate_key, residue_key = jax.random.split(jax.random.fold_in(key, 29))
    lowest = min(0.5 / SEQ, 1.0 / 60.0)
    highest = 1.0 / 30.0
    spread = jax.random.uniform(rate_key, (D, MODES), jnp.float32)
    rate = jnp.exp(jnp.log(lowest) + spread * (jnp.log(highest) - jnp.log(lowest)))
    noise = jnp.clip(jax.random.normal(residue_key, (D, MODES), jnp.float32), -4.0, 4.0)
    weights = noise * jnp.sqrt(1.0 - jnp.exp(-2.0 * rate)) / jnp.sqrt(jnp.float32(MODES))
    return (rate, weights)


def draw_decay_rate(key, part):
    return mode_table(key)[0]


def draw_residue(key, part):
    return mode_table(key)[1]


def levels(stream_key, shape, shards, smallest, top_value):
    def one(axis_at, blocks):
        draws = jax.random.uniform(jax.random.fold_in(jax.random.fold_in(stream_key, 6), axis_at), (blocks,), jnp.float32, smallest / len(shards), top_value / len(shards))
        return jnp.repeat(jnp.exp(draws), shape[axis_at] // blocks).reshape((-1,) + (1,) * (len(shape) - axis_at - 1))

    factor_of = one(*shards[0])
    for cut in shards[1:]:
        factor_of = factor_of * one(*cut)
    return factor_of


def normal_values(own_key, shape, deviation, bound, shards=(), kind=jnp.bfloat16):
    array = deviation * jax.random.normal(own_key, shape, jnp.float32)
    if shards:
        array = array * levels(own_key, shape, shards, -0.22, 0.18)
    return jnp.clip(array, -bound, bound).astype(kind)


def setup_inputs(seed: int = 0, part: int = 0) -> dict:
    seeds = jax.random.split(jax.random.key(seed), 6)
    part_splits = jax.random.split(jax.random.fold_in(seeds[5], part), 6)
    return {
        "streams": normal_values(part_splits[0], (SEQ, 3, D), 1.0, 6.0, ((0, 4), (2, 4))),
        "short_filter": normal_values(seeds[1], (3, 3, D), 0.6, 3.0, ((2, 4),), jnp.float32),
        "decay_rate": draw_decay_rate(jax.random.fold_in(seeds[5], 71), part),
        "residue": draw_residue(jax.random.fold_in(seeds[5], 71), part),
        "bias": normal_values(seeds[4], (D,), 1.0, 4.0, ((0, 4),), jnp.float32),
    }


def featurize(raw, weights):
    padded = jnp.pad(raw, ((2, 0), (0, 0)))
    return weights[0] * raw + weights[1] * padded[1:-1] + weights[2] * padded[:-2]


def reference(streams, short_filter, decay_rate, residue, bias):
    values = streams.astype(jnp.float32)
    query = featurize(values[:, 0], short_filter[0])
    keyf = featurize(values[:, 1], short_filter[1])
    valuef = featurize(values[:, 2], short_filter[2])
    key_value = lax.optimization_barrier((keyf * valuef).astype(jnp.bfloat16))
    widened = key_value.astype(jnp.float32)
    length = widened.shape[0]
    fft_len = 2 * length
    per_map = 64 if D % 64 == 0 else D
    map_count = D // per_map
    positions = jnp.arange(length, dtype=jnp.float32)
    grouped = widened.reshape(length, map_count, per_map).transpose(1, 0, 2)
    rate_rows = decay_rate.reshape(map_count, per_map, MODES)
    residue_rows = residue.reshape(map_count, per_map, MODES)

    def filter_block(member):
        signal, rates, residues = member
        filter_taps = jnp.sum(residues[None] * jnp.exp(-positions[:, None, None] * rates[None]), axis=2)
        spectrum = jnp.fft.rfft(signal, n=fft_len, axis=0)
        response = jnp.fft.rfft(filter_taps, n=fft_len, axis=0)
        return jnp.fft.irfft(spectrum * response, n=fft_len, axis=0)[:length]

    convolved = lax.map(filter_block, (grouped, rate_rows, residue_rows))
    convolved = convolved.transpose(1, 0, 2).reshape(length, D).astype(jnp.float32)
    mixed = lax.optimization_barrier((convolved + bias * widened).astype(jnp.bfloat16))
    return (query * mixed.astype(jnp.float32)).astype(jnp.bfloat16)
```

```python
import functools

import jax
import jax.numpy as jnp
from jax import lax
from jax.experimental import pallas as pl
from jax.experimental.pallas import tpu as pltpu
from jax.sharding import PartitionSpec as P

F32 = jnp.float32
BF16 = jnp.bfloat16
LANES = 128
SUB = 8
GROUP = LANES * SUB
CHUNK = 16
PAD = 8


def total(values):
    values = list(values)
    while len(values) > 1:
        pairs = [values[i] + values[i + 1] for i in range(0, len(values) - 1, 2)]
        values = pairs + ([values[-1]] if len(values) % 2 else [])
    return values[0]


def lay_rows(scratch, stride, source, rows, base=0):
    for j in range(SUB):
        scratch[pl.ds(j * stride + base, rows), :] = source(j)


def row(scratch, stride, t):
    return scratch[pl.ds(t, SUB, stride=stride), :]


def lanes(j):
    return pl.ds(j * LANES, LANES)


def state_kernel(k_ref, v_ref, w_ref, rate_ref, kv_ref, states_ref, end_ref, rate_out_ref, ks, vs, small, power):
    tokens, modes = k_ref.shape[1], rate_ref.shape[0]
    stride = tokens + PAD
    small_stride = modes + PAD
    lay_rows(ks, stride, lambda j: k_ref[0, :, lanes(j)].astype(F32), tokens)
    lay_rows(vs, stride, lambda j: v_ref[0, :, lanes(j)].astype(F32), tokens)
    lay_rows(small, small_stride, lambda j: rate_ref[:, lanes(j)], modes)
    p = []
    for m in range(modes):
        rate = row(small, small_stride, m)
        rate_out_ref[0, m] = rate
        p.append(jnp.exp(-rate))
        power[m] = jnp.exp(-CHUNK * rate)
        end_ref[0, m] = jnp.zeros((SUB, LANES), F32)
    for stream in (1, 2):
        lay_rows(small, small_stride, lambda j: w_ref[stream, :, lanes(j)], 3, base=3 * (stream - 1))
    wk = [row(small, small_stride, i) for i in range(3)]
    wv = [row(small, small_stride, 3 + i) for i in range(3)]

    def chunk(c, carry):
        k1, k2, v1, v2 = carry
        acc = None
        for i in range(CHUNK):
            t = c * CHUNK + i
            k, v = row(ks, stride, t), row(vs, stride, t)
            key = wk[0] * k + wk[1] * k1 + wk[2] * k2
            value = wv[0] * v + wv[1] * v1 + wv[2] * v2
            k1, k2, v1, v2 = k, k1, v, v1
            product = (key * value).astype(BF16).astype(F32)
            if i < 2:
                product = jnp.where(c > 0, product, 0.0)
            kv_ref[0, t] = product
            acc = [product] * modes if acc is None else [a * b + product for a, b in zip(acc, p)]
        for m in range(modes):
            states_ref[0, c, m] = acc[m]
            end_ref[0, m] = end_ref[0, m] * power[m] + acc[m]
        return k1, k2, v1, v2

    zero = jnp.zeros((SUB, LANES), F32)
    lax.fori_loop(0, tokens // CHUNK, chunk, (zero,) * 4)


def near_kernel(q_ref, w_ref, rate_ref, residue_ref, bias_ref, kv_ref, near_ref, query_ref, gains_ref, qs, small, taps):
    tokens, modes = q_ref.shape[1], residue_ref.shape[0]
    stride = tokens + PAD
    small_stride = modes + PAD
    lay_rows(qs, stride, lambda j: q_ref[0, :, lanes(j)].astype(F32), tokens)
    lay_rows(small, small_stride, lambda j: residue_ref[:, lanes(j)], modes)
    lay_rows(small, small_stride, lambda j: bias_ref[:, lanes(j)], 1, base=modes)
    lay_rows(small, small_stride, lambda j: w_ref[0, :, lanes(j)], 3, base=modes + 1)
    bias = row(small, small_stride, modes)
    gains_ref[0, modes] = bias
    gain = []
    for m in range(modes):
        residue = row(small, small_stride, m)
        gains_ref[0, m] = residue
        gain.append(residue)
    p = [jnp.exp(-rate_ref[0, m]) for m in range(modes)]
    taps[0] = total(gain) + bias
    for i in range(1, CHUNK):
        gain = [a * b for a, b in zip(gain, p)]
        taps[i] = total(gain)
    w = [row(small, small_stride, modes + 1 + i) for i in range(3)]
    h = [taps[i] for i in range(CHUNK)]

    def chunk(c, carry):
        q1, q2 = carry
        window = []
        for i in range(CHUNK):
            t = c * CHUNK + i
            q = row(qs, stride, t)
            query_ref[0, t] = w[0] * q + w[1] * q1 + w[2] * q2
            q1, q2 = q, q1
            window.append(kv_ref[0, t])
            near_ref[0, t] = total(h[n] * window[i - n] for n in range(i + 1))
        return q1, q2

    zero = jnp.zeros((SUB, LANES), F32)
    lax.fori_loop(0, tokens // CHUNK, chunk, (zero, zero))


def emit_kernel(near_ref, query_ref, states_ref, entering_ref, rate_ref, gains_ref, rim_ref, out_ref, power, state, turned):
    tokens, modes = near_ref.shape[1], rate_ref.shape[1]
    stride = CHUNK + PAD
    p = []
    for m in range(modes):
        rate = rate_ref[0, m]
        p.append(jnp.exp(-rate))
        power[m] = jnp.exp(-CHUNK * rate)
        state[m] = entering_ref[0, m]
    kv0, kv1, query0, query1 = (rim_ref[i, 0] for i in range(4))

    def chunk(c, first):
        g = [gains_ref[0, m] * state[m] for m in range(modes)]
        for i in range(CHUNK):
            t = c * CHUNK + i
            g = [a * b for a, b in zip(g, p)]
            near, query = near_ref[0, t], query_ref[0, t]
            if first and i < 2:
                kv = (kv0, kv1)[i]
                g = [a + gains_ref[0, m] * kv for m, a in enumerate(g)]
                near = near + gains_ref[0, modes] * kv
                query = query + (query0, query1)[i]
            mixed = (near + total(g)).astype(BF16).astype(F32)
            turned[pl.ds(i, SUB, stride=stride), :] = query * mixed
        for m in range(modes):
            held = state[m]
            if first:
                held = (held * p[m] + kv0) * p[m] + kv1
                held = held * jnp.exp(-(CHUNK - 2) * rate_ref[0, m])
            else:
                held = held * power[m]
            state[m] = held + states_ref[0, c, m]
        rows = pl.ds(c * CHUNK if first else pl.multiple_of(c * CHUNK, CHUNK), CHUNK)
        for j in range(SUB):
            out_ref[rows, lanes(j)] = turned[pl.ds(j * stride, CHUNK), :].astype(BF16)

    chunk(0, True)

    def later(c, carry):
        chunk(c, False)
        return carry

    lax.fori_loop(1, tokens // CHUNK, later, 0)


def whole(shape):
    return pl.BlockSpec((1,) + shape[1:], lambda g: (g,) + (0,) * (len(shape) - 1))


def params():
    return pltpu.CompilerParams(vmem_limit_bytes=48 * 2**20)


def cost(flops, nbytes):
    return pl.CostEstimate(flops=flops, bytes_accessed=nbytes, transcendentals=0)


def body(streams, short_filter, decay_rate, residue, bias):
    tokens, _, channels = streams.shape
    modes = decay_rate.shape[1]
    groups = channels // GROUP
    chunks = tokens // CHUNK
    size = lax.axis_size("context")
    rank = lax.axis_index("context")
    by_stream = streams.transpose(1, 0, 2)
    rate_rows, residue_rows, bias_row = decay_rate.T, residue.T, bias.reshape(1, channels)

    ring = [(i, (i + 1) % size) for i in range(size)]
    rim = lax.ppermute(streams[-2:], "context", ring)

    def stream_spec(which):
        return pl.BlockSpec((1, tokens, GROUP), lambda g: (which, 0, g))

    def column_spec(rows):
        return pl.BlockSpec((rows, GROUP), lambda g: (0, g))

    filter_spec = pl.BlockSpec((3, 3, GROUP), lambda g: (0, 0, g))
    kv_shape = (groups, tokens, SUB, LANES)
    states_shape = (groups, chunks, modes, SUB, LANES)
    mode_shape = (groups, modes, SUB, LANES)
    gains_shape = (groups, modes + 1, SUB, LANES)
    shape = functools.partial(jax.ShapeDtypeStruct, dtype=F32)
    turn = pltpu.VMEM((SUB * (tokens + PAD), LANES), F32)
    small = pltpu.VMEM((SUB * (modes + PAD), LANES), F32)
    key_value, states, end, rate = pl.pallas_call(
        state_kernel,
        grid=(groups,),
        in_specs=[stream_spec(1), stream_spec(2), filter_spec, column_spec(modes)],
        out_specs=[whole(kv_shape), whole(states_shape), whole(mode_shape), whole(mode_shape)],
        out_shape=[shape(kv_shape), shape(states_shape), shape(mode_shape), shape(mode_shape)],
        scratch_shapes=[turn, turn, small, pltpu.VMEM((modes, SUB, LANES), F32)],
        compiler_params=params(),
        cost_estimate=cost(48 * tokens * channels, 6 * 2**20),
        name="states",
    )(by_stream, by_stream, short_filter, rate_rows)

    edge = jnp.where(rank == 0, 0.0, rim.astype(F32))
    head = streams[:2].astype(F32)
    rows = jnp.concatenate([edge, head], axis=0)
    features = [
        [
            short_filter[i, 0] * rows[2 + t, i] + short_filter[i, 1] * rows[1 + t, i] + short_filter[i, 2] * rows[t, i]
            for t in range(2)
        ]
        for i in (1, 2)
    ]
    kv_head = [lax.reduce_precision(features[0][t] * features[1][t], 8, 7) for t in range(2)]
    query_head = [
        short_filter[0, 1] * edge[1, 0] + short_filter[0, 2] * edge[0, 0],
        short_filter[0, 2] * edge[1, 0],
    ]
    tiled = [x.reshape(groups, SUB, LANES) for x in kv_head + query_head]
    rim_terms = jnp.stack(tiled)
    end = end + jnp.exp(-(tokens - 1.0) * rate) * tiled[0][:, None] + jnp.exp(-(tokens - 2.0) * rate) * tiled[1][:, None]

    entering = jnp.zeros_like(end)
    span = 1
    near = None
    while span < size:
        other = lax.ppermute(end, "context", [(i, i ^ span) for i in range(size)])
        if near is None:
            near, query, gains = pl.pallas_call(
                near_kernel,
                grid=(groups,),
                in_specs=[
                    stream_spec(0), filter_spec, whole(mode_shape), column_spec(modes), column_spec(1), whole(kv_shape),
                ],
                out_specs=[whole(kv_shape), whole(kv_shape), whole(gains_shape)],
                out_shape=[shape(kv_shape), shape(kv_shape), shape(gains_shape)],
                scratch_shapes=[
                    turn, pltpu.VMEM((SUB * (modes + 2 * PAD), LANES), F32), pltpu.VMEM((CHUNK, SUB, LANES), F32),
                ],
                compiler_params=params(),
                cost_estimate=cost(24 * tokens * channels, 7 * 2**20),
                name="near",
            )(by_stream, short_filter, rate, residue_rows, bias_row, key_value)
        right = (rank & span) != 0
        ahead = (rank & (span - 1)).astype(F32)
        entering = jnp.where(right, entering + jnp.exp(-(tokens * ahead) * rate) * other, entering)
        if 2 * span < size:
            late, early = jnp.where(right, end, other), jnp.where(right, other, end)
            end = late + jnp.exp(-(1.0 * tokens * span) * rate) * early
        span *= 2

    return pl.pallas_call(
        emit_kernel,
        grid=(groups,),
        in_specs=[
            whole(kv_shape), whole(kv_shape), whole(states_shape), whole(mode_shape), whole(mode_shape), whole(gains_shape),
            pl.BlockSpec((4, 1, SUB, LANES), lambda g: (0, g, 0, 0)),
        ],
        out_specs=pl.BlockSpec((tokens, GROUP), lambda g: (0, g)),
        out_shape=jax.ShapeDtypeStruct((tokens, channels), BF16),
        scratch_shapes=[
            pltpu.VMEM((modes, SUB, LANES), F32),
            pltpu.VMEM((modes, SUB, LANES), F32),
            pltpu.VMEM((SUB * (CHUNK + PAD), LANES), F32),
        ],
        compiler_params=params(),
        cost_estimate=cost(40 * tokens * channels, 7 * 2**20),
        name="emit",
    )(near, query, states, entering, rate, gains, rim_terms)


def solution(mesh):
    in_specs = (
        P(("dp", "context"), None, "tensor"),
        P(None, None, "tensor"),
        P("tensor", None),
        P("tensor", None),
        P("tensor"),
    )
    out_specs = P(("dp", "context"), "tensor")
    return jax.shard_map(body, mesh=mesh, in_specs=in_specs, out_specs=out_specs, check_vma=False)
```

```python
import functools

import jax
import jax.numpy as jnp
from jax import lax
from jax.experimental import pallas as pl
from jax.experimental.pallas import tpu as pltpu
from jax.sharding import PartitionSpec as P

F32 = jnp.float32
BF16 = jnp.bfloat16
LANES = 128
SUB = 8
GROUP = LANES * SUB
CHUNK = 16
PIECE = 64
STRIDE = CHUNK + 8
HEAD = 4
TAIL = 6


def total(values):
    values = list(values)
    while len(values) > 1:
        pairs = [values[i] + values[i + 1] for i in range(0, len(values) - 1, 2)]
        values = pairs + ([values[-1]] if len(values) % 2 else [])
    return values[0]


def column(g, j):
    return pl.ds(pl.multiple_of(g * GROUP + j * LANES, LANES), LANES)


def group_columns(g):
    return pl.ds(pl.multiple_of(g * GROUP, GROUP), GROUP)


def turn_in(source, turned, start, g):
    for j in range(SUB):
        turned[pl.ds(j * STRIDE, CHUNK), :] = source[pl.ds(start, CHUNK), column(g, j)].astype(F32)


def turn_rows(source, turned, rows, g):
    for j in range(SUB):
        turned[pl.ds(j * STRIDE, rows), :] = source[:, column(g, j)]


def row(turned, i):
    return turned[pl.ds(i, SUB, stride=STRIDE), :]


def state_kernel(
    streams, taps_hbm, rate_hbm, residue_hbm, bias_hbm,
    kv_ref, states_ref, own_ref, message_ref, tables_ref, q_ref,
    k_buf, v_buf, taps_buf, rate_buf, residue_buf, bias_buf, ka, kb, va, vb, table_sems, stream_sems, q_sem,
):
    tokens, modes = k_buf.shape[0], rate_buf.shape[0]
    groups = k_buf.shape[1] // GROUP
    pieces, chunks = tokens // PIECE, tokens // CHUNK

    def fetch(stream, g, n):
        rows = pl.ds(pl.multiple_of(n * PIECE, PIECE), PIECE)
        return pltpu.make_async_copy(
            streams.at[stream, rows, group_columns(g)],
            (k_buf, v_buf)[stream - 1].at[rows, group_columns(g)],
            stream_sems.at[stream - 1, g, n],
        )

    tables = [
        pltpu.make_async_copy(src, dst, table_sems.at[i])
        for i, (src, dst) in enumerate(
            [(rate_hbm, rate_buf), (taps_hbm, taps_buf), (residue_hbm, residue_buf), (bias_hbm, bias_buf)]
        )
    ]
    for copy in tables[:2]:
        copy.start()
    for g in range(groups):
        for n in range(pieces):
            fetch(1, g, n).start()
            fetch(2, g, n).start()
    fetch_q = pltpu.make_async_copy(streams.at[0], q_ref, q_sem)
    fetch_q.start()
    for copy in tables[2:]:
        copy.start()
    tables[0].wait()
    tables[1].wait()
    zero = jnp.zeros((SUB, LANES), F32)

    def one_group(g, none):
        turn_rows(rate_buf, ka, modes, g)
        for stream in range(3):
            turn_rows(taps_buf.at[stream], (kb, va, vb)[stream], 3, g)
        p = []
        for m in range(modes):
            rate = row(ka, m)
            tables_ref[g, m] = rate
            p.append(jnp.exp(-rate))
        w = []
        for i in range(9):
            w.append(row((kb, va, vb)[i // 3], i % 3))
            tables_ref[g, modes + i] = w[i]
        wk, wv = w[3:6], w[6:9]
        fetch(1, g, 0).wait()
        fetch(2, g, 0).wait()
        turn_in(k_buf, ka, 0, g)
        turn_in(v_buf, va, 0, g)
        for i in range(2):
            own_ref[g, modes + 2 * i] = row(ka, i)
            own_ref[g, modes + 2 * i + 1] = row(va, i)

        def one_chunk(c, ks, vs, acc, last):
            k1, k2, v1, v2 = last
            for m in range(modes):
                states_ref[g, c, m] = acc[m]
            for i in range(CHUNK):
                k, v = row(ks, i), row(vs, i)
                key = wk[0] * k + wk[1] * k1 + wk[2] * k2
                value = wv[0] * v + wv[1] * v1 + wv[2] * v2
                k1, k2, v1, v2 = k, k1, v, v1
                product = (key * value).astype(BF16).astype(F32)
                if i < 2:
                    product = jnp.where(c > 0, product, 0.0)
                kv_ref[g, c * CHUNK + i] = product
                acc = [a * b + product for a, b in zip(acc, p)]
            return acc, (k1, k2, v1, v2)

        def two_chunks(it, carry):
            acc, last = carry

            @pl.when(((it & 1) == 1) & (it < chunks // 2 - 1))
            def _():
                n = (it + 1) * 2 * CHUNK // PIECE
                fetch(1, g, n).wait()
                fetch(2, g, n).wait()

            c = 2 * it
            here = pl.multiple_of((c + 1) * CHUNK, CHUNK)
            turn_in(k_buf, kb, here, g)
            turn_in(v_buf, vb, here, g)
            acc, last = one_chunk(c, ka, va, acc, last)
            ahead = pl.multiple_of(jnp.minimum(c + 2, chunks - 1) * CHUNK, CHUNK)
            turn_in(k_buf, ka, ahead, g)
            turn_in(v_buf, va, ahead, g)
            return one_chunk(c + 1, kb, vb, acc, last)

        acc, last = lax.fori_loop(0, chunks // 2, two_chunks, ([zero] * modes, (zero,) * 4))
        for m in range(modes):
            own_ref[g, m] = acc[m]
        k1, k2, v1, v2 = last
        for i, value in ((1, k2), (2, v2), (4, k1), (5, v1)):
            own_ref[g, modes + HEAD + i] = value
        return none

    lax.fori_loop(0, groups, one_group, 0)
    fetch_q.wait()
    tables[2].wait()
    tables[3].wait()

    def rest(g, none):
        turn_rows(residue_buf, ka, modes, g)
        for m in range(modes):
            tables_ref[g, modes + 9 + m] = row(ka, m)
        tables_ref[g, 2 * modes + 9] = bias_buf[g]
        turn_in(q_ref, va, tokens - CHUNK, g)
        for i in range(2):
            own_ref[g, modes + HEAD + 3 * i] = row(va, CHUNK - 2 + i)
        pack(message_ref, g, [own_ref[g, i] for i in range(modes + HEAD + TAIL)])
        return none

    lax.fori_loop(0, groups, rest, 0)


def pack(message_ref, g, rows):
    for i in range(0, len(rows), 2):
        message_ref[g, i // 2] = jnp.concatenate(rows[i : i + 2], axis=0).astype(BF16)


def unpack(message_ref, g, first, count):
    rows = []
    for i in range(first // 2, (first + count) // 2):
        pair = message_ref[g, i].astype(F32)
        rows += [pair[:SUB], pair[SUB:]]
    return rows


def first_products(w, head, tail):
    features = []
    for s, rows in ((1, (tail[1], tail[4], head[0], head[2])), (2, (tail[2], tail[5], head[1], head[3]))):
        features.append([w[3 * s] * rows[2 + t] + w[3 * s + 1] * rows[1 + t] + w[3 * s + 2] * rows[t] for t in range(2)])
    return [(features[0][t] * features[1][t]).astype(BF16).astype(F32) for t in range(2)]


def first_terms(rate, products, steps):
    return jnp.exp((1.0 - steps) * rate) * products[0] + jnp.exp((2.0 - steps) * rate) * products[1]


def enter(tokens, span, rank, tables_ref, g, state, head, other, other_head, other_tail, entering):
    modes = len(other)
    rate = [tables_ref[g, m] for m in range(modes)]
    w = [tables_ref[g, modes + i] for i in range(9)]
    right = (rank & span) != 0
    ahead = rank & (span - 1)
    steps = (tokens * ahead).astype(F32)
    products = first_products(w, head, other_tail)
    result = []
    for m in range(modes):
        missing = jnp.where(ahead > 0, first_terms(rate[m], products, jnp.maximum(steps, 2.0)), 0.0)
        result.append(jnp.where(right, entering[m] + jnp.exp(-steps * rate[m]) * other[m] + missing, entering[m]))
    return result


def merge_kernel(span, tokens, own_ref, got_ref, tables_ref, entering_ref, rim_ref, *outs):
    next_ref, message_ref, entering_out, rim_out = outs
    groups = tables_ref.shape[0]
    modes = (tables_ref.shape[1] - 10) // 2
    rank = lax.axis_index("context")
    right = (rank & span) != 0
    ahead = rank & (span - 1)
    length = 1.0 * tokens * span
    zero = jnp.zeros((SUB, LANES), F32)

    def one_group(g, none):
        rate = [tables_ref[g, m] for m in range(modes)]
        w = [tables_ref[g, modes + i] for i in range(9)]
        state = [own_ref[g, m] for m in range(modes)]
        head = [own_ref[g, modes + i] for i in range(HEAD)]
        tail = [own_ref[g, modes + HEAD + i] for i in range(TAIL)]
        other = unpack(got_ref, g, 0, modes)
        other_head = unpack(got_ref, g, modes, HEAD)
        other_tail = unpack(got_ref, g, modes + HEAD, TAIL)

        def pick(a, b):
            return [jnp.where(right, x, y) for x, y in zip(a, b)]

        left_state, right_state = pick(other, state), pick(state, other)
        left_head, right_head = pick(other_head, head), pick(head, other_head)
        left_tail, right_tail = pick(other_tail, tail), pick(tail, other_tail)
        if span == 1:
            products = first_products(w, left_head, [zero] * TAIL)
            left_state = [
                a + jnp.where(rank < 2, first_terms(rate[m], products, length), 0.0) for m, a in enumerate(left_state)
            ]
        entering = [zero] * modes if entering_ref is None else [entering_ref[g, m] for m in range(modes)]
        entering = enter(tokens, span, rank, tables_ref, g, state, head, left_state, None, other_tail, entering)
        products = first_products(w, right_head, left_tail)
        rows = [
            right_state[m] + jnp.exp(-length * rate[m]) * left_state[m] + first_terms(rate[m], products, length)
            for m in range(modes)
        ]
        rows = rows + left_head + right_tail
        pack(message_ref, g, rows)
        for i, value in enumerate(rows):
            next_ref[g, i] = value
        for m in range(modes):
            entering_out[g, m] = entering[m]
        for i in range(TAIL):
            old = zero if rim_ref is None else rim_ref[g, i]
            rim_out[g, i] = jnp.where(right & (ahead == 0), other_tail[i], old)
        return none

    lax.fori_loop(0, groups, one_group, 0)


def near_kernel(q_ref, tables_ref, kv_ref, near_ref, query_ref, taps, qa, qb):
    tokens, groups = kv_ref.shape[1], kv_ref.shape[0]
    modes = (tables_ref.shape[1] - 10) // 2
    chunks = tokens // CHUNK
    zero = jnp.zeros((SUB, LANES), F32)

    def one_group(g, none):
        p = [jnp.exp(-tables_ref[g, m]) for m in range(modes)]
        gain = [tables_ref[g, modes + 9 + m] for m in range(modes)]
        taps[0] = total(gain) + tables_ref[g, 2 * modes + 9]
        for i in range(1, CHUNK):
            gain = [a * b for a, b in zip(gain, p)]
            taps[i] = total(gain)
        w = [tables_ref[g, modes + i] for i in range(3)]
        h = [taps[i] for i in range(CHUNK)]
        turn_in(q_ref, qa, 0, g)

        def one_chunk(c, qs, last):
            q1, q2 = last
            window = []
            for i in range(CHUNK):
                t = c * CHUNK + i
                q = row(qs, i)
                query_ref[g, t] = w[0] * q + w[1] * q1 + w[2] * q2
                q1, q2 = q, q1
                window.append(kv_ref[g, t])
                near_ref[g, t] = total(h[n] * window[i - n] for n in range(i + 1))
            return q1, q2

        def two_chunks(it, last):
            c = 2 * it
            turn_in(q_ref, qb, pl.multiple_of((c + 1) * CHUNK, CHUNK), g)
            last = one_chunk(c, qa, last)
            turn_in(q_ref, qa, pl.multiple_of(jnp.minimum(c + 2, chunks - 1) * CHUNK, CHUNK), g)
            return one_chunk(c + 1, qb, last)

        lax.fori_loop(0, chunks // 2, two_chunks, (zero, zero))
        return none

    lax.fori_loop(0, groups, one_group, 0)


def emit_kernel(
    span, near_ref, query_ref, states_ref, tables_ref, own_ref, merged_ref, got_ref, entering_ref, old_rim_ref,
    out_hbm, out_buf, power, state, rim_ref, ta, tb, out_sems,
):
    groups, tokens = near_ref.shape[:2]
    modes = (tables_ref.shape[1] - 10) // 2
    pieces, chunks = tokens // PIECE, tokens // CHUNK
    rank = lax.axis_index("context")

    def send(g, n):
        rows = pl.ds(pl.multiple_of(n * PIECE, PIECE), PIECE)
        return pltpu.make_async_copy(
            out_buf.at[rows, group_columns(g)], out_hbm.at[rows, group_columns(g)], out_sems.at[g, n]
        )

    def one_group(g, none):
        p = []
        for m in range(modes):
            rate = tables_ref[g, m]
            p.append(jnp.exp(-rate))
            power[m] = jnp.exp(-CHUNK * rate)
        w = [tables_ref[g, modes + i] for i in range(9)]
        other_tail = unpack(got_ref, g, modes + HEAD, TAIL)
        entering = enter(
            tokens, span, rank, tables_ref, g, None, [merged_ref[g, modes + i] for i in range(HEAD)],
            unpack(got_ref, g, 0, modes), None, other_tail, [entering_ref[g, m] for m in range(modes)],
        )
        for m in range(modes):
            state[m] = entering[m]
        begins = ((rank & span) != 0) & ((rank & (span - 1)) == 0)
        rim = [jnp.where(begins, other_tail[i], old_rim_ref[g, i]) for i in range(TAIL)]
        products = first_products(w, [own_ref[g, modes + i] for i in range(HEAD)], rim)
        rim_ref[0], rim_ref[1] = products
        rim_ref[2] = w[1] * rim[3] + w[2] * rim[0]
        rim_ref[3] = w[2] * rim[3]

        def one_chunk(c, turned, first):
            gains = [tables_ref[g, modes + 9 + m] for m in range(modes)]
            x = [gain * (states_ref[g, c, m] + state[m]) for m, gain in enumerate(gains)]
            for i in range(CHUNK):
                t = c * CHUNK + i
                x = [a * b for a, b in zip(x, p)]
                near, query = near_ref[g, t], query_ref[g, t]
                if first and i < 2:
                    x = [a + tables_ref[g, modes + 9 + m] * rim_ref[i] for m, a in enumerate(x)]
                    near = near + tables_ref[g, 2 * modes + 9] * rim_ref[i]
                    query = query + rim_ref[2 + i]
                mixed = (near + total(x)).astype(BF16).astype(F32)
                turned[pl.ds(i, SUB, stride=STRIDE), :] = query * mixed
            for m in range(modes):
                if first:
                    held = (state[m] * p[m] + rim_ref[0]) * p[m] + rim_ref[1]
                    state[m] = held * jnp.exp(-(CHUNK - 2) * tables_ref[g, m])
                else:
                    state[m] = state[m] * power[m]

        def turn_out(turned, c):
            rows = pl.ds(pl.multiple_of(c * CHUNK, CHUNK), CHUNK)
            for j in range(SUB):
                out_buf[rows, column(g, j)] = turned[pl.ds(j * STRIDE, CHUNK), :].astype(BF16)

        one_chunk(0, ta, True)
        one_chunk(1, tb, False)
        turn_out(ta, 0)

        def two_chunks(it, none):
            c = 2 * it
            one_chunk(c, ta, False)
            turn_out(tb, c - 1)
            one_chunk(c + 1, tb, False)
            turn_out(ta, c)

            @pl.when((it & 1) == 0)
            def _():
                send(g, it * 2 * CHUNK // PIECE - 1).start()

            return none

        lax.fori_loop(1, chunks // 2, two_chunks, 0)
        turn_out(tb, chunks - 1)
        send(g, pieces - 1).start()
        return none

    lax.fori_loop(0, groups, one_group, 0)
    for g in range(groups):
        for n in range(pieces):
            send(g, n).wait()


VM = pl.BlockSpec(memory_space=pltpu.VMEM)
HB = pl.BlockSpec(memory_space=pltpu.HBM)


def in_vmem(x):
    return pltpu.with_memory_space_constraint(x, pltpu.VMEM)


def in_hbm(x):
    return pltpu.with_memory_space_constraint(x, pltpu.HBM)


def params(mib):
    return pltpu.CompilerParams(vmem_limit_bytes=mib * 2**20)


def cost(flops, nbytes):
    return pl.CostEstimate(flops=flops, bytes_accessed=nbytes, transcendentals=0)


def body(streams, short_filter, decay_rate, residue, bias):
    tokens, _, channels = streams.shape
    modes = decay_rate.shape[1]
    groups = channels // GROUP
    chunks, pieces = tokens // CHUNK, tokens // PIECE
    size = lax.axis_size("context")
    rank = lax.axis_index("context")
    turned = pltpu.VMEM((SUB * STRIDE, LANES), F32)
    vector = (SUB, LANES)
    kv_shape = (groups, tokens) + vector
    table_rows = 2 * modes + 10
    dma = pltpu.SemaphoreType.DMA

    message_rows = modes + HEAD + TAIL
    own_shape, message_shape = (groups, message_rows) + vector, (groups, message_rows // 2, 2 * SUB, LANES)
    mode_shape, rim_shape = (groups, modes) + vector, (groups, TAIL) + vector
    key_value, states, own, message, tables, q = pl.pallas_call(
        state_kernel,
        in_specs=[HB] * 5,
        out_specs=[VM] * 6,
        out_shape=[
            pltpu.VMEM(kv_shape, F32),
            pltpu.VMEM((groups, chunks, modes) + vector, F32),
            pltpu.VMEM(own_shape, F32),
            pltpu.VMEM(message_shape, BF16),
            pltpu.VMEM((groups, table_rows) + vector, F32),
            pltpu.VMEM((tokens, channels), BF16),
        ],
        scratch_shapes=[
            pltpu.VMEM((tokens, channels), BF16),
            pltpu.VMEM((tokens, channels), BF16),
            pltpu.VMEM((3, 3, channels), F32),
            pltpu.VMEM((modes, channels), F32),
            pltpu.VMEM((modes, channels), F32),
            pltpu.VMEM((groups,) + vector, F32),
            turned, turned, turned, turned,
            dma((4,)), dma((2, groups, pieces)), dma(()),
        ],
        compiler_params=params(8),
        cost_estimate=cost(48 * tokens * channels, 6 * 2**20),
        name="states",
    )(
        in_hbm(streams.transpose(1, 0, 2)), in_hbm(short_filter), in_hbm(decay_rate.T), in_hbm(residue.T),
        in_hbm(bias.reshape((groups,) + vector)),
    )

    merged, entering, rim, near = own, None, None, None
    span = 1
    while span < size:
        got = lax.ppermute(message, "context", [(i, i ^ span) for i in range(size)])
        if near is None:
            near, query = pl.pallas_call(
                near_kernel,
                in_specs=[VM] * 3,
                out_specs=[VM] * 2,
                out_shape=[pltpu.VMEM(kv_shape, F32)] * 2,
                scratch_shapes=[pltpu.VMEM((CHUNK,) + vector, F32), turned, turned],
                compiler_params=params(4),
                cost_estimate=cost(24 * tokens * channels, 7 * 2**20),
                name="near",
            )(in_vmem(q), in_vmem(tables), in_vmem(key_value))
        if 2 * span >= size:
            break
        operands = [merged, got, tables] + ([] if entering is None else [entering, rim])

        def merge(*refs, span=span, first=entering is None):
            refs = refs[:3] + (None, None) + refs[3:] if first else refs
            merge_kernel(span, tokens, *refs)

        merged, message, entering, rim = pl.pallas_call(
            merge,
            in_specs=[VM] * len(operands),
            out_specs=[VM] * 4,
            out_shape=[
                pltpu.VMEM(own_shape, F32), pltpu.VMEM(message_shape, BF16), pltpu.VMEM(mode_shape, F32),
                pltpu.VMEM(rim_shape, F32),
            ],
            compiler_params=params(4),
            cost_estimate=cost(2**20, 2**20),
            name="merge",
        )(*[in_vmem(x) for x in operands])
        span *= 2

    return pl.pallas_call(
        functools.partial(emit_kernel, span),
        in_specs=[VM] * 9,
        out_specs=HB,
        out_shape=pltpu.HBM((tokens, channels), BF16),
        scratch_shapes=[
            pltpu.VMEM((tokens, channels), BF16),
            pltpu.VMEM((modes,) + vector, F32),
            pltpu.VMEM((modes,) + vector, F32),
            pltpu.VMEM((4,) + vector, F32),
            turned, turned, dma((groups, pieces)),
        ],
        compiler_params=params(4),
        cost_estimate=cost(40 * tokens * channels, 7 * 2**20),
        name="emit",
    )(*[in_vmem(x) for x in (near, query, states, tables, own, merged, got, entering, rim)])


def solution(mesh):
    in_specs = (
        P(("dp", "context"), None, "tensor"),
        P(None, None, "tensor"),
        P("tensor", None),
        P("tensor", None),
        P("tensor"),
    )
    out_specs = P(("dp", "context"), "tensor")
    return jax.shard_map(body, mesh=mesh, in_specs=in_specs, out_specs=out_specs, check_vma=False)
```

```python
import jax
import jax.numpy as jnp
from jax import lax
from jax.experimental import pallas as pl
from jax.experimental.pallas import tpu as pltpu
from jax.sharding import PartitionSpec as P

F32 = jnp.float32
BF16 = jnp.bfloat16
LANES = 128
SUB = 8
GROUP = LANES * SUB
CHUNK = 16
PIECE = 64
STRIDE = CHUNK + 8
HEAD = 4
TAIL = 6


def total(values):
    values = list(values)
    while len(values) > 1:
        pairs = [values[i] + values[i + 1] for i in range(0, len(values) - 1, 2)]
        values = pairs + ([values[-1]] if len(values) % 2 else [])
    return values[0]


def columns(g):
    return pl.ds(g * GROUP, GROUP)


def turn_in(source, turned, start, g):
    for j in range(SUB):
        turned[pl.ds(j * STRIDE, CHUNK), :] = source[pl.ds(start, CHUNK), pl.ds(g * GROUP + j * LANES, LANES)].astype(F32)


def turn_rows(source, turned, rows, g):
    for j in range(SUB):
        turned[pl.ds(j * STRIDE, rows), :] = source[:, pl.ds(g * GROUP + j * LANES, LANES)]


def row(turned, i):
    return turned[pl.ds(i, SUB, stride=STRIDE), :]


def chunk_rows(c):
    return pl.multiple_of(c * CHUNK, CHUNK)


def pack(message_ref, rows):
    for i in range(message_ref.shape[0]):
        message_ref[i] = jnp.concatenate(rows[2 * i : 2 * i + 2], axis=0).astype(BF16)


def unpack(message_ref, first, count):
    rows = []
    for i in range(first // 2, (first + count) // 2):
        pair = message_ref[i].astype(F32)
        rows += [pair[:SUB], pair[SUB:]]
    return rows


def first_products(w, head, tail):
    features = []
    for s, rows in ((1, (tail[1], tail[4], head[0], head[2])), (2, (tail[2], tail[5], head[1], head[3]))):
        features.append([w[3 * s] * rows[2 + t] + w[3 * s + 1] * rows[1 + t] + w[3 * s + 2] * rows[t] for t in range(2)])
    return [(features[0][t] * features[1][t]).astype(BF16).astype(F32) for t in range(2)]


def first_terms(rate, products, steps):
    return jnp.exp((1.0 - steps) * rate) * products[0] + jnp.exp((2.0 - steps) * rate) * products[1]


def enter(tokens, span, rank, rate, w, head, other, other_tail, entering):
    right = (rank & span) != 0
    ahead = rank & (span - 1)
    steps = (tokens * ahead).astype(F32)
    products = first_products(w, head, other_tail)
    result = []
    for m, r in enumerate(rate):
        missing = jnp.where(ahead > 0, first_terms(r, products, jnp.maximum(steps, 2.0)), 0.0)
        result.append(jnp.where(right, entering[m] + jnp.exp(-steps * r) * other[m] + missing, entering[m]))
    return result


def table_parts(tables_ref):
    modes = (tables_ref.shape[0] - 10) // 2
    rate = [tables_ref[m] for m in range(modes)]
    return modes, rate, [tables_ref[modes + i] for i in range(9)]


def gain_row(modes, m):
    return modes + 9 + m


def state_kernel(
    g, rate_nat, taps_nat, residue_nat, bias_nat, natural,
    kv_ref, states_ref, own_ref, message_ref, tables_ref, ka, kb, va, vb, wait_piece, wait_rest,
):
    q_nat, k_nat, v_nat = (natural.at[i] for i in range(3))
    tokens, modes = natural.shape[1], rate_nat.shape[0]
    chunks = tokens // CHUNK
    rank = lax.axis_index("context")
    zero = jnp.zeros((SUB, LANES), F32)
    turn_rows(rate_nat, ka, modes, g)
    for stream in range(3):
        turn_rows(taps_nat.at[stream], (kb, va, vb)[stream], 3, g)
    p = []
    for m in range(modes):
        rate = row(ka, m)
        tables_ref[m] = rate
        p.append(jnp.exp(-rate))
    w = []
    for i in range(9):
        w.append(row((kb, va, vb)[i // 3], i % 3))
        tables_ref[modes + i] = w[i]
    wk, wv = w[3:6], w[6:9]
    wait_piece(0)
    turn_in(k_nat, ka, 0, g)
    turn_in(v_nat, va, 0, g)
    for i in range(2):
        own_ref[modes + TAIL + 2 * i] = row(ka, i)
        own_ref[modes + TAIL + 2 * i + 1] = row(va, i)

    def one_chunk(c, ks, vs, acc, last):
        k1, k2, v1, v2 = last
        for m in range(modes):
            states_ref[c, m] = acc[m]
        for i in range(CHUNK):
            k, v = row(ks, i), row(vs, i)
            key = wk[0] * k + wk[1] * k1 + wk[2] * k2
            value = wv[0] * v + wv[1] * v1 + wv[2] * v2
            k1, k2, v1, v2 = k, k1, v, v1
            product = (key * value).astype(BF16).astype(F32)
            if i < 2:
                product = jnp.where((c > 0) | (rank == 0), product, 0.0)
            kv_ref[c * CHUNK + i] = product
            acc = [a * b + product for a, b in zip(acc, p)]
        return acc, (k1, k2, v1, v2)

    def two_chunks(it, carry):
        acc, last = carry
        c = 2 * it
        pl.when(it == PIECE // (2 * CHUNK) - 1)(lambda: wait_piece(1))
        turn_in(k_nat, kb, chunk_rows(c + 1), g)
        turn_in(v_nat, vb, chunk_rows(c + 1), g)
        acc, last = one_chunk(c, ka, va, acc, last)
        ahead = chunk_rows(jnp.minimum(c + 2, chunks - 1))
        turn_in(k_nat, ka, ahead, g)
        turn_in(v_nat, va, ahead, g)
        return one_chunk(c + 1, kb, vb, acc, last)

    acc, last = lax.fori_loop(0, chunks // 2, two_chunks, ([zero] * modes, (zero,) * 4))
    for m in range(modes):
        own_ref[m] = acc[m]
    k1, k2, v1, v2 = last
    for i, value in ((1, k2), (2, v2), (4, k1), (5, v1)):
        own_ref[modes + i] = value
    wait_rest()
    turn_rows(residue_nat, ka, modes, g)
    for m in range(modes):
        tables_ref[gain_row(modes, m)] = row(ka, m)
    tables_ref[gain_row(modes, modes)] = bias_nat[g]
    turn_in(q_nat, va, tokens - CHUNK, g)
    for i in range(2):
        own_ref[modes + 3 * i] = row(va, CHUNK - 2 + i)
    pack(message_ref, [own_ref[i] for i in range(modes + TAIL + HEAD)])


def first_states_kernel(
    streams, taps_hbm, rate_hbm, residue_hbm, bias_hbm,
    kv_ref, states_ref, own_ref, message_ref, tables_ref, rate_nat, taps_nat, residue_nat, bias_nat, natural,
    ka, kb, va, vb, table_sems, stream_sems,
):
    _, tokens, channels = natural.shape
    groups = channels // GROUP

    def fetch(i, *where):
        return pltpu.make_async_copy(streams.at[where], natural.at[where], stream_sems.at[i])

    keys_values = pl.ds(1, 2)
    pieces = [
        fetch(0, keys_values, pl.ds(0, PIECE), columns(0)),
        fetch(1, keys_values, pl.ds(PIECE, tokens - PIECE), columns(0)),
    ]
    rest = [fetch(2, pl.ds(0, 1), slice(None), columns(0))]
    rest += [fetch(2 + g, slice(None), slice(None), columns(g)) for g in range(1, groups)]
    tables = [
        pltpu.make_async_copy(src, dst, table_sems.at[i])
        for i, (src, dst) in enumerate(
            [(rate_hbm, rate_nat), (taps_hbm, taps_nat), (residue_hbm, residue_nat), (bias_hbm, bias_nat)]
        )
    ]
    for copy in tables[:2] + pieces + rest + tables[2:]:
        copy.start()
    for copy in tables[:2]:
        copy.wait()

    def wait_rest():
        for copy in tables[2:] + rest:
            copy.wait()

    state_kernel(
        0, rate_nat, taps_nat, residue_nat, bias_nat, natural,
        kv_ref, states_ref, own_ref, message_ref, tables_ref, ka, kb, va, vb, lambda n: pieces[n].wait(), wait_rest,
    )


def later_states_kernel(g, *refs):
    state_kernel(g, *refs, lambda n: None, lambda: None)


def near_group(g, q_nat, tables_ref, kv_ref, near_ref, query_ref, taps, qa, qb):
    tokens = kv_ref.shape[0]
    chunks = tokens // CHUNK
    zero = jnp.zeros((SUB, LANES), F32)
    modes, rate, w = table_parts(tables_ref)
    p = [jnp.exp(-r) for r in rate]
    gain = [tables_ref[gain_row(modes, m)] for m in range(modes)]
    taps[0] = total(gain) + tables_ref[gain_row(modes, modes)]
    for i in range(1, CHUNK):
        gain = [a * b for a, b in zip(gain, p)]
        taps[i] = total(gain)
    h = [taps[i] for i in range(CHUNK)]
    turn_in(q_nat, qa, 0, g)

    def one_chunk(c, qs, last):
        q1, q2 = last
        window = []
        for i in range(CHUNK):
            t = c * CHUNK + i
            q = row(qs, i)
            query_ref[t] = w[0] * q + w[1] * q1 + w[2] * q2
            q1, q2 = q, q1
            window.append(kv_ref[t])
            near_ref[t] = total(h[n] * window[i - n] for n in range(i + 1))
        return q1, q2

    def two_chunks(it, last):
        c = 2 * it
        turn_in(q_nat, qb, chunk_rows(c + 1), g)
        last = one_chunk(c, qa, last)
        turn_in(q_nat, qa, chunk_rows(jnp.minimum(c + 2, chunks - 1)), g)
        return one_chunk(c + 1, qb, last)

    lax.fori_loop(0, chunks // 2, two_chunks, (zero, zero))


def merge_group(span, tokens, own_ref, got_ref, tables_ref, entering_ref, rim_ref, next_ref, message_ref, entering_out, rim_out):
    modes, rate, w = table_parts(tables_ref)
    rank = lax.axis_index("context")
    right = (rank & span) != 0
    ahead = rank & (span - 1)
    length = 1.0 * tokens * span
    zero = jnp.zeros((SUB, LANES), F32)
    state = [own_ref[m] for m in range(modes)]
    tail = [own_ref[modes + i] for i in range(TAIL)]
    head = [own_ref[modes + TAIL + i] for i in range(HEAD)]
    other = unpack(got_ref, 0, modes)
    other_tail = unpack(got_ref, modes, TAIL)
    other_head = unpack(got_ref, modes + TAIL, HEAD)

    def pick(a, b):
        return [jnp.where(right, x, y) for x, y in zip(a, b)]

    left_state, right_state = pick(other, state), pick(state, other)
    left_head, right_head = pick(other_head, head), pick(head, other_head)
    left_tail, right_tail = pick(other_tail, tail), pick(tail, other_tail)
    products = first_products(w, right_head, left_tail)
    rows = [
        right_state[m] + jnp.exp(-length * rate[m]) * left_state[m] + first_terms(rate[m], products, length)
        for m in range(modes)
    ]
    rows = rows + right_tail + left_head
    pack(message_ref, rows)
    for i, value in enumerate(rows):
        next_ref[i] = value
    entering = [zero if entering_ref is None else entering_ref[m] for m in range(modes)]
    entering = enter(tokens, span, rank, rate, w, head, other, other_tail, entering)
    for m in range(modes):
        entering_out[m] = entering[m]
    for i in range(TAIL):
        old = zero if rim_ref is None else rim_ref[i]
        rim_out[i] = jnp.where(right & (ahead == 0), other_tail[i], old)


def emit_group(
    near_ref, query_ref, states_ref, tables_ref, own_ref, entering, rim, out_ref, power, state, rim_ref, ta, tb, piece_done
):
    tokens = near_ref.shape[0]
    chunks = tokens // CHUNK
    rank = lax.axis_index("context")
    modes, rate, w = table_parts(tables_ref)
    p = [jnp.exp(-r) for r in rate]
    for m in range(modes):
        power[m] = jnp.exp(-CHUNK * rate[m])
        state[m] = entering[m]
    products = first_products(w, [own_ref[modes + TAIL + i] for i in range(HEAD)], rim)
    for i in range(2):
        rim_ref[i] = jnp.where(rank == 0, 0.0, products[i])
    rim_ref[2] = w[1] * rim[3] + w[2] * rim[0]
    rim_ref[3] = w[2] * rim[3]

    def one_chunk(c, turned, first):
        x = [tables_ref[gain_row(modes, m)] * (states_ref[c, m] + state[m]) for m in range(modes)]
        for i in range(CHUNK):
            t = c * CHUNK + i
            x = [a * b for a, b in zip(x, p)]
            near, query = near_ref[t], query_ref[t]
            if first and i < 2:
                x = [a + tables_ref[gain_row(modes, m)] * rim_ref[i] for m, a in enumerate(x)]
                near = near + tables_ref[gain_row(modes, modes)] * rim_ref[i]
                query = query + rim_ref[2 + i]
            mixed = (near + total(x)).astype(BF16).astype(F32)
            turned[pl.ds(i, SUB, stride=STRIDE), :] = query * mixed
        for m in range(modes):
            if first:
                held = (state[m] * p[m] + rim_ref[0]) * p[m] + rim_ref[1]
                state[m] = held * jnp.exp(-(CHUNK - 2) * tables_ref[m])
            else:
                state[m] = state[m] * power[m]

    def turn_out(turned, c):
        for j in range(SUB):
            out_ref[pl.ds(chunk_rows(c), CHUNK), pl.ds(j * LANES, LANES)] = turned[pl.ds(j * STRIDE, CHUNK), :].astype(BF16)

    one_chunk(0, ta, True)
    one_chunk(1, tb, False)
    turn_out(ta, 0)

    def two_chunks(it, none):
        c = 2 * it
        one_chunk(c, ta, False)
        turn_out(tb, c - 1)
        one_chunk(c + 1, tb, False)
        turn_out(ta, c)
        pl.when((it & 1) == 0)(lambda: piece_done(it * 2 * CHUNK // PIECE - 1))
        return none

    lax.fori_loop(1, chunks // 2, two_chunks, 0)
    turn_out(tb, chunks - 1)
    piece_done(tokens // PIECE - 1)


def emit_out(emit, halves, out_hbm, out_ref, half_sems, sems):
    tokens, last = out_ref.shape[0], len(halves)
    copies = [pltpu.make_async_copy(half, out_hbm.at[:, columns(g)], half_sems.at[g]) for g, half in enumerate(halves)]
    for copy in copies:
        copy.start()

    def send(n):
        rows = pl.ds(pl.multiple_of(n * PIECE, PIECE), PIECE)
        return pltpu.make_async_copy(out_ref.at[rows], out_hbm.at[rows, columns(last)], sems.at[n])

    emit(out_ref, lambda n: send(n).start())
    for copy in copies + [send(n) for n in range(tokens // PIECE)]:
        copy.wait()


def is_early(span):
    return (lax.axis_index("context") & span) == 0


def emit_known(near_ref, query_ref, states_ref, tables_ref, own_ref, entering_ref, rim_ref, out_ref, scratch, piece_done):
    entering = [entering_ref[m] for m in range(entering_ref.shape[0])]
    rim = [rim_ref[i] for i in range(TAIL)]
    emit_group(near_ref, query_ref, states_ref, tables_ref, own_ref, entering, rim, out_ref, *scratch, piece_done)


def emit_merged(
    span, near_ref, query_ref, states_ref, tables_ref, own_ref, entering_ref, rim_ref, head, got_ref, out_ref, scratch, piece_done
):
    tokens, modes = near_ref.shape[0], entering_ref.shape[0]
    rank = lax.axis_index("context")
    _, rate, w = table_parts(tables_ref)
    other_tail = unpack(got_ref, modes, TAIL)
    entering = enter(
        tokens, span, rank, rate, w, head, unpack(got_ref, 0, modes), other_tail, [entering_ref[m] for m in range(modes)]
    )
    begins = (rank & (span - 1)) == 0
    rim = [jnp.where(begins, other_tail[i], rim_ref[i]) for i in range(TAIL)]
    emit_group(near_ref, query_ref, states_ref, tables_ref, own_ref, entering, rim, out_ref, *scratch, piece_done)


def early_kernel(span, inputs, out_hbm, out_refs, scratch, half_sems, sems):
    @pl.when(is_early(span))
    def _():
        for g in range(len(inputs) - 1):
            emit_known(*inputs[g], out_refs[g], scratch, lambda n: None)

        def emit(out, piece_done):
            emit_known(*inputs[-1], out, scratch, piece_done)

        emit_out(emit, out_refs[:-1], out_hbm, out_refs[-1], half_sems, sems)


def late_kernel(span, inputs, merged_ref, got_ref, halves, outs, scratch, half_sems=None, sems=None):
    modes = inputs[-2].shape[0]

    @pl.when(jnp.logical_not(is_early(span)))
    def _():
        def emit(out, piece_done):
            head = [merged_ref[modes + TAIL + i] for i in range(HEAD)]
            emit_merged(span, *inputs, head, got_ref, out, scratch, piece_done)

        if sems is None:
            emit(outs[0], lambda n: None)
        else:
            emit_out(emit, halves, outs[0], outs[1], half_sems, sems)


VM = pl.BlockSpec(memory_space=pltpu.VMEM)
HB = pl.BlockSpec(memory_space=pltpu.HBM)


def call(kernel, name, operands, outs, scratch, mib, flops, in_specs=None, out_specs=None, aliases=None):
    in_specs = in_specs or [VM] * len(operands)
    operands = [
        pltpu.with_memory_space_constraint(x, pltpu.VMEM if spec is VM else pltpu.HBM) for x, spec in zip(operands, in_specs)
    ]
    return pl.pallas_call(
        kernel,
        in_specs=in_specs,
        out_specs=[VM] * len(outs) if out_specs is None else out_specs,
        out_shape=outs,
        scratch_shapes=scratch,
        input_output_aliases=aliases or {},
        compiler_params=pltpu.CompilerParams(vmem_limit_bytes=mib * 2**20),
        cost_estimate=pl.CostEstimate(flops=flops, bytes_accessed=2**20, transcendentals=0),
        name=name,
    )(*operands)


def body(streams, short_filter, decay_rate, residue, bias):
    tokens, _, channels = streams.shape
    modes = decay_rate.shape[1]
    groups = channels // GROUP
    chunks, pieces = tokens // CHUNK, tokens // PIECE
    size = lax.axis_size("context")
    vector = (SUB, LANES)
    turned = pltpu.VMEM((SUB * STRIDE, LANES), F32)
    dma = pltpu.SemaphoreType.DMA
    work = tokens * channels
    rows = modes + TAIL + HEAD

    def vectors(*shape):
        return pltpu.VMEM(shape + vector, F32)

    def message_type(count):
        return pltpu.VMEM((count // 2, 2 * SUB, LANES), BF16)

    def swap(message, span):
        return lax.ppermute(message, "context", [(i, i ^ span) for i in range(size)])

    state_types = [vectors(tokens), vectors(chunks, modes), vectors(rows), message_type(rows), vectors(2 * modes + 10)]
    input_types = [
        pltpu.VMEM((modes, channels), F32), pltpu.VMEM((3, 3, channels), F32), pltpu.VMEM((modes, channels), F32),
        vectors(groups), pltpu.VMEM((3, tokens, channels), BF16),
    ]
    made = call(
        first_states_kernel, "states",
        [streams.transpose(1, 0, 2), short_filter, decay_rate.T, residue.T, bias.reshape((groups,) + vector)],
        state_types + input_types, [turned] * 4 + [dma((4,)), dma((groups + 2,))], 4, 24 * work, in_specs=[HB] * 5,
    )
    made, inputs = [made[:5]], made[5:]
    for g in range(1, groups):

        def kernel(*refs, g=g):
            later_states_kernel(g, *refs)

        made.append(call(kernel, "states", inputs, state_types, [turned] * 4, 4, 24 * work))
    key_value, states, own, message, tables = zip(*made)

    def near_of(g, after):
        def kernel(*refs):
            natural, tables_ref, kv_ref = refs[:3]
            near_group(g, natural.at[0], tables_ref, kv_ref, *refs[3 + len(after) :])

        return call(
            kernel, "near", [inputs[-1], tables[g], key_value[g]] + after, [vectors(tokens)] * 2,
            [vectors(CHUNK), turned, turned], 4, 12 * work,
        )

    merged, message = list(own), list(message)
    entering, rim, near = [None] * groups, [None] * groups, [None] * groups
    span = 1
    while True:
        got = [swap(message[g], span) for g in range(groups)]
        if 2 * span >= size:
            break
        for g in range(groups):
            first = entering[g] is None
            after = []
            if first and g == 1:
                near[0] = near_of(0, [rim[0]])
                near[1] = near_of(1, [near[0][0]])
                after = [near[1][0]]
            count = rows if 4 * span < size else modes + TAIL

            def kernel(*refs, span=span, skip=len(after), first=first):
                refs = refs[skip:]
                refs = refs[:3] + (None, None) + refs[3:] if first else refs
                merge_group(span, tokens, *refs)

            merged[g], message[g], entering[g], rim[g] = call(
                kernel, "merge", after + [merged[g], got[g], tables[g]] + ([] if first else [entering[g], rim[g]]),
                [vectors(rows), message_type(count), vectors(modes), vectors(TAIL)], [], 4, 2**20,
            )
        span *= 2

    half = pltpu.VMEM((tokens, GROUP), BF16)
    emit_scratch = [vectors(modes), vectors(modes), vectors(4), turned, turned]
    out_type = pltpu.HBM((tokens, channels), BF16)
    operands = [[*near[g], states[g], tables[g], own[g], entering[g], rim[g]] for g in range(groups)]
    count = len(operands[0])

    def kernel(*refs):
        ins, refs = [refs[i * count : (i + 1) * count] for i in range(groups)], refs[groups * count :]
        out_hbm, out_refs, scratch = refs[0], refs[1 : 1 + groups], refs[1 + groups :]
        early_kernel(span, ins, out_hbm, out_refs, scratch[:5], *scratch[5:])

    out = call(
        kernel, "early", sum(operands, []), [out_type], [half] * groups + emit_scratch + [dma((groups,)), dma((pieces,))],
        4, 40 * work, out_specs=[HB],
    )[0]
    halves = []
    for g in range(groups - 1):

        def kernel(*refs):
            ins, (merged_ref, got_ref, out, *scratch) = refs[:count], refs[count:]
            late_kernel(span, ins, merged_ref, got_ref, (), [out], scratch)

        halves += call(kernel, "late", operands[g] + [merged[g], got[g]], [half], emit_scratch, 4, 20 * work)

    def kernel(*refs):
        ins, (merged_ref, got_ref, *refs) = refs[:count], refs[count:]
        done, (_, out_hbm, out_ref, *scratch) = refs[: groups - 1], refs[groups - 1 :]
        late_kernel(span, ins, merged_ref, got_ref, done, (out_hbm, out_ref), scratch[:5], *scratch[5:])

    operands = operands[-1] + [merged[-1], got[-1]] + halves + [out]
    return call(
        kernel, "late", operands, [out_type], [half] + emit_scratch + [dma((groups,)), dma((pieces,))], 4, 20 * work,
        in_specs=[VM] * (len(operands) - 1) + [HB], out_specs=[HB], aliases={len(operands) - 1: 0},
    )[0]


def solution(mesh):
    in_specs = (
        P(("dp", "context"), None, "tensor"),
        P(None, None, "tensor"),
        P("tensor", None),
        P("tensor", None),
        P("tensor"),
    )
    out_specs = P(("dp", "context"), "tensor")
    return jax.shard_map(body, mesh=mesh, in_specs=in_specs, out_specs=out_specs, check_vma=False)
```

```python
import jax
import jax.numpy as jnp
from jax import lax
from jax.experimental import pallas as pl
from jax.experimental.pallas import tpu as pltpu
from jax.sharding import PartitionSpec as P

F32 = jnp.float32
BF16 = jnp.bfloat16
LANES = 128
SUB = 8
GROUP = LANES * SUB
CHUNK = 16
PIECE = 64
STRIDE = CHUNK + 8
EARLY = (4, 8)
HEAD = 4
TAIL = 6


def total(values):
    values = list(values)
    while len(values) > 1:
        pairs = [values[i] + values[i + 1] for i in range(0, len(values) - 1, 2)]
        values = pairs + ([values[-1]] if len(values) % 2 else [])
    return values[0]


def columns(g):
    return pl.ds(g * GROUP, GROUP)


def turn_in(source, turned, start, g):
    for j in range(SUB):
        turned[pl.ds(j * STRIDE, CHUNK), :] = source[pl.ds(start, CHUNK), pl.ds(g * GROUP + j * LANES, LANES)].astype(F32)


def turn_rows(source, turned, rows, g):
    for j in range(SUB):
        turned[pl.ds(j * STRIDE, rows), :] = source[:, pl.ds(g * GROUP + j * LANES, LANES)]


def row(turned, i):
    return turned[pl.ds(i, SUB, stride=STRIDE), :]


def chunk_rows(c):
    return pl.multiple_of(c * CHUNK, CHUNK)


def pack(message_ref, rows):
    for i in range(message_ref.shape[0]):
        message_ref[i] = jnp.concatenate(rows[2 * i : 2 * i + 2], axis=0).astype(BF16)


def unpack(message_ref, first, count):
    rows = []
    for i in range(first // 2, (first + count) // 2):
        pair = message_ref[i].astype(F32)
        rows += [pair[:SUB], pair[SUB:]]
    return rows


def first_products(w, head, tail):
    features = []
    for s, rows in ((1, (tail[1], tail[4], head[0], head[2])), (2, (tail[2], tail[5], head[1], head[3]))):
        features.append([w[3 * s] * rows[2 + t] + w[3 * s + 1] * rows[1 + t] + w[3 * s + 2] * rows[t] for t in range(2)])
    return [(features[0][t] * features[1][t]).astype(BF16).astype(F32) for t in range(2)]


def first_terms(rate, products, steps):
    return jnp.exp((1.0 - steps) * rate) * products[0] + jnp.exp((2.0 - steps) * rate) * products[1]


def enter(tokens, span, rank, rate, w, head, other, other_tail, entering):
    right = (rank & span) != 0
    ahead = rank & (span - 1)
    steps = (tokens * ahead).astype(F32)
    products = first_products(w, head, other_tail)
    result = []
    for m, r in enumerate(rate):
        missing = jnp.where(ahead > 0, first_terms(r, products, jnp.maximum(steps, 2.0)), 0.0)
        result.append(jnp.where(right, entering[m] + jnp.exp(-steps * r) * other[m] + missing, entering[m]))
    return result


def table_parts(tables_ref):
    modes = (tables_ref.shape[0] - 10) // 2
    rate = [tables_ref[m] for m in range(modes)]
    return modes, rate, [tables_ref[modes + i] for i in range(9)]


def gain_row(modes, m):
    return modes + 9 + m


def state_kernel(
    g, rate_nat, taps_nat, residue_nat, bias_nat, natural,
    kv_ref, states_ref, own_ref, tables_ref, ka, kb, va, vb, wait_piece, wait_rest,
):
    q_nat, k_nat, v_nat = (natural.at[i] for i in range(3))
    tokens, modes = natural.shape[1], rate_nat.shape[0]
    chunks = tokens // CHUNK
    rank = lax.axis_index("context")
    zero = jnp.zeros((SUB, LANES), F32)
    turn_rows(rate_nat, ka, modes, g)
    for stream in range(3):
        turn_rows(taps_nat.at[stream], (kb, va, vb)[stream], 3, g)
    p = []
    for m in range(modes):
        rate = row(ka, m)
        tables_ref[m] = rate
        p.append(jnp.exp(-rate))
    w = []
    for i in range(9):
        w.append(row((kb, va, vb)[i // 3], i % 3))
        tables_ref[modes + i] = w[i]
    wk, wv = w[3:6], w[6:9]
    wait_piece(0)
    turn_in(k_nat, ka, 0, g)
    turn_in(v_nat, va, 0, g)
    def one_chunk(c, ks, vs, acc, last):
        k1, k2, v1, v2 = last
        for m in range(modes):
            states_ref[c, m] = acc[m]
        for i in range(CHUNK):
            k, v = row(ks, i), row(vs, i)
            key = wk[0] * k + wk[1] * k1 + wk[2] * k2
            value = wv[0] * v + wv[1] * v1 + wv[2] * v2
            k1, k2, v1, v2 = k, k1, v, v1
            product = (key * value).astype(BF16).astype(F32)
            if i < 2:
                product = jnp.where((c > 0) | (rank == 0), product, 0.0)
            kv_ref[c * CHUNK + i] = product
            acc = [a * b + product for a, b in zip(acc, p)]
        return acc, (k1, k2, v1, v2)

    def two_chunks(it, carry):
        acc, last = carry
        c = 2 * it
        pl.when(it == PIECE // (2 * CHUNK) - 1)(lambda: wait_piece(1))
        turn_in(k_nat, kb, chunk_rows(c + 1), g)
        turn_in(v_nat, vb, chunk_rows(c + 1), g)
        acc, last = one_chunk(c, ka, va, acc, last)
        ahead = chunk_rows(jnp.minimum(c + 2, chunks - 1))
        turn_in(k_nat, ka, ahead, g)
        turn_in(v_nat, va, ahead, g)
        return one_chunk(c + 1, kb, vb, acc, last)

    acc, _ = lax.fori_loop(0, chunks // 2, two_chunks, ([zero] * modes, (zero,) * 4))
    for m in range(modes):
        own_ref[m] = acc[m]
    wait_rest()
    turn_rows(residue_nat, ka, modes, g)
    for m in range(modes):
        tables_ref[gain_row(modes, m)] = row(ka, m)
    tables_ref[gain_row(modes, modes)] = bias_nat[g]


def edge_rows(natural, edges_ref, turned, g):
    tokens = natural.shape[1]
    for stream in range(3):
        turn_in(natural.at[stream], turned, tokens - CHUNK, g)
        for i in range(2):
            edges_ref[g, 3 * i + stream] = row(turned, CHUNK - 2 + i)
        if stream:
            turn_in(natural.at[stream], turned, 0, g)
            for i in range(2):
                edges_ref[g, TAIL + 2 * i + stream - 1] = row(turned, i)


def tails_and_heads(edges, heads):
    rows = sum([e[:TAIL] for e in edges], [])
    return rows + sum([e[TAIL:] for e in edges], []) if heads else rows


def other_edges(first_got, g, groups, modes, heads):
    tail = unpack(first_got, modes + TAIL * g, TAIL)
    return tail, unpack(first_got, modes + TAIL * groups + HEAD * g, HEAD) if heads else None


def first_states_kernel(
    streams, taps_hbm, rate_hbm, residue_hbm, bias_hbm,
    kv_ref, states_ref, own_ref, tables_ref, message_ref, edges_ref, rate_nat, taps_nat, residue_nat, bias_nat, natural,
    ka, kb, va, vb, table_sems, stream_sems,
):
    _, tokens, channels = natural.shape
    groups = channels // GROUP

    def fetch(i, *where):
        return pltpu.make_async_copy(streams.at[where], natural.at[where], stream_sems.at[i])

    keys_values = pl.ds(1, 2)
    pieces = [
        fetch(0, keys_values, pl.ds(0, PIECE), columns(0)),
        fetch(1, keys_values, pl.ds(PIECE, tokens - PIECE), columns(0)),
    ]
    rest = [fetch(2, pl.ds(0, 1), slice(None), columns(0))]
    rest += [fetch(2 + g, slice(None), slice(None), columns(g)) for g in range(1, groups)]
    tables = [
        pltpu.make_async_copy(src, dst, table_sems.at[i])
        for i, (src, dst) in enumerate(
            [(rate_hbm, rate_nat), (taps_hbm, taps_nat), (residue_hbm, residue_nat), (bias_hbm, bias_nat)]
        )
    ]
    for copy in tables[:2] + pieces + rest + tables[2:]:
        copy.start()
    for copy in tables[:2]:
        copy.wait()

    def wait_rest():
        for copy in tables[2:] + rest:
            copy.wait()

    state_kernel(
        0, rate_nat, taps_nat, residue_nat, bias_nat, natural,
        kv_ref, states_ref, own_ref, tables_ref, ka, kb, va, vb, lambda n: pieces[n].wait(), wait_rest,
    )
    for g in range(groups):
        edge_rows(natural, edges_ref, ka, g)
    state = [own_ref[m] for m in range(own_ref.shape[0])]
    pack(message_ref, state + tails_and_heads([[edges_ref[g, i] for i in range(TAIL + HEAD)] for g in range(groups)], True))


def later_states_kernel(
    g, rate_nat, taps_nat, residue_nat, bias_nat, natural, kv_ref, states_ref, own_ref, tables_ref, message_ref, *scratch
):
    state_kernel(
        g, rate_nat, taps_nat, residue_nat, bias_nat, natural, kv_ref, states_ref, own_ref, tables_ref, *scratch,
        lambda n: None, lambda: None,
    )
    pack(message_ref, [own_ref[m] for m in range(own_ref.shape[0])])


def near_group(g, q_nat, tables_ref, kv_ref, near_ref, query_ref, taps, qa, qb):
    tokens = kv_ref.shape[0]
    chunks = tokens // CHUNK
    zero = jnp.zeros((SUB, LANES), F32)
    modes, rate, w = table_parts(tables_ref)
    p = [jnp.exp(-r) for r in rate]
    gain = [tables_ref[gain_row(modes, m)] for m in range(modes)]
    taps[0] = total(gain) + tables_ref[gain_row(modes, modes)]
    for i in range(1, CHUNK):
        gain = [a * b for a, b in zip(gain, p)]
        taps[i] = total(gain)
    h = [taps[i] for i in range(CHUNK)]
    turn_in(q_nat, qa, 0, g)

    def one_chunk(c, qs, last):
        q1, q2 = last
        window = []
        for i in range(CHUNK):
            t = c * CHUNK + i
            q = row(qs, i)
            query_ref[t] = w[0] * q + w[1] * q1 + w[2] * q2
            q1, q2 = q, q1
            window.append(kv_ref[t])
            near_ref[t] = total(h[n] * window[i - n] for n in range(i + 1))
        return q1, q2

    def two_chunks(it, last):
        c = 2 * it
        turn_in(q_nat, qb, chunk_rows(c + 1), g)
        last = one_chunk(c, qa, last)
        turn_in(q_nat, qa, chunk_rows(jnp.minimum(c + 2, chunks - 1)), g)
        return one_chunk(c + 1, qb, last)

    lax.fori_loop(0, chunks // 2, two_chunks, (zero, zero))


def merge_group(
    span, tokens, g, last, own_ref, edges_ref, got_ref, first_got, tables_ref, entering_ref, rim_ref,
    message_ref, entering_out, rim_out, next_ref, edges_out,
):
    modes, rate, w = table_parts(tables_ref)
    groups = edges_ref.shape[0]
    rank = lax.axis_index("context")
    right = (rank & span) != 0
    ahead = rank & (span - 1)
    length = 1.0 * tokens * span
    zero = jnp.zeros((SUB, LANES), F32)

    def pick(a, b):
        return [jnp.where(right, x, y) for x, y in zip(a, b)]

    def edge(group):
        rows = [edges_ref[group, i] for i in range(TAIL + HEAD)]
        return rows[:TAIL], rows[TAIL:]

    state, other = [own_ref[m] for m in range(modes)], unpack(got_ref, 0, modes)
    tail, head = edge(g)
    other_tail, other_head = other_edges(first_got, g, groups, modes, True)
    products = first_products(w, pick(head, other_head), pick(other_tail, tail))
    left_state, right_state = pick(other, state), pick(state, other)
    rows = [
        right_state[m] + jnp.exp(-length * rate[m]) * left_state[m] + first_terms(rate[m], products, length)
        for m in range(modes)
    ]
    if not last:
        for m in range(modes):
            next_ref[m] = rows[m]
    if g == 0:
        edges = []
        for group in range(groups):
            mine, theirs = edge(group), other_edges(first_got, group, groups, modes, True)
            edges.append(pick(mine[0], theirs[0]) + pick(theirs[1], mine[1]))
            for i, value in enumerate(edges[-1]):
                edges_out[group, i] = value
        rows = rows + tails_and_heads(edges, not last)
    pack(message_ref, rows)
    entering = [zero if entering_ref is None else entering_ref[m] for m in range(modes)]
    entering = enter(tokens, span, rank, rate, w, head, other, other_tail, entering)
    for m in range(modes):
        entering_out[m] = entering[m]
    for i in range(TAIL):
        old = zero if rim_ref is None else rim_ref[i]
        rim_out[i] = jnp.where(right & (ahead == 0), other_tail[i], old)


def emit_group(
    which, near_ref, query_ref, states_ref, tables_ref, head, entering, rim, out_ref, state, power, rim_ref, ta, tb, piece_done
):
    rank = lax.axis_index("context")
    modes, rate, w = table_parts(tables_ref)
    p = [jnp.exp(-r) for r in rate]
    for m in range(modes):
        power[m] = jnp.exp(-CHUNK * rate[m])
    if which.start == 0:
        for m in range(modes):
            state[m] = entering[m]
        products = first_products(w, head, rim)
        for i in range(2):
            rim_ref[i] = jnp.where(rank == 0, 0.0, products[i])
        rim_ref[2] = w[1] * rim[3] + w[2] * rim[0]
        rim_ref[3] = w[2] * rim[3]

    def one_chunk(c, turned, first):
        x = [tables_ref[gain_row(modes, m)] * (states_ref[c, m] + state[m]) for m in range(modes)]
        for i in range(CHUNK):
            t = c * CHUNK + i
            x = [a * b for a, b in zip(x, p)]
            near, query = near_ref[t], query_ref[t]
            if first and i < 2:
                x = [a + tables_ref[gain_row(modes, m)] * rim_ref[i] for m, a in enumerate(x)]
                near = near + tables_ref[gain_row(modes, modes)] * rim_ref[i]
                query = query + rim_ref[2 + i]
            mixed = (near + total(x)).astype(BF16).astype(F32)
            turned[pl.ds(i, SUB, stride=STRIDE), :] = query * mixed
        for m in range(modes):
            if first:
                held = (state[m] * p[m] + rim_ref[0]) * p[m] + rim_ref[1]
                state[m] = held * jnp.exp(-(CHUNK - 2) * tables_ref[m])
            else:
                state[m] = state[m] * power[m]

    def turn_out(turned, c):
        for j in range(SUB):
            out_ref[pl.ds(chunk_rows(c), CHUNK), pl.ds(j * LANES, LANES)] = turned[pl.ds(j * STRIDE, CHUNK), :].astype(BF16)

    begin = which.start
    one_chunk(begin, ta, begin == 0)
    one_chunk(begin + 1, tb, False)
    turn_out(ta, begin)

    def two_chunks(it, none):
        c = 2 * it
        one_chunk(c, ta, False)
        turn_out(tb, c - 1)
        one_chunk(c + 1, tb, False)
        turn_out(ta, c)
        pl.when((it & 1) == 0)(lambda: piece_done(it * 2 * CHUNK // PIECE - 1))
        return none

    lax.fori_loop(begin // 2 + 1, which.stop // 2, two_chunks, 0)
    turn_out(tb, which.stop - 1)
    piece_done(which.stop * CHUNK // PIECE - 1)


def emit_out(emit, ready, out_hbm, out_ref, ready_sems, sems):
    tokens, last = out_ref.shape[0], out_hbm.shape[1] // GROUP - 1
    copies = [
        pltpu.make_async_copy(buffer.at[rows], out_hbm.at[rows, columns(g)], ready_sems.at[i])
        for i, (rows, g, buffer) in enumerate(ready)
    ]
    for copy in copies:
        copy.start()

    def send(n):
        rows = pl.ds(pl.multiple_of(n * PIECE, PIECE), PIECE)
        return pltpu.make_async_copy(out_ref.at[rows], out_hbm.at[rows, columns(last)], sems.at[n])

    emit(out_ref, lambda n: send(n).start())
    for copy in copies + [send(n) for n in range(tokens // PIECE)]:
        copy.wait()


def is_early(span):
    return (lax.axis_index("context") & span) == 0


def emit_known(which, g, fixed, edges_ref, entering_ref, rim_ref, out_ref, scratch, piece_done):
    entering = [entering_ref[m] for m in range(entering_ref.shape[0])]
    rim = [rim_ref[i] for i in range(TAIL)]
    head = [edges_ref[g, TAIL + i] for i in range(HEAD)]
    emit_group(which, *fixed, head, entering, rim, out_ref, *scratch, piece_done)


def emit_merged(span, g, fixed, edges_ref, entering_ref, rim_ref, merged_edges, got_ref, first_got, out_ref, scratch, piece_done):
    tokens, modes = fixed[0].shape[0], entering_ref.shape[0]
    rank = lax.axis_index("context")
    _, rate, w = table_parts(fixed[3])
    other_tail, _ = other_edges(first_got, g, edges_ref.shape[0], modes, False)
    entering = enter(
        tokens, span, rank, rate, w, [merged_edges[g, TAIL + i] for i in range(HEAD)],
        unpack(got_ref, 0, modes), other_tail, [entering_ref[m] for m in range(modes)],
    )
    begins = (rank & (span - 1)) == 0
    rim = [jnp.where(begins, other_tail[i], rim_ref[i]) for i in range(TAIL)]
    head = [edges_ref[g, TAIL + i] for i in range(HEAD)]
    emit_group(range(tokens // CHUNK), *fixed, head, entering, rim, out_ref, *scratch, piece_done)


VM = pl.BlockSpec(memory_space=pltpu.VMEM)
HB = pl.BlockSpec(memory_space=pltpu.HBM)


def call(kernel, name, operands, outs, scratch, mib, flops, in_specs=None, out_specs=None, aliases=None):
    in_specs = in_specs or [VM] * len(operands)
    operands = [
        pltpu.with_memory_space_constraint(x, pltpu.VMEM if spec is VM else pltpu.HBM) for x, spec in zip(operands, in_specs)
    ]
    return pl.pallas_call(
        kernel,
        in_specs=in_specs,
        out_specs=[VM] * len(outs) if out_specs is None else out_specs,
        out_shape=outs,
        scratch_shapes=scratch,
        input_output_aliases=aliases or {},
        compiler_params=pltpu.CompilerParams(vmem_limit_bytes=mib * 2**20),
        cost_estimate=pl.CostEstimate(flops=flops, bytes_accessed=2**20, transcendentals=0),
        name=name,
    )(*operands)


def body(streams, short_filter, decay_rate, residue, bias):
    tokens, _, channels = streams.shape
    modes = decay_rate.shape[1]
    groups = channels // GROUP
    chunks, pieces = tokens // CHUNK, tokens // PIECE
    size = lax.axis_size("context")
    vector = (SUB, LANES)
    turned = pltpu.VMEM((SUB * STRIDE, LANES), F32)
    dma = pltpu.SemaphoreType.DMA
    work = tokens * channels

    def vectors(*shape):
        return pltpu.VMEM(shape + vector, F32)

    def message_type(count):
        return pltpu.VMEM((count // 2, 2 * SUB, LANES), BF16)

    def swap(message, span):
        return lax.ppermute(message, "context", [(i, i ^ span) for i in range(size)])

    edge = TAIL + HEAD
    state_types = [vectors(tokens), vectors(chunks, modes), vectors(modes), vectors(2 * modes + 10)]
    input_types = [
        pltpu.VMEM((modes, channels), F32), pltpu.VMEM((3, 3, channels), F32), pltpu.VMEM((modes, channels), F32),
        vectors(groups), pltpu.VMEM((3, tokens, channels), BF16),
    ]
    *first, first_message, own_edges, rates, taps, residues, biases, natural = call(
        first_states_kernel, "states",
        [streams.transpose(1, 0, 2), short_filter, decay_rate.T, residue.T, bias.reshape((groups,) + vector)],
        state_types + [message_type(modes + groups * edge), vectors(groups, edge)] + input_types,
        [turned] * 4 + [dma((4,)), dma((groups + 2,))], 4, 24 * work, in_specs=[HB] * 5,
    )
    made, message = [first], [first_message]
    for g in range(1, groups):

        def kernel(*refs, g=g):
            later_states_kernel(g, *refs)

        *later, later_message = call(
            kernel, "states", [rates, taps, residues, biases, natural], state_types + [message_type(modes)], [turned] * 4, 4, 24 * work
        )
        made.append(later)
        message.append(later_message)
    key_value, states, own, tables = zip(*made)

    def near_all(early, after):
        def kernel(*refs):
            natural, refs = refs[0], refs[1 + len(after) :]
            ins, outs, scratch = refs[: 2 * groups], refs[2 * groups : 4 * groups], refs[4 * groups :]

            @pl.when(is_early(size // 2) == early)
            def _():
                for g in range(groups):
                    near_group(g, natural.at[0], *ins[2 * g : 2 * g + 2], *outs[2 * g : 2 * g + 2], *scratch)

        operands = sum([[tables[g], key_value[g]] for g in range(groups)], [])
        outs = call(
            kernel, "near", [natural] + after + operands, [vectors(tokens)] * (2 * groups),
            [vectors(CHUNK), turned, turned], 4, 24 * work,
        )
        return [list(outs[2 * g : 2 * g + 2]) for g in range(groups)]

    half = pltpu.VMEM((tokens, GROUP), BF16)
    emit_scratch = [vectors(modes), vectors(4), turned, turned]

    merged, edges = list(own), own_edges
    entering, rim = [None] * groups, [None] * groups
    begun, begun_state = [], []
    span = 1
    while True:
        got = [swap(message[g], span) for g in range(groups)]
        if 2 * span >= size:
            break
        last, first = 4 * span >= size, entering[0] is None
        if first:
            near = near_all(True, [])
        old_edges = edges
        for g in range(groups):
            part = range(EARLY[g - 1] if g else 0, EARLY[g]) if last and g < len(EARLY) else range(0)
            early = []
            if part:
                early = [*near[0], states[0], tables[0], own_edges] + ([entering[0], rim[0], begun_state[-1]] if g else [])
            operands = [merged[g], old_edges, got[g], got[0], tables[g]] + ([] if first else [entering[g], rim[g]])
            count = modes + (groups * (TAIL if last else edge) if g == 0 else 0)
            outs = [message_type(count), vectors(modes), vectors(TAIL)]
            outs += [] if last else [vectors(modes)]
            outs += [vectors(groups, edge)] if g == 0 else []
            outs += [half, vectors(modes)] if part else []

            def kernel(*refs, g=g, span=span, last=last, first=first, part=part, extra=len(early), results=len(outs)):
                refs = list(refs)
                ins = [refs.pop(0) for _ in range(5)] + ([None, None] if first else [refs.pop(0) for _ in range(2)])
                more = [refs.pop(0) for _ in range(extra)]
                produced = [refs.pop(0) for _ in range(results)]
                state_out = None if last else produced[3]
                edges_out = produced[3 if last else 4] if g == 0 else None
                merge_group(span, tokens, g, last, *ins, *produced[:3], state_out, edges_out)
                if part:

                    @pl.when(is_early(2 * span))
                    def _():
                        out_ref, state_ref = produced[-2:]
                        for m in range(modes if g else 0):
                            state_ref[m] = more[7][m]
                        known = more[5:7] if g else produced[1:3]
                        emit_known(part, 0, more[:4], more[4], *known, out_ref, [state_ref] + refs, lambda n: None)

            made = list(call(kernel, "merge", operands + early, outs, emit_scratch if part else [], 4, 2**20))
            message[g], entering[g], rim[g] = made[:3]
            if not last:
                merged[g] = made[3]
            if g == 0:
                edges = made[3 if last else 4]
            if part:
                begun.append((pl.ds(part.start * CHUNK, len(part) * CHUNK), made[-2]))
                begun_state.append(made[-1])
        span *= 2

    out_type = pltpu.HBM((tokens, channels), BF16)
    pair = [[entering[g], rim[g]] for g in range(groups)]
    begin = EARLY[len(begun) - 1] if begun else 0

    def kernel(own_edges, *refs):
        refs = list(refs)
        ready = [refs.pop(0) for _ in begun]
        begun_state = refs.pop(0) if begun else None
        ins, refs = [refs[i * 6 : i * 6 + 6] for i in range(groups)], refs[groups * 6 :]
        out_hbm, out_refs, state, scratch = refs[0], refs[1 : 1 + groups], refs[1 + groups], refs[2 + groups : 6 + groups]

        @pl.when(is_early(span))
        def _():
            for m in range(modes if begun else 0):
                state[m] = begun_state[m]
            for g in range(groups - 1):
                which = range(0 if g else begin, chunks)
                emit_known(which, g, ins[g][:4], own_edges, *ins[g][4:], out_refs[g], [state, *scratch], lambda n: None)

            def emit(out, piece_done):
                emit_known(range(chunks), groups - 1, ins[-1][:4], own_edges, *ins[-1][4:], out, [state, *scratch], piece_done)

            done = [(rows, 0, buffer) for (rows, _), buffer in zip(begun, ready)]
            done += [(pl.ds(begin * CHUNK, tokens - begin * CHUNK), 0, out_refs[0])]
            done += [(pl.ds(0, tokens), g, out_refs[g]) for g in range(1, groups - 1)]
            emit_out(emit, done, out_hbm, out_refs[-1], *refs[6 + groups :])

    out = call(
        kernel, "early",
        [own_edges] + [buffer for _, buffer in begun] + begun_state[-1:]
        + sum([[*near[g], states[g], tables[g], *pair[g]] for g in range(groups)], []),
        [out_type], [half] * groups + [vectors(modes)] + emit_scratch + [dma((groups + 1,)), dma((pieces,))],
        4, 40 * work, out_specs=[HB],
    )[0]
    near = near_all(False, [entering[-1]])
    fixed = [[*near[g], states[g], tables[g]] for g in range(groups)]
    halves = []
    for g in range(groups):
        final = g + 1 == groups
        operands = fixed[g] + [own_edges] + pair[g] + [edges, got[g], got[0]] + (halves + [out] if final else [])

        def kernel(*refs, g=g, final=final):
            ins, refs = refs[:10], refs[10:]
            if final:
                done, (_, out_hbm, out_ref, *scratch) = refs[: groups - 1], refs[groups - 1 :]
            else:
                out_ref, *scratch = refs

            @pl.when(jnp.logical_not(is_early(span)))
            def _():
                def emit(out, piece_done):
                    emit_merged(span, g, ins[:4], *ins[4:], out, scratch[:5], piece_done)

                if final:
                    ready = [(pl.ds(0, tokens), i, x) for i, x in enumerate(done)]
                    emit_out(emit, ready, out_hbm, out_ref, *scratch[5:])
                else:
                    emit(out_ref, lambda n: None)

        if not final:
            halves += call(kernel, "late", operands, [half], [vectors(modes)] + emit_scratch, 4, 20 * work)
    return call(
        kernel, "late", operands, [out_type],
        [half, vectors(modes)] + emit_scratch + [dma((groups,)), dma((pieces,))], 4, 20 * work,
        in_specs=[VM] * (len(operands) - 1) + [HB], out_specs=[HB], aliases={len(operands) - 1: 0},
    )[0]


def solution(mesh):
    in_specs = (
        P(("dp", "context"), None, "tensor"),
        P(None, None, "tensor"),
        P("tensor", None),
        P("tensor", None),
        P("tensor"),
    )
    out_specs = P(("dp", "context"), "tensor")
    return jax.shard_map(body, mesh=mesh, in_specs=in_specs, out_specs=out_specs, check_vma=False)
```

```python
import jax
import jax.numpy as jnp
from jax import lax
from jax.experimental import pallas as pl
from jax.experimental.pallas import tpu as pltpu
from jax.sharding import PartitionSpec as P

F32 = jnp.float32
BF16 = jnp.bfloat16
LANES = 128
SUB = 8
GROUP = LANES * SUB
CHUNK = 16
PIECE = 64
STRIDE = CHUNK + 8
EARLY = (4, 6)
HEAD = 4
TAIL = 6


def total(values):
    values = list(values)
    while len(values) > 1:
        pairs = [values[i] + values[i + 1] for i in range(0, len(values) - 1, 2)]
        values = pairs + ([values[-1]] if len(values) % 2 else [])
    return values[0]


def columns(g):
    return pl.ds(g * GROUP, GROUP)


def turn_in(source, turned, start, g):
    for j in range(SUB):
        turned[pl.ds(j * STRIDE, CHUNK), :] = source[pl.ds(start, CHUNK), pl.ds(g * GROUP + j * LANES, LANES)].astype(F32)


def turn_rows(source, turned, rows, g):
    for j in range(SUB):
        turned[pl.ds(j * STRIDE, rows), :] = source[:, pl.ds(g * GROUP + j * LANES, LANES)]


def row(turned, i):
    return turned[pl.ds(i, SUB, stride=STRIDE), :]


def chunk_rows(c):
    return pl.multiple_of(c * CHUNK, CHUNK)


def pack(message_ref, rows):
    for i in range(message_ref.shape[0]):
        message_ref[i] = jnp.concatenate(rows[2 * i : 2 * i + 2], axis=0).astype(BF16)


def unpack(message_ref, first, count):
    rows = []
    for i in range(first // 2, (first + count) // 2):
        pair = message_ref[i].astype(F32)
        rows += [pair[:SUB], pair[SUB:]]
    return rows


def first_products(w, head, tail):
    features = []
    for s, rows in ((1, (tail[1], tail[4], head[0], head[2])), (2, (tail[2], tail[5], head[1], head[3]))):
        features.append([w[3 * s] * rows[2 + t] + w[3 * s + 1] * rows[1 + t] + w[3 * s + 2] * rows[t] for t in range(2)])
    return [(features[0][t] * features[1][t]).astype(BF16).astype(F32) for t in range(2)]


def first_terms(rate, products, steps):
    return jnp.exp((1.0 - steps) * rate) * products[0] + jnp.exp((2.0 - steps) * rate) * products[1]


def enter(tokens, span, rank, rate, w, head, other, other_tail, entering):
    right = (rank & span) != 0
    ahead = rank & (span - 1)
    steps = (tokens * ahead).astype(F32)
    products = first_products(w, head, other_tail)
    result = []
    for m, r in enumerate(rate):
        missing = jnp.where(ahead > 0, first_terms(r, products, jnp.maximum(steps, 2.0)), 0.0)
        result.append(jnp.where(right, entering[m] + jnp.exp(-steps * r) * other[m] + missing, entering[m]))
    return result


def table_parts(tables_ref):
    modes = (tables_ref.shape[0] - 10) // 2
    rate = [tables_ref[m] for m in range(modes)]
    return modes, rate, [tables_ref[modes + i] for i in range(9)]


def gain_row(modes, m):
    return modes + 9 + m


def state_kernel(
    g, rate_nat, taps_nat, residue_nat, bias_nat, natural,
    kv_ref, states_ref, own_ref, tables_ref, ka, kb, va, vb, wait_piece, wait_rest,
):
    q_nat, k_nat, v_nat = (natural.at[i] for i in range(3))
    tokens, modes = natural.shape[1], rate_nat.shape[0]
    chunks = tokens // CHUNK
    rank = lax.axis_index("context")
    zero = jnp.zeros((SUB, LANES), F32)
    turn_rows(rate_nat, ka, modes, g)
    for stream in range(3):
        turn_rows(taps_nat.at[stream], (kb, va, vb)[stream], 3, g)
    p = []
    for m in range(modes):
        rate = row(ka, m)
        tables_ref[m] = rate
        p.append(jnp.exp(-rate))
    w = []
    for i in range(9):
        w.append(row((kb, va, vb)[i // 3], i % 3))
        tables_ref[modes + i] = w[i]
    wk, wv = w[3:6], w[6:9]
    wait_piece(0)
    turn_in(k_nat, ka, 0, g)
    turn_in(v_nat, va, 0, g)
    def one_chunk(c, ks, vs, acc, last):
        k1, k2, v1, v2 = last
        for m in range(modes):
            states_ref[c, m] = acc[m]
        for i in range(CHUNK):
            k, v = row(ks, i), row(vs, i)
            key = wk[0] * k + wk[1] * k1 + wk[2] * k2
            value = wv[0] * v + wv[1] * v1 + wv[2] * v2
            k1, k2, v1, v2 = k, k1, v, v1
            product = (key * value).astype(BF16).astype(F32)
            if i < 2:
                product = jnp.where((c > 0) | (rank == 0), product, 0.0)
            kv_ref[c * CHUNK + i] = product
            acc = [a * b + product for a, b in zip(acc, p)]
        return acc, (k1, k2, v1, v2)

    def two_chunks(it, carry):
        acc, last = carry
        c = 2 * it
        pl.when(it == PIECE // (2 * CHUNK) - 1)(lambda: wait_piece(1))
        turn_in(k_nat, kb, chunk_rows(c + 1), g)
        turn_in(v_nat, vb, chunk_rows(c + 1), g)
        acc, last = one_chunk(c, ka, va, acc, last)
        ahead = chunk_rows(jnp.minimum(c + 2, chunks - 1))
        turn_in(k_nat, ka, ahead, g)
        turn_in(v_nat, va, ahead, g)
        return one_chunk(c + 1, kb, vb, acc, last)

    acc, _ = lax.fori_loop(0, chunks // 2, two_chunks, ([zero] * modes, (zero,) * 4))
    for m in range(modes):
        own_ref[m] = acc[m]
    wait_rest()
    turn_rows(residue_nat, ka, modes, g)
    for m in range(modes):
        tables_ref[gain_row(modes, m)] = row(ka, m)
    tables_ref[gain_row(modes, modes)] = bias_nat[g]


def edge_rows(natural, edges_ref, turned, g):
    tokens = natural.shape[1]
    for stream in range(3):
        turn_in(natural.at[stream], turned, tokens - CHUNK, g)
        for i in range(2):
            edges_ref[g, 3 * i + stream] = row(turned, CHUNK - 2 + i)
        if stream:
            turn_in(natural.at[stream], turned, 0, g)
            for i in range(2):
                edges_ref[g, TAIL + 2 * i + stream - 1] = row(turned, i)


def tails_and_heads(edges, heads):
    rows = sum([e[:TAIL] for e in edges], [])
    return rows + sum([e[TAIL:] for e in edges], []) if heads else rows


def other_edges(first_got, g, groups, modes, heads):
    tail = unpack(first_got, modes + TAIL * g, TAIL)
    return tail, unpack(first_got, modes + TAIL * groups + HEAD * g, HEAD) if heads else None


def first_states_kernel(
    streams, taps_hbm, rate_hbm, residue_hbm, bias_hbm,
    kv_ref, states_ref, own_ref, tables_ref, message_ref, edges_ref, rate_nat, taps_nat, residue_nat, bias_nat, natural,
    ka, kb, va, vb, table_sems, stream_sems,
):
    _, tokens, channels = natural.shape
    groups = channels // GROUP

    def fetch(i, *where):
        return pltpu.make_async_copy(streams.at[where], natural.at[where], stream_sems.at[i])

    keys_values = pl.ds(1, 2)
    pieces = [
        fetch(0, keys_values, pl.ds(0, PIECE), columns(0)),
        fetch(1, keys_values, pl.ds(PIECE, tokens - PIECE), columns(0)),
    ]
    rest = [fetch(2, pl.ds(0, 1), slice(None), columns(0))]
    rest += [fetch(2 + g, slice(None), slice(None), columns(g)) for g in range(1, groups)]
    tables = [
        pltpu.make_async_copy(src, dst, table_sems.at[i])
        for i, (src, dst) in enumerate(
            [(rate_hbm, rate_nat), (taps_hbm, taps_nat), (residue_hbm, residue_nat), (bias_hbm, bias_nat)]
        )
    ]
    for copy in tables[:2] + pieces + rest + tables[2:]:
        copy.start()
    for copy in tables[:2]:
        copy.wait()

    def wait_rest():
        for copy in tables[2:] + rest:
            copy.wait()


    @pl.when(jnp.logical_not(is_last()))
    def _():
        state_kernel(
            0, rate_nat, taps_nat, residue_nat, bias_nat, natural,
            kv_ref, states_ref, own_ref, tables_ref, ka, kb, va, vb, lambda n: pieces[n].wait(), wait_rest,
        )
        for g in range(groups):
            edge_rows(natural, edges_ref, ka, g)
        state = [own_ref[m] for m in range(own_ref.shape[0])]
        edges = [[edges_ref[g, i] for i in range(TAIL + HEAD)] for g in range(groups)]
        pack(message_ref, state + tails_and_heads(edges, True))

    @pl.when(is_last())
    def _():
        for copy in pieces:
            copy.wait()
        wait_rest()
        message_ref[...] = jnp.zeros(message_ref.shape, BF16)


def is_last():
    return lax.axis_index("context") == lax.axis_size("context") - 1


def later_states_kernel(g, inputs, before, own_edges, outs, scratch):
    def states(group, refs):
        state_kernel(group, *inputs, *refs, *scratch, lambda n: None, lambda: None)

    if outs:

        @pl.when(jnp.logical_not(is_last()))
        def _():
            states(g, outs[:4])
            pack(outs[4], [outs[2][m] for m in range(outs[2].shape[0])])

    @pl.when(is_last())
    def _():
        states(g - 1, before)
        if own_edges is not None:
            for group in range(own_edges.shape[0]):
                edge_rows(inputs[-1], own_edges, scratch[0], group)
        if outs:
            outs[4][...] = jnp.zeros(outs[4].shape, BF16)


def near_group(g, q_nat, tables_ref, kv_ref, near_ref, query_ref, taps, qa, qb):
    tokens = kv_ref.shape[0]
    chunks = tokens // CHUNK
    zero = jnp.zeros((SUB, LANES), F32)
    modes, rate, w = table_parts(tables_ref)
    p = [jnp.exp(-r) for r in rate]
    gain = [tables_ref[gain_row(modes, m)] for m in range(modes)]
    taps[0] = total(gain) + tables_ref[gain_row(modes, modes)]
    for i in range(1, CHUNK):
        gain = [a * b for a, b in zip(gain, p)]
        taps[i] = total(gain)
    h = [taps[i] for i in range(CHUNK)]
    turn_in(q_nat, qa, 0, g)

    def one_chunk(c, qs, last):
        q1, q2 = last
        window = []
        for i in range(CHUNK):
            t = c * CHUNK + i
            q = row(qs, i)
            query_ref[t] = w[0] * q + w[1] * q1 + w[2] * q2
            q1, q2 = q, q1
            window.append(kv_ref[t])
            near_ref[t] = total(h[n] * window[i - n] for n in range(i + 1))
        return q1, q2

    def two_chunks(it, last):
        c = 2 * it
        turn_in(q_nat, qb, chunk_rows(c + 1), g)
        last = one_chunk(c, qa, last)
        turn_in(q_nat, qa, chunk_rows(jnp.minimum(c + 2, chunks - 1)), g)
        return one_chunk(c + 1, qb, last)

    lax.fori_loop(0, chunks // 2, two_chunks, (zero, zero))


def merge_group(
    span, tokens, g, last, own_ref, edges_ref, got_ref, first_got, tables_ref, entering_ref, rim_ref,
    message_ref, entering_out, rim_out, next_ref, edges_out,
):
    modes, rate, w = table_parts(tables_ref)
    groups = edges_ref.shape[0]
    rank = lax.axis_index("context")
    right = (rank & span) != 0
    ahead = rank & (span - 1)
    length = 1.0 * tokens * span
    zero = jnp.zeros((SUB, LANES), F32)

    def pick(a, b):
        return [jnp.where(right, x, y) for x, y in zip(a, b)]

    def edge(group):
        rows = [edges_ref[group, i] for i in range(TAIL + HEAD)]
        return rows[:TAIL], rows[TAIL:]

    state, other = [own_ref[m] for m in range(modes)], unpack(got_ref, 0, modes)
    tail, head = edge(g)
    other_tail, other_head = other_edges(first_got, g, groups, modes, True)
    products = first_products(w, pick(head, other_head), pick(other_tail, tail))
    left_state, right_state = pick(other, state), pick(state, other)
    rows = [
        right_state[m] + jnp.exp(-length * rate[m]) * left_state[m] + first_terms(rate[m], products, length)
        for m in range(modes)
    ]
    if not last:
        for m in range(modes):
            next_ref[m] = rows[m]
    if g == 0:
        edges = []
        for group in range(groups):
            mine, theirs = edge(group), other_edges(first_got, group, groups, modes, True)
            edges.append(pick(mine[0], theirs[0]) + pick(theirs[1], mine[1]))
            for i, value in enumerate(edges[-1]):
                edges_out[group, i] = value
        rows = rows + tails_and_heads(edges, not last)
    pack(message_ref, rows)
    entering = [zero if entering_ref is None else entering_ref[m] for m in range(modes)]
    entering = enter(tokens, span, rank, rate, w, head, other, other_tail, entering)
    for m in range(modes):
        entering_out[m] = entering[m]
    for i in range(TAIL):
        old = zero if rim_ref is None else rim_ref[i]
        rim_out[i] = jnp.where(right & (ahead == 0), other_tail[i], old)


def emit_group(
    which, near_ref, query_ref, states_ref, tables_ref, head, entering, rim, out_ref, state, power, rim_ref, ta, tb, piece_done
):
    rank = lax.axis_index("context")
    modes, rate, w = table_parts(tables_ref)
    p = [jnp.exp(-r) for r in rate]
    for m in range(modes):
        power[m] = jnp.exp(-CHUNK * rate[m])
    if which.start == 0:
        for m in range(modes):
            state[m] = entering[m]
        products = first_products(w, head, rim)
        for i in range(2):
            rim_ref[i] = jnp.where(rank == 0, 0.0, products[i])
        rim_ref[2] = w[1] * rim[3] + w[2] * rim[0]
        rim_ref[3] = w[2] * rim[3]

    def one_chunk(c, turned, first):
        x = [tables_ref[gain_row(modes, m)] * (states_ref[c, m] + state[m]) for m in range(modes)]
        for i in range(CHUNK):
            t = c * CHUNK + i
            x = [a * b for a, b in zip(x, p)]
            near, query = near_ref[t], query_ref[t]
            if first and i < 2:
                x = [a + tables_ref[gain_row(modes, m)] * rim_ref[i] for m, a in enumerate(x)]
                near = near + tables_ref[gain_row(modes, modes)] * rim_ref[i]
                query = query + rim_ref[2 + i]
            mixed = (near + total(x)).astype(BF16).astype(F32)
            turned[pl.ds(i, SUB, stride=STRIDE), :] = query * mixed
        for m in range(modes):
            if first:
                held = (state[m] * p[m] + rim_ref[0]) * p[m] + rim_ref[1]
                state[m] = held * jnp.exp(-(CHUNK - 2) * tables_ref[m])
            else:
                state[m] = state[m] * power[m]

    def turn_out(turned, c):
        for j in range(SUB):
            out_ref[pl.ds(chunk_rows(c), CHUNK), pl.ds(j * LANES, LANES)] = turned[pl.ds(j * STRIDE, CHUNK), :].astype(BF16)

    begin = which.start
    one_chunk(begin, ta, begin == 0)
    one_chunk(begin + 1, tb, False)
    turn_out(ta, begin)

    def two_chunks(it, none):
        c = 2 * it
        one_chunk(c, ta, False)
        turn_out(tb, c - 1)
        one_chunk(c + 1, tb, False)
        turn_out(ta, c)
        pl.when((it & 1) == 0)(lambda: piece_done(it * 2 * CHUNK // PIECE - 1))
        return none

    lax.fori_loop(begin // 2 + 1, which.stop // 2, two_chunks, 0)
    turn_out(tb, which.stop - 1)
    piece_done(which.stop * CHUNK // PIECE - 1)


def emit_out(emit, ready, out_hbm, out_ref, ready_sems, sems):
    tokens, last = out_ref.shape[0], out_hbm.shape[1] // GROUP - 1
    copies = [
        pltpu.make_async_copy(buffer.at[rows], out_hbm.at[rows, columns(g)], ready_sems.at[i])
        for i, (rows, g, buffer) in enumerate(ready)
    ]
    for copy in copies:
        copy.start()

    def send(n):
        rows = pl.ds(pl.multiple_of(n * PIECE, PIECE), PIECE)
        return pltpu.make_async_copy(out_ref.at[rows], out_hbm.at[rows, columns(last)], sems.at[n])

    emit(out_ref, lambda n: send(n).start())
    for copy in copies + [send(n) for n in range(tokens // PIECE)]:
        copy.wait()


def is_early(span):
    return (lax.axis_index("context") & span) == 0


def emit_known(which, g, fixed, edges_ref, entering_ref, rim_ref, out_ref, scratch, piece_done):
    entering = [entering_ref[m] for m in range(entering_ref.shape[0])]
    rim = [rim_ref[i] for i in range(TAIL)]
    head = [edges_ref[g, TAIL + i] for i in range(HEAD)]
    emit_group(which, *fixed, head, entering, rim, out_ref, *scratch, piece_done)


def emit_merged(span, g, fixed, edges_ref, entering_ref, rim_ref, merged_edges, got_ref, first_got, out_ref, scratch, piece_done):
    tokens, modes = fixed[0].shape[0], entering_ref.shape[0]
    rank = lax.axis_index("context")
    _, rate, w = table_parts(fixed[3])
    other_tail, _ = other_edges(first_got, g, edges_ref.shape[0], modes, False)
    entering = enter(
        tokens, span, rank, rate, w, [merged_edges[g, TAIL + i] for i in range(HEAD)],
        unpack(got_ref, 0, modes), other_tail, [entering_ref[m] for m in range(modes)],
    )
    begins = (rank & (span - 1)) == 0
    rim = [jnp.where(begins, other_tail[i], rim_ref[i]) for i in range(TAIL)]
    head = [edges_ref[g, TAIL + i] for i in range(HEAD)]
    emit_group(range(tokens // CHUNK), *fixed, head, entering, rim, out_ref, *scratch, piece_done)


VM = pl.BlockSpec(memory_space=pltpu.VMEM)
HB = pl.BlockSpec(memory_space=pltpu.HBM)


def call(kernel, name, operands, outs, scratch, mib, flops, in_specs=None, out_specs=None, aliases=None):
    in_specs = in_specs or [VM] * len(operands)
    operands = [
        pltpu.with_memory_space_constraint(x, pltpu.VMEM if spec is VM else pltpu.HBM) for x, spec in zip(operands, in_specs)
    ]
    return pl.pallas_call(
        kernel,
        in_specs=in_specs,
        out_specs=[VM] * len(outs) if out_specs is None else out_specs,
        out_shape=outs,
        scratch_shapes=scratch,
        input_output_aliases=aliases or {},
        compiler_params=pltpu.CompilerParams(vmem_limit_bytes=mib * 2**20),
        cost_estimate=pl.CostEstimate(flops=flops, bytes_accessed=2**20, transcendentals=0),
        name=name,
    )(*operands)


def body(streams, short_filter, decay_rate, residue, bias):
    tokens, _, channels = streams.shape
    modes = decay_rate.shape[1]
    groups = channels // GROUP
    chunks, pieces = tokens // CHUNK, tokens // PIECE
    size = lax.axis_size("context")
    vector = (SUB, LANES)
    turned = pltpu.VMEM((SUB * STRIDE, LANES), F32)
    dma = pltpu.SemaphoreType.DMA
    work = tokens * channels

    def vectors(*shape):
        return pltpu.VMEM(shape + vector, F32)

    def message_type(count):
        return pltpu.VMEM((count // 2, 2 * SUB, LANES), BF16)

    def swap(message, span):
        return lax.ppermute(message, "context", [(i, i ^ span) for i in range(size)])

    edge = TAIL + HEAD
    state_types = [vectors(tokens), vectors(chunks, modes), vectors(modes), vectors(2 * modes + 10)]
    input_types = [
        pltpu.VMEM((modes, channels), F32), pltpu.VMEM((3, 3, channels), F32), pltpu.VMEM((modes, channels), F32),
        vectors(groups), pltpu.VMEM((3, tokens, channels), BF16),
    ]
    *first, first_message, own_edges, rates, taps, residues, biases, natural = call(
        first_states_kernel, "states",
        [streams.transpose(1, 0, 2), short_filter, decay_rate.T, residue.T, bias.reshape((groups,) + vector)],
        state_types + [message_type(modes + groups * edge), vectors(groups, edge)] + input_types,
        [turned] * 4 + [dma((4,)), dma((groups + 2,))], 4, 24 * work, in_specs=[HB] * 5,
    )
    made, message = [first], [first_message]
    inputs = [rates, taps, residues, biases, natural]
    for g in range(1, groups + 1):
        held = made[-1] + ([own_edges] if g == 1 else [])
        outs = state_types + [message_type(modes)] if g < groups else []

        def kernel(*refs, g=g, count=len(held), fresh=len(outs)):
            ins, refs = refs[:5], refs[5 + count :]
            before, outs, scratch = refs[:count], refs[count : count + fresh], refs[count + fresh :]
            later_states_kernel(g, ins, before[:4], before[4] if g == 1 else None, outs, scratch)

        results = call(
            kernel, "states", inputs + held, state_types + ([vectors(groups, edge)] if g == 1 else []) + outs,
            [turned] * 4, 4, 24 * work, aliases={5 + i: i for i in range(len(held))},
        )
        made[-1] = list(results[:4])
        own_edges = results[4] if g == 1 else own_edges
        if outs:
            made.append(list(results[len(held) : len(held) + 4]))
            message.append(results[-1])
    key_value, states, own, tables = zip(*made)

    def near_all(early, after):
        def kernel(*refs):
            natural, refs = refs[0], refs[1 + len(after) :]
            ins, outs, scratch = refs[: 2 * groups], refs[2 * groups : 4 * groups], refs[4 * groups :]

            @pl.when(is_early(size // 2) == early)
            def _():
                for g in range(groups):
                    near_group(g, natural.at[0], *ins[2 * g : 2 * g + 2], *outs[2 * g : 2 * g + 2], *scratch)

        operands = sum([[tables[g], key_value[g]] for g in range(groups)], [])
        outs = call(
            kernel, "near", [natural] + after + operands, [vectors(tokens)] * (2 * groups),
            [vectors(CHUNK), turned, turned], 4, 24 * work,
        )
        return [list(outs[2 * g : 2 * g + 2]) for g in range(groups)]

    half = pltpu.VMEM((tokens, GROUP), BF16)
    emit_scratch = [vectors(modes), vectors(4), turned, turned]

    merged, edges = list(own), own_edges
    entering, rim = [None] * groups, [None] * groups
    begun, begun_state = [], []
    span = 1
    while True:
        got = [swap(message[g], span) for g in range(groups)]
        if 2 * span >= size:
            break
        last, first = 4 * span >= size, entering[0] is None
        if first:
            near = near_all(True, [])
        old_edges = edges
        for g in range(groups):
            part = range(EARLY[g - 1] if g else 0, EARLY[g]) if last and g < len(EARLY) else range(0)
            early = []
            if part:
                early = [*near[0], states[0], tables[0], own_edges] + ([entering[0], rim[0], begun_state[-1]] if g else [])
            operands = [merged[g], old_edges, got[g], got[0], tables[g]] + ([] if first else [entering[g], rim[g]])
            count = modes + (groups * (TAIL if last else edge) if g == 0 else 0)
            outs = [message_type(count), vectors(modes), vectors(TAIL)]
            outs += [] if last else [vectors(modes)]
            outs += [vectors(groups, edge)] if g == 0 else []
            outs += [half, vectors(modes)] if part else []

            def kernel(*refs, g=g, span=span, last=last, first=first, part=part, extra=len(early), results=len(outs)):
                refs = list(refs)
                ins = [refs.pop(0) for _ in range(5)] + ([None, None] if first else [refs.pop(0) for _ in range(2)])
                more = [refs.pop(0) for _ in range(extra)]
                produced = [refs.pop(0) for _ in range(results)]
                state_out = None if last else produced[3]
                edges_out = produced[3 if last else 4] if g == 0 else None
                merge_group(span, tokens, g, last, *ins, *produced[:3], state_out, edges_out)
                if part:

                    @pl.when(is_early(2 * span))
                    def _():
                        out_ref, state_ref = produced[-2:]
                        for m in range(modes if g else 0):
                            state_ref[m] = more[7][m]
                        known = more[5:7] if g else produced[1:3]
                        emit_known(part, 0, more[:4], more[4], *known, out_ref, [state_ref] + refs, lambda n: None)

            made = list(call(kernel, "merge", operands + early, outs, emit_scratch if part else [], 4, 2**20))
            message[g], entering[g], rim[g] = made[:3]
            if not last:
                merged[g] = made[3]
            if g == 0:
                edges = made[3 if last else 4]
            if part:
                begun.append((pl.ds(part.start * CHUNK, len(part) * CHUNK), made[-2]))
                begun_state.append(made[-1])
        span *= 2

    out_type = pltpu.HBM((tokens, channels), BF16)
    pair = [[entering[g], rim[g]] for g in range(groups)]
    begin = EARLY[len(begun) - 1] if begun else 0

    def kernel(own_edges, *refs):
        refs = list(refs)
        ready = [refs.pop(0) for _ in begun]
        begun_state = refs.pop(0) if begun else None
        ins, refs = [refs[i * 6 : i * 6 + 6] for i in range(groups)], refs[groups * 6 :]
        out_hbm, out_refs, state, scratch = refs[0], refs[1 : 1 + groups], refs[1 + groups], refs[2 + groups : 6 + groups]

        @pl.when(is_early(span))
        def _():
            for m in range(modes if begun else 0):
                state[m] = begun_state[m]
            for g in range(groups - 1):
                which = range(0 if g else begin, chunks)
                emit_known(which, g, ins[g][:4], own_edges, *ins[g][4:], out_refs[g], [state, *scratch], lambda n: None)

            def emit(out, piece_done):
                emit_known(range(chunks), groups - 1, ins[-1][:4], own_edges, *ins[-1][4:], out, [state, *scratch], piece_done)

            done = [(rows, 0, buffer) for (rows, _), buffer in zip(begun, ready)]
            done += [(pl.ds(begin * CHUNK, tokens - begin * CHUNK), 0, out_refs[0])]
            done += [(pl.ds(0, tokens), g, out_refs[g]) for g in range(1, groups - 1)]
            emit_out(emit, done, out_hbm, out_refs[-1], *refs[6 + groups :])

    out = call(
        kernel, "early",
        [own_edges] + [buffer for _, buffer in begun] + begun_state[-1:]
        + sum([[*near[g], states[g], tables[g], *pair[g]] for g in range(groups)], []),
        [out_type], [half] * groups + [vectors(modes)] + emit_scratch + [dma((groups + 1,)), dma((pieces,))],
        4, 40 * work, out_specs=[HB],
    )[0]
    near = near_all(False, [entering[-1]])
    fixed = [[*near[g], states[g], tables[g]] for g in range(groups)]
    halves = []
    for g in range(groups):
        final = g + 1 == groups
        operands = fixed[g] + [own_edges] + pair[g] + [edges, got[g], got[0]] + (halves + [out] if final else [])

        def kernel(*refs, g=g, final=final):
            ins, refs = refs[:10], refs[10:]
            if final:
                done, (_, out_hbm, out_ref, *scratch) = refs[: groups - 1], refs[groups - 1 :]
            else:
                out_ref, *scratch = refs

            @pl.when(jnp.logical_not(is_early(span)))
            def _():
                def emit(out, piece_done):
                    emit_merged(span, g, ins[:4], *ins[4:], out, scratch[:5], piece_done)

                if final:
                    ready = [(pl.ds(0, tokens), i, x) for i, x in enumerate(done)]
                    emit_out(emit, ready, out_hbm, out_ref, *scratch[5:])
                else:
                    emit(out_ref, lambda n: None)

        if not final:
            halves += call(kernel, "late", operands, [half], [vectors(modes)] + emit_scratch, 4, 20 * work)
    return call(
        kernel, "late", operands, [out_type],
        [half, vectors(modes)] + emit_scratch + [dma((groups,)), dma((pieces,))], 4, 20 * work,
        in_specs=[VM] * (len(operands) - 1) + [HB], out_specs=[HB], aliases={len(operands) - 1: 0},
    )[0]


def solution(mesh):
    in_specs = (
        P(("dp", "context"), None, "tensor"),
        P(None, None, "tensor"),
        P("tensor", None),
        P("tensor", None),
        P("tensor"),
    )
    out_specs = P(("dp", "context"), "tensor")
    return jax.shard_map(body, mesh=mesh, in_specs=in_specs, out_specs=out_specs, check_vma=False)
```

```python
import jax
import jax.numpy as jnp
from jax import lax
from jax.experimental import pallas as pl
from jax.experimental.pallas import tpu as pltpu
from jax.sharding import PartitionSpec as P

F32 = jnp.float32
BF16 = jnp.bfloat16
LANES = 128
SUB = 8
GROUP = LANES * SUB
CHUNK = 16
PIECE = 64
STRIDE = CHUNK + 8
EARLY = (4, 6)
HEAD = 4
TAIL = 6


def total(values):
    values = list(values)
    while len(values) > 1:
        pairs = [values[i] + values[i + 1] for i in range(0, len(values) - 1, 2)]
        values = pairs + ([values[-1]] if len(values) % 2 else [])
    return values[0]


def columns(g):
    return pl.ds(g * GROUP, GROUP)


def turn_in(source, turned, start, g):
    for j in range(SUB):
        turned[pl.ds(j * STRIDE, CHUNK), :] = source[pl.ds(start, CHUNK), pl.ds(g * GROUP + j * LANES, LANES)].astype(F32)


def turn_rows(source, turned, rows, g):
    for j in range(SUB):
        turned[pl.ds(j * STRIDE, rows), :] = source[:, pl.ds(g * GROUP + j * LANES, LANES)]


def row(turned, i):
    return turned[pl.ds(i, SUB, stride=STRIDE), :]


def chunk_rows(c):
    return pl.multiple_of(c * CHUNK, CHUNK)


def pack(message_ref, rows):
    for i in range(message_ref.shape[0]):
        message_ref[i] = jnp.concatenate(rows[2 * i : 2 * i + 2], axis=0).astype(BF16)


def unpack(message_ref, first, count):
    rows = []
    for i in range(first // 2, (first + count) // 2):
        pair = message_ref[i].astype(F32)
        rows += [pair[:SUB], pair[SUB:]]
    return rows


def first_products(w, head, tail):
    features = []
    for s, rows in ((1, (tail[1], tail[4], head[0], head[2])), (2, (tail[2], tail[5], head[1], head[3]))):
        features.append([w[3 * s] * rows[2 + t] + w[3 * s + 1] * rows[1 + t] + w[3 * s + 2] * rows[t] for t in range(2)])
    return [(features[0][t] * features[1][t]).astype(BF16).astype(F32) for t in range(2)]


def first_terms(rate, products, steps):
    return jnp.exp((1.0 - steps) * rate) * products[0] + jnp.exp((2.0 - steps) * rate) * products[1]


def enter(tokens, span, rank, rate, w, head, other, other_tail, entering):
    right = (rank & span) != 0
    ahead = rank & (span - 1)
    steps = (tokens * ahead).astype(F32)
    products = first_products(w, head, other_tail)
    result = []
    for m, r in enumerate(rate):
        missing = jnp.where(ahead > 0, first_terms(r, products, jnp.maximum(steps, 2.0)), 0.0)
        result.append(jnp.where(right, entering[m] + jnp.exp(-steps * r) * other[m] + missing, entering[m]))
    return result


def table_parts(tables_ref):
    modes = (tables_ref.shape[0] - 10) // 2
    rate = [tables_ref[m] for m in range(modes)]
    return modes, rate, [tables_ref[modes + i] for i in range(9)]


def gain_row(modes, m):
    return modes + 9 + m


def state_kernel(
    g, rate_nat, taps_nat, residue_nat, bias_nat, natural,
    kv_ref, states_ref, own_ref, tables_ref, ka, kb, va, vb, wait_piece, wait_rest,
):
    q_nat, k_nat, v_nat = (natural.at[i] for i in range(3))
    tokens, modes = natural.shape[1], rate_nat.shape[0]
    chunks = tokens // CHUNK
    rank = lax.axis_index("context")
    zero = jnp.zeros((SUB, LANES), F32)
    turn_rows(rate_nat, ka, modes, g)
    for stream in range(3):
        turn_rows(taps_nat.at[stream], (kb, va, vb)[stream], 3, g)
    p = []
    for m in range(modes):
        rate = row(ka, m)
        tables_ref[m] = rate
        p.append(jnp.exp(-rate))
    w = []
    for i in range(9):
        w.append(row((kb, va, vb)[i // 3], i % 3))
        tables_ref[modes + i] = w[i]
    wk, wv = w[3:6], w[6:9]
    wait_piece(0)
    turn_in(k_nat, ka, 0, g)
    turn_in(v_nat, va, 0, g)
    def one_chunk(c, ks, vs, acc, last):
        k1, k2, v1, v2 = last
        for m in range(modes):
            states_ref[c, m] = acc[m]
        for i in range(CHUNK):
            k, v = row(ks, i), row(vs, i)
            key = wk[0] * k + wk[1] * k1 + wk[2] * k2
            value = wv[0] * v + wv[1] * v1 + wv[2] * v2
            k1, k2, v1, v2 = k, k1, v, v1
            product = (key * value).astype(BF16).astype(F32)
            if i < 2:
                product = jnp.where((c > 0) | (rank == 0), product, 0.0)
            kv_ref[c * CHUNK + i] = product
            acc = [a * b + product for a, b in zip(acc, p)]
        return acc, (k1, k2, v1, v2)

    def two_chunks(it, carry):
        acc, last = carry
        c = 2 * it
        pl.when(it == PIECE // (2 * CHUNK) - 1)(lambda: wait_piece(1))
        turn_in(k_nat, kb, chunk_rows(c + 1), g)
        turn_in(v_nat, vb, chunk_rows(c + 1), g)
        acc, last = one_chunk(c, ka, va, acc, last)
        ahead = chunk_rows(jnp.minimum(c + 2, chunks - 1))
        turn_in(k_nat, ka, ahead, g)
        turn_in(v_nat, va, ahead, g)
        return one_chunk(c + 1, kb, vb, acc, last)

    acc, _ = lax.fori_loop(0, chunks // 2, two_chunks, ([zero] * modes, (zero,) * 4))
    for m in range(modes):
        own_ref[m] = acc[m]
    wait_rest()
    turn_rows(residue_nat, ka, modes, g)
    for m in range(modes):
        tables_ref[gain_row(modes, m)] = row(ka, m)
    tables_ref[gain_row(modes, modes)] = bias_nat[g]


def edge_rows(natural, edges_ref, turned, g):
    tokens = natural.shape[1]
    for stream in range(3):
        turn_in(natural.at[stream], turned, tokens - CHUNK, g)
        for i in range(2):
            edges_ref[g, 3 * i + stream] = row(turned, CHUNK - 2 + i)
        if stream:
            turn_in(natural.at[stream], turned, 0, g)
            for i in range(2):
                edges_ref[g, TAIL + 2 * i + stream - 1] = row(turned, i)


def tails_and_heads(edges, heads):
    rows = sum([e[:TAIL] for e in edges], [])
    return rows + sum([e[TAIL:] for e in edges], []) if heads else rows


def other_edges(first_got, g, groups, modes, heads):
    tail = unpack(first_got, modes + TAIL * g, TAIL)
    return tail, unpack(first_got, modes + TAIL * groups + HEAD * g, HEAD) if heads else None


def first_states_kernel(
    streams, taps_hbm, rate_hbm, residue_hbm, bias_hbm,
    kv_ref, states_ref, own_ref, tables_ref, message_ref, edges_ref, rate_nat, taps_nat, residue_nat, bias_nat, natural,
    ka, kb, va, vb, table_sems, stream_sems,
):
    _, tokens, channels = natural.shape
    groups = channels // GROUP
    keys_values = pl.ds(1, 2)
    pieces = [
        fetch(streams, natural, stream_sems.at[0], keys_values, pl.ds(0, PIECE), columns(0)),
        fetch(streams, natural, stream_sems.at[1], keys_values, pl.ds(PIECE, tokens - PIECE), columns(0)),
    ]
    rest = other_inputs(streams, natural, stream_sems, 2)
    tables = [
        pltpu.make_async_copy(src, dst, table_sems.at[i])
        for i, (src, dst) in enumerate(
            [(rate_hbm, rate_nat), (taps_hbm, taps_nat), (residue_hbm, residue_nat), (bias_hbm, bias_nat)]
        )
    ]
    for copy in tables[:2] + pieces + tables[2:]:
        copy.start()

    def wait_rest():
        for copy in tables[2:] + rest:
            copy.wait()

    @pl.when(jnp.logical_not(is_last()))
    def _():
        for copy in rest:
            copy.start()
        for copy in tables[:2]:
            copy.wait()
        state_kernel(
            0, rate_nat, taps_nat, residue_nat, bias_nat, natural,
            kv_ref, states_ref, own_ref, tables_ref, ka, kb, va, vb, lambda n: pieces[n].wait(), wait_rest,
        )
        for g in range(groups):
            edge_rows(natural, edges_ref, ka, g)
        state = [own_ref[m] for m in range(own_ref.shape[0])]
        edges = [[edges_ref[g, i] for i in range(TAIL + HEAD)] for g in range(groups)]
        pack(message_ref, state + tails_and_heads(edges, True))

    @pl.when(is_last())
    def _():
        for copy in tables + pieces:
            copy.wait()
        message_ref[...] = jnp.zeros(message_ref.shape, BF16)


def fetch(streams, natural, sem, *where):
    return pltpu.make_async_copy(streams.at[where], natural.at[where], sem)


def other_inputs(streams, natural, sems, first):
    groups = natural.shape[2] // GROUP
    copies = [fetch(streams, natural, sems.at[first], pl.ds(0, 1), slice(None), columns(0))]
    for g in range(1, groups):
        copies.append(fetch(streams, natural, sems.at[first + g], slice(None), slice(None), columns(g)))
    return copies


def is_last():
    return lax.axis_index("context") == lax.axis_size("context") - 1


def later_states_kernel(g, inputs, before, own_edges, streams, sems, outs, scratch):
    def states(group, refs):
        state_kernel(group, *inputs, *refs, *scratch, lambda n: None, lambda: None)

    if outs:

        @pl.when(jnp.logical_not(is_last()))
        def _():
            states(g, outs[:4])
            pack(outs[4], [outs[2][m] for m in range(outs[2].shape[0])])

    @pl.when(is_last())
    def _():
        rest = other_inputs(streams, inputs[-1], sems, 0) if g == 1 else []
        for copy in rest:
            copy.start()
        states(g - 1, before)
        for copy in rest:
            copy.wait()
        if g == 1:
            for group in range(own_edges.shape[0]):
                edge_rows(inputs[-1], own_edges, scratch[0], group)
        if outs:
            outs[4][...] = jnp.zeros(outs[4].shape, BF16)


def near_group(g, q_nat, tables_ref, kv_ref, near_ref, query_ref, taps, qa, qb):
    tokens = kv_ref.shape[0]
    chunks = tokens // CHUNK
    zero = jnp.zeros((SUB, LANES), F32)
    modes, rate, w = table_parts(tables_ref)
    p = [jnp.exp(-r) for r in rate]
    gain = [tables_ref[gain_row(modes, m)] for m in range(modes)]
    taps[0] = total(gain) + tables_ref[gain_row(modes, modes)]
    for i in range(1, CHUNK):
        gain = [a * b for a, b in zip(gain, p)]
        taps[i] = total(gain)
    h = [taps[i] for i in range(CHUNK)]
    turn_in(q_nat, qa, 0, g)

    def one_chunk(c, qs, last):
        q1, q2 = last
        window = []
        for i in range(CHUNK):
            t = c * CHUNK + i
            q = row(qs, i)
            query_ref[t] = w[0] * q + w[1] * q1 + w[2] * q2
            q1, q2 = q, q1
            window.append(kv_ref[t])
            near_ref[t] = total(h[n] * window[i - n] for n in range(i + 1))
        return q1, q2

    def two_chunks(it, last):
        c = 2 * it
        turn_in(q_nat, qb, chunk_rows(c + 1), g)
        last = one_chunk(c, qa, last)
        turn_in(q_nat, qa, chunk_rows(jnp.minimum(c + 2, chunks - 1)), g)
        return one_chunk(c + 1, qb, last)

    lax.fori_loop(0, chunks // 2, two_chunks, (zero, zero))


def merge_group(
    span, tokens, g, last, own_ref, edges_ref, got_ref, first_got, tables_ref, entering_ref, rim_ref,
    message_ref, entering_out, rim_out, next_ref, edges_out,
):
    modes, rate, w = table_parts(tables_ref)
    groups = edges_ref.shape[0]
    rank = lax.axis_index("context")
    right = (rank & span) != 0
    ahead = rank & (span - 1)
    length = 1.0 * tokens * span
    zero = jnp.zeros((SUB, LANES), F32)

    def pick(a, b):
        return [jnp.where(right, x, y) for x, y in zip(a, b)]

    def edge(group):
        rows = [edges_ref[group, i] for i in range(TAIL + HEAD)]
        return rows[:TAIL], rows[TAIL:]

    state, other = [own_ref[m] for m in range(modes)], unpack(got_ref, 0, modes)
    tail, head = edge(g)
    other_tail, other_head = other_edges(first_got, g, groups, modes, True)
    products = first_products(w, pick(head, other_head), pick(other_tail, tail))
    left_state, right_state = pick(other, state), pick(state, other)
    rows = [
        right_state[m] + jnp.exp(-length * rate[m]) * left_state[m] + first_terms(rate[m], products, length)
        for m in range(modes)
    ]
    if not last:
        for m in range(modes):
            next_ref[m] = rows[m]
    if g == 0:
        edges = []
        for group in range(groups):
            mine, theirs = edge(group), other_edges(first_got, group, groups, modes, True)
            edges.append(pick(mine[0], theirs[0]) + pick(theirs[1], mine[1]))
            for i, value in enumerate(edges[-1]):
                edges_out[group, i] = value
        rows = rows + tails_and_heads(edges, not last)
    pack(message_ref, rows)
    entering = [zero if entering_ref is None else entering_ref[m] for m in range(modes)]
    entering = enter(tokens, span, rank, rate, w, head, other, other_tail, entering)
    for m in range(modes):
        entering_out[m] = entering[m]
    for i in range(TAIL):
        old = zero if rim_ref is None else rim_ref[i]
        rim_out[i] = jnp.where(right & (ahead == 0), other_tail[i], old)


def emit_group(
    which, near_ref, query_ref, states_ref, tables_ref, head, entering, rim, out_ref, state, power, rim_ref, ta, tb, piece_done
):
    rank = lax.axis_index("context")
    modes, rate, w = table_parts(tables_ref)
    p = [jnp.exp(-r) for r in rate]
    for m in range(modes):
        power[m] = jnp.exp(-CHUNK * rate[m])
    if which.start == 0:
        for m in range(modes):
            state[m] = entering[m]
        products = first_products(w, head, rim)
        for i in range(2):
            rim_ref[i] = jnp.where(rank == 0, 0.0, products[i])
        rim_ref[2] = w[1] * rim[3] + w[2] * rim[0]
        rim_ref[3] = w[2] * rim[3]

    def one_chunk(c, turned, first):
        x = [tables_ref[gain_row(modes, m)] * (states_ref[c, m] + state[m]) for m in range(modes)]
        for i in range(CHUNK):
            t = c * CHUNK + i
            x = [a * b for a, b in zip(x, p)]
            near, query = near_ref[t], query_ref[t]
            if first and i < 2:
                x = [a + tables_ref[gain_row(modes, m)] * rim_ref[i] for m, a in enumerate(x)]
                near = near + tables_ref[gain_row(modes, modes)] * rim_ref[i]
                query = query + rim_ref[2 + i]
            mixed = (near + total(x)).astype(BF16).astype(F32)
            turned[pl.ds(i, SUB, stride=STRIDE), :] = query * mixed
        for m in range(modes):
            if first:
                held = (state[m] * p[m] + rim_ref[0]) * p[m] + rim_ref[1]
                state[m] = held * jnp.exp(-(CHUNK - 2) * tables_ref[m])
            else:
                state[m] = state[m] * power[m]

    def turn_out(turned, c):
        for j in range(SUB):
            out_ref[pl.ds(chunk_rows(c), CHUNK), pl.ds(j * LANES, LANES)] = turned[pl.ds(j * STRIDE, CHUNK), :].astype(BF16)

    begin = which.start
    one_chunk(begin, ta, begin == 0)
    one_chunk(begin + 1, tb, False)
    turn_out(ta, begin)

    def two_chunks(it, none):
        c = 2 * it
        one_chunk(c, ta, False)
        turn_out(tb, c - 1)
        one_chunk(c + 1, tb, False)
        turn_out(ta, c)
        pl.when((it & 1) == 0)(lambda: piece_done(it * 2 * CHUNK // PIECE - 1))
        return none

    lax.fori_loop(begin // 2 + 1, which.stop // 2, two_chunks, 0)
    turn_out(tb, which.stop - 1)
    piece_done(which.stop * CHUNK // PIECE - 1)


def emit_out(emit, ready, out_hbm, out_ref, ready_sems, sems):
    tokens, last = out_ref.shape[0], out_hbm.shape[1] // GROUP - 1
    copies = [
        pltpu.make_async_copy(buffer.at[rows], out_hbm.at[rows, columns(g)], ready_sems.at[i])
        for i, (rows, g, buffer) in enumerate(ready)
    ]
    for copy in copies:
        copy.start()

    def send(n):
        rows = pl.ds(pl.multiple_of(n * PIECE, PIECE), PIECE)
        return pltpu.make_async_copy(out_ref.at[rows], out_hbm.at[rows, columns(last)], sems.at[n])

    emit(out_ref, lambda n: send(n).start())
    for copy in copies + [send(n) for n in range(tokens // PIECE)]:
        copy.wait()


def is_early(span):
    return (lax.axis_index("context") & span) == 0


def is_first(span):
    rank = lax.axis_index("context")
    return is_early(span) & ((rank & (span // 2)) == 0)


def emit_known(which, g, fixed, edges_ref, entering_ref, rim_ref, out_ref, scratch, piece_done):
    entering = [entering_ref[m] for m in range(entering_ref.shape[0])]
    rim = [rim_ref[i] for i in range(TAIL)]
    head = [edges_ref[g, TAIL + i] for i in range(HEAD)]
    emit_group(which, *fixed, head, entering, rim, out_ref, *scratch, piece_done)


def emit_merged(span, g, fixed, edges_ref, entering_ref, rim_ref, merged_edges, got_ref, first_got, out_ref, scratch, piece_done):
    tokens, modes = fixed[0].shape[0], entering_ref.shape[0]
    rank = lax.axis_index("context")
    _, rate, w = table_parts(fixed[3])
    other_tail, _ = other_edges(first_got, g, edges_ref.shape[0], modes, False)
    entering = enter(
        tokens, span, rank, rate, w, [merged_edges[g, TAIL + i] for i in range(HEAD)],
        unpack(got_ref, 0, modes), other_tail, [entering_ref[m] for m in range(modes)],
    )
    begins = (rank & (span - 1)) == 0
    rim = [jnp.where(begins, other_tail[i], rim_ref[i]) for i in range(TAIL)]
    head = [edges_ref[g, TAIL + i] for i in range(HEAD)]
    emit_group(range(tokens // CHUNK), *fixed, head, entering, rim, out_ref, *scratch, piece_done)


VM = pl.BlockSpec(memory_space=pltpu.VMEM)
HB = pl.BlockSpec(memory_space=pltpu.HBM)


def call(kernel, name, operands, outs, scratch, mib, flops, in_specs=None, out_specs=None, aliases=None):
    in_specs = in_specs or [VM] * len(operands)
    operands = [
        pltpu.with_memory_space_constraint(x, pltpu.VMEM if spec is VM else pltpu.HBM) for x, spec in zip(operands, in_specs)
    ]
    return pl.pallas_call(
        kernel,
        in_specs=in_specs,
        out_specs=[VM] * len(outs) if out_specs is None else out_specs,
        out_shape=outs,
        scratch_shapes=scratch,
        input_output_aliases=aliases or {},
        compiler_params=pltpu.CompilerParams(vmem_limit_bytes=mib * 2**20),
        cost_estimate=pl.CostEstimate(flops=flops, bytes_accessed=2**20, transcendentals=0),
        name=name,
    )(*operands)


def body(streams, short_filter, decay_rate, residue, bias):
    tokens, _, channels = streams.shape
    modes = decay_rate.shape[1]
    groups = channels // GROUP
    chunks, pieces = tokens // CHUNK, tokens // PIECE
    size = lax.axis_size("context")
    vector = (SUB, LANES)
    turned = pltpu.VMEM(((SUB + 1) * STRIDE, LANES), F32)
    dma = pltpu.SemaphoreType.DMA
    work = tokens * channels

    def vectors(*shape):
        return pltpu.VMEM(shape + vector, F32)

    def message_type(count):
        return pltpu.VMEM((count // 2, 2 * SUB, LANES), BF16)

    def swap(message, span):
        return lax.ppermute(message, "context", [(i, i ^ span) for i in range(size)])

    edge = TAIL + HEAD
    state_types = [vectors(tokens), vectors(chunks, modes), vectors(modes), vectors(2 * modes + 10)]
    input_types = [
        pltpu.VMEM((modes, channels), F32), pltpu.VMEM((3, 3, channels), F32), pltpu.VMEM((modes, channels), F32),
        vectors(groups), pltpu.VMEM((3, tokens, channels), BF16),
    ]
    by_stream = streams.transpose(1, 0, 2)
    *first, first_message, own_edges, rates, taps, residues, biases, natural = call(
        first_states_kernel, "states",
        [by_stream, short_filter, decay_rate.T, residue.T, bias.reshape((groups,) + vector)],
        state_types + [message_type(modes + groups * edge), vectors(groups, edge)] + input_types,
        [turned] * 4 + [dma((4,)), dma((groups + 2,))], 4, 24 * work, in_specs=[HB] * 5,
    )
    made, message = [first], [first_message]
    def state_slot(g, after=()):
        nonlocal own_edges, natural
        held = made[-1] + ([own_edges, natural] if g == 1 else [])
        outs = state_types + [message_type(modes)] if g < groups else []
        ins = [rates, taps, residues, biases] + ([by_stream] if g == 1 else [natural])

        def kernel(*refs, g=g, count=len(held), fresh=len(outs)):
            ins, refs = refs[:5], refs[5 + count + len(after) :]
            before, outs, scratch = refs[:count], refs[count : count + fresh], refs[count + fresh :]
            if g == 1:
                later_states_kernel(g, ins[:4] + (before[5],), before[:4], before[4], ins[4], scratch[4], outs, scratch[:4])
            else:
                later_states_kernel(g, ins, before, None, None, None, outs, scratch)

        results = call(
            kernel, "states", ins + held + list(after),
            state_types + ([vectors(groups, edge), pltpu.VMEM((3, tokens, channels), BF16)] if g == 1 else []) + outs,
            [turned] * 4 + ([dma((groups,))] if g == 1 else []), 4, 24 * work,
            in_specs=[VM] * 4 + [HB if g == 1 else VM] + [VM] * (len(held) + len(after)), aliases={5 + i: i for i in range(len(held))},
        )
        made[-1] = list(results[:4])
        if g == 1:
            own_edges, natural = results[4:6]
        if outs:
            made.append(list(results[len(held) : len(held) + 4]))
            message.append(results[-1])
    for g in range(1, groups):
        state_slot(g)

    def near_all(condition, after, held):
        def kernel(*refs):
            natural, refs = refs[0], refs[1 + len(after) :]
            ins, refs = refs[: 2 * groups], refs[2 * groups + len(held) :]
            outs, scratch = refs[: 2 * groups], refs[2 * groups :]

            @pl.when(condition())
            def _():
                for g in range(groups):
                    near_group(g, natural.at[0], *ins[2 * g : 2 * g + 2], *outs[2 * g : 2 * g + 2], *scratch)

        operands = [natural] + after + sum([[made[g][3], made[g][0]] for g in range(groups)], [])
        outs = call(
            kernel, "near", operands + held, [vectors(tokens)] * (2 * groups), [vectors(CHUNK), turned, turned], 4, 24 * work,
            aliases={len(operands) + i: i for i in range(len(held))},
        )
        return list(outs)

    half = pltpu.VMEM((tokens, GROUP), BF16)
    emit_scratch = [vectors(modes), vectors(4), turned, turned]

    merged, edges = [m[2] for m in made], own_edges
    entering, rim = [None] * groups, [None] * groups
    span = 1
    while True:
        got = [swap(message[g], span) for g in range(groups)]
        if 2 * span >= size:
            break
        last, first = 4 * span >= size, entering[0] is None
        if first:
            near = near_all(lambda: is_first(size // 2), [], [])
        old_edges = edges
        for g in range(groups):
            if first and g == 1:
                state_slot(groups, [rim[0]])
                near = near_all(lambda: is_early(size // 2) & jnp.logical_not(is_first(size // 2)), [rim[0]], near)
            part = range(EARLY[g - 1] if g else 0, EARLY[g]) if last and g < len(EARLY) else range(0)
            early, held = [], []
            if part:
                early = [*near[:2], made[0][1], made[0][3], own_edges] + ([entering[0], rim[0]] if g else [])
                held = [begun, begun_state] if g else []
            operands = [merged[g], old_edges, got[g], got[0], made[g][3]] + ([] if first else [entering[g], rim[g]])
            count = modes + (groups * (TAIL if last else edge) if g == 0 else 0)
            outs = [message_type(count), vectors(modes), vectors(TAIL)]
            outs += [] if last else [vectors(modes)]
            outs += [vectors(groups, edge)] if g == 0 else []
            outs += [half, vectors(modes)] if part else []

            def kernel(*refs, g=g, span=span, last=last, first=first, part=part, counts=(len(early), len(held), len(outs))):
                refs = list(refs)
                ins = [refs.pop(0) for _ in range(5)] + ([None, None] if first else [refs.pop(0) for _ in range(2)])
                more, _, produced = ([refs.pop(0) for _ in range(n)] for n in counts)
                state_out = None if last else produced[3]
                edges_out = produced[3 if last else 4] if g == 0 else None
                merge_group(span, tokens, g, last, *ins, *produced[:3], state_out, edges_out)

                def emit(which):
                    known = more[5:7] if g else produced[1:3]
                    emit_known(which, 0, more[:4], more[4], *known, produced[-2], [produced[-1]] + refs, lambda n: None)

                if part:
                    pl.when(is_first(2 * span))(lambda: emit(part))
                if part and g == 1:
                    pl.when(is_early(2 * span) & jnp.logical_not(is_first(2 * span)))(lambda: emit(range(part.stop)))

            results = list(
                call(
                    kernel, "merge", operands + early + held, outs, emit_scratch if part else [], 4, 2**20,
                    aliases={len(operands) + len(early) + i: len(outs) - 2 + i for i in range(len(held))},
                )
            )
            message[g], entering[g], rim[g] = results[:3]
            if not last:
                merged[g] = results[3]
            if g == 0:
                edges = results[3 if last else 4]
            if part:
                begun, begun_state = results[-2:]
        span *= 2

    out_type = pltpu.HBM((tokens, channels), BF16)
    pair = [[entering[g], rim[g]] for g in range(groups)]
    begin = EARLY[-1]

    def kernel(own_edges, begun, begun_state, *refs):
        ins, refs = [refs[i * 6 : i * 6 + 6] for i in range(groups)], refs[groups * 6 :]
        out_hbm, out_refs, state, scratch = refs[0], refs[1 : 1 + groups], refs[1 + groups], refs[2 + groups : 6 + groups]

        @pl.when(is_early(span))
        def _():
            for m in range(modes):
                state[m] = begun_state[m]
            for g in range(groups - 1):
                which = range(0 if g else begin, chunks)
                emit_known(which, g, ins[g][:4], own_edges, *ins[g][4:], out_refs[g], [state, *scratch], lambda n: None)

            def emit(out, piece_done):
                emit_known(range(chunks), groups - 1, ins[-1][:4], own_edges, *ins[-1][4:], out, [state, *scratch], piece_done)

            done = [(pl.ds(0, begin * CHUNK), 0, begun), (pl.ds(begin * CHUNK, tokens - begin * CHUNK), 0, out_refs[0])]
            done += [(pl.ds(0, tokens), g, out_refs[g]) for g in range(1, groups - 1)]
            emit_out(emit, done, out_hbm, out_refs[-1], *refs[6 + groups :])

    def fixed_of():
        return [[*near[2 * g : 2 * g + 2], made[g][1], made[g][3]] for g in range(groups)]

    out = call(
        kernel, "early", [own_edges, begun, begun_state] + sum([f + p for f, p in zip(fixed_of(), pair)], []),
        [out_type], [half] * groups + [vectors(modes)] + emit_scratch + [dma((groups,)), dma((pieces,))],
        4, 40 * work, out_specs=[HB],
    )[0]
    near = near_all(lambda: jnp.logical_not(is_early(span)), [entering[-1]], [])
    fixed = fixed_of()
    halves = []
    for g in range(groups):
        final = g + 1 == groups
        operands = fixed[g] + [own_edges] + pair[g] + [edges, got[g], got[0]] + (halves + [out] if final else [])

        def kernel(*refs, g=g, final=final):
            ins, refs = refs[:10], refs[10:]
            if final:
                done, (_, out_hbm, out_ref, *scratch) = refs[: groups - 1], refs[groups - 1 :]
            else:
                out_ref, *scratch = refs

            @pl.when(jnp.logical_not(is_early(span)))
            def _():
                def emit(out, piece_done):
                    emit_merged(span, g, ins[:4], *ins[4:], out, scratch[:5], piece_done)

                if final:
                    ready = [(pl.ds(0, tokens), i, x) for i, x in enumerate(done)]
                    emit_out(emit, ready, out_hbm, out_ref, *scratch[5:])
                else:
                    emit(out_ref, lambda n: None)

        if not final:
            halves += call(kernel, "late", operands, [half], [vectors(modes)] + emit_scratch, 4, 20 * work)
    return call(
        kernel, "late", operands, [out_type],
        [half, vectors(modes)] + emit_scratch + [dma((groups,)), dma((pieces,))], 4, 20 * work,
        in_specs=[VM] * (len(operands) - 1) + [HB], out_specs=[HB], aliases={len(operands) - 1: 0},
    )[0]


def solution(mesh):
    in_specs = (
        P(("dp", "context"), None, "tensor"),
        P(None, None, "tensor"),
        P("tensor", None),
        P("tensor", None),
        P("tensor"),
    )
    out_specs = P(("dp", "context"), "tensor")
    return jax.shard_map(body, mesh=mesh, in_specs=in_specs, out_specs=out_specs, check_vma=False)
```

```python
import jax
import jax.numpy as jnp
from jax import lax
from jax.experimental import pallas as pl
from jax.experimental.pallas import tpu as pltpu
from jax.sharding import PartitionSpec as P

F32 = jnp.float32
BF16 = jnp.bfloat16
LANES = 128
SUB = 8
GROUP = LANES * SUB
CHUNK = 16
PIECE = 64
STRIDE = CHUNK + 8
EARLY = 2
HEAD = 4
TAIL = 6


def total(values):
    values = list(values)
    while len(values) > 1:
        pairs = [values[i] + values[i + 1] for i in range(0, len(values) - 1, 2)]
        values = pairs + ([values[-1]] if len(values) % 2 else [])
    return values[0]


def columns(g):
    return pl.ds(g * GROUP, GROUP)


def turn_in(source, turned, start, g):
    for j in range(SUB):
        turned[pl.ds(j * STRIDE, CHUNK), :] = source[pl.ds(start, CHUNK), pl.ds(g * GROUP + j * LANES, LANES)].astype(F32)


def turn_rows(source, turned, rows, g):
    for j in range(SUB):
        turned[pl.ds(j * STRIDE, rows), :] = source[:, pl.ds(g * GROUP + j * LANES, LANES)]


def row(turned, i):
    return turned[pl.ds(i, SUB, stride=STRIDE), :]


def chunk_rows(c):
    return pl.multiple_of(c * CHUNK, CHUNK)


def pack(message_ref, rows):
    for i in range(message_ref.shape[0]):
        message_ref[i] = jnp.concatenate(rows[2 * i : 2 * i + 2], axis=0).astype(BF16)


def unpack(message_ref, first, count):
    rows = []
    for i in range(first // 2, (first + count) // 2):
        pair = message_ref[i].astype(F32)
        rows += [pair[:SUB], pair[SUB:]]
    return rows


def first_products(w, head, tail):
    features = []
    for s, rows in ((1, (tail[1], tail[4], head[0], head[2])), (2, (tail[2], tail[5], head[1], head[3]))):
        features.append([w[3 * s] * rows[2 + t] + w[3 * s + 1] * rows[1 + t] + w[3 * s + 2] * rows[t] for t in range(2)])
    return [(features[0][t] * features[1][t]).astype(BF16).astype(F32) for t in range(2)]


def first_terms(rate, products, steps):
    return jnp.exp((1.0 - steps) * rate) * products[0] + jnp.exp((2.0 - steps) * rate) * products[1]


def enter(tokens, span, rank, rate, w, head, other, other_tail, entering):
    right = (rank & span) != 0
    ahead = rank & (span - 1)
    steps = (tokens * ahead).astype(F32)
    products = first_products(w, head, other_tail)
    result = []
    for m, r in enumerate(rate):
        missing = jnp.where(ahead > 0, first_terms(r, products, jnp.maximum(steps, 2.0)), 0.0)
        result.append(jnp.where(right, entering[m] + jnp.exp(-steps * r) * other[m] + missing, entering[m]))
    return result


def table_parts(tables_ref):
    modes = (tables_ref.shape[0] - 10) // 2
    rate = [tables_ref[m] for m in range(modes)]
    return modes, rate, [tables_ref[modes + i] for i in range(9)]


def gain_row(modes, m):
    return modes + 9 + m


def state_kernel(
    g, rate_nat, taps_nat, residue_nat, bias_nat, natural,
    kv_ref, states_ref, own_ref, tables_ref, ka, kb, va, vb, wait_piece, wait_rest,
):
    q_nat, k_nat, v_nat = (natural.at[i] for i in range(3))
    tokens, modes = natural.shape[1], rate_nat.shape[0]
    chunks = tokens // CHUNK
    rank = lax.axis_index("context")
    zero = jnp.zeros((SUB, LANES), F32)
    turn_rows(rate_nat, ka, modes, g)
    for stream in range(3):
        turn_rows(taps_nat.at[stream], (kb, va, vb)[stream], 3, g)
    p = []
    for m in range(modes):
        rate = row(ka, m)
        tables_ref[m] = rate
        p.append(jnp.exp(-rate))
    w = []
    for i in range(9):
        w.append(row((kb, va, vb)[i // 3], i % 3))
        tables_ref[modes + i] = w[i]
    wk, wv = w[3:6], w[6:9]
    wait_piece(0)
    turn_in(k_nat, ka, 0, g)
    turn_in(v_nat, va, 0, g)
    def one_chunk(c, ks, vs, acc, last):
        k1, k2, v1, v2 = last
        for m in range(modes):
            states_ref[c, m] = acc[m]
        for i in range(CHUNK):
            k, v = row(ks, i), row(vs, i)
            key = wk[0] * k + wk[1] * k1 + wk[2] * k2
            value = wv[0] * v + wv[1] * v1 + wv[2] * v2
            k1, k2, v1, v2 = k, k1, v, v1
            product = (key * value).astype(BF16).astype(F32)
            if i < 2:
                product = jnp.where((c > 0) | (rank == 0), product, 0.0)
            kv_ref[c * CHUNK + i] = product
            acc = [a * b + product for a, b in zip(acc, p)]
        return acc, (k1, k2, v1, v2)

    def two_chunks(it, carry):
        acc, last = carry
        c = 2 * it
        pl.when(it == PIECE // (2 * CHUNK) - 1)(lambda: wait_piece(1))
        turn_in(k_nat, kb, chunk_rows(c + 1), g)
        turn_in(v_nat, vb, chunk_rows(c + 1), g)
        acc, last = one_chunk(c, ka, va, acc, last)
        ahead = chunk_rows(jnp.minimum(c + 2, chunks - 1))
        turn_in(k_nat, ka, ahead, g)
        turn_in(v_nat, va, ahead, g)
        return one_chunk(c + 1, kb, vb, acc, last)

    acc, _ = lax.fori_loop(0, chunks // 2, two_chunks, ([zero] * modes, (zero,) * 4))
    for m in range(modes):
        own_ref[m] = acc[m]
    wait_rest()
    turn_rows(residue_nat, ka, modes, g)
    for m in range(modes):
        tables_ref[gain_row(modes, m)] = row(ka, m)
    tables_ref[gain_row(modes, modes)] = bias_nat[g]


def edge_rows(natural, edges_ref, turned, g):
    tokens = natural.shape[1]
    for stream in range(3):
        turn_in(natural.at[stream], turned, tokens - CHUNK, g)
        for i in range(2):
            edges_ref[g, 3 * i + stream] = row(turned, CHUNK - 2 + i)
        if stream:
            turn_in(natural.at[stream], turned, 0, g)
            for i in range(2):
                edges_ref[g, TAIL + 2 * i + stream - 1] = row(turned, i)


def tails_and_heads(edges, heads):
    rows = sum([e[:TAIL] for e in edges], [])
    return rows + sum([e[TAIL:] for e in edges], []) if heads else rows


def other_edges(first_got, g, groups, modes, heads):
    tail = unpack(first_got, modes + TAIL * g, TAIL)
    return tail, unpack(first_got, modes + TAIL * groups + HEAD * g, HEAD) if heads else None


def first_states_kernel(
    streams, taps_hbm, rate_hbm, residue_hbm, bias_hbm,
    kv_ref, states_ref, own_ref, tables_ref, message_ref, edges_ref, rate_nat, taps_nat, residue_nat, bias_nat, natural,
    ka, kb, va, vb, table_sems, stream_sems,
):
    _, tokens, channels = natural.shape
    groups = channels // GROUP
    keys_values = pl.ds(1, 2)
    pieces = [
        fetch(streams, natural, stream_sems.at[0], keys_values, pl.ds(0, PIECE), columns(0)),
        fetch(streams, natural, stream_sems.at[1], keys_values, pl.ds(PIECE, tokens - PIECE), columns(0)),
    ]
    rest = other_inputs(streams, natural, stream_sems, 2)
    tables = [
        pltpu.make_async_copy(src, dst, table_sems.at[i])
        for i, (src, dst) in enumerate(
            [(rate_hbm, rate_nat), (taps_hbm, taps_nat), (residue_hbm, residue_nat), (bias_hbm, bias_nat)]
        )
    ]
    for copy in tables[:2] + pieces + tables[2:]:
        copy.start()

    def wait_rest():
        for copy in tables[2:] + rest:
            copy.wait()

    @pl.when(jnp.logical_not(is_last()))
    def _():
        for copy in rest:
            copy.start()
        for copy in tables[:2]:
            copy.wait()
        state_kernel(
            0, rate_nat, taps_nat, residue_nat, bias_nat, natural,
            kv_ref, states_ref, own_ref, tables_ref, ka, kb, va, vb, lambda n: pieces[n].wait(), wait_rest,
        )
        for g in range(groups):
            edge_rows(natural, edges_ref, ka, g)
        state = [own_ref[m] for m in range(own_ref.shape[0])]
        edges = [[edges_ref[g, i] for i in range(TAIL + HEAD)] for g in range(groups)]
        pack(message_ref, state + tails_and_heads(edges, True))

    @pl.when(is_last())
    def _():
        for copy in tables + pieces:
            copy.wait()
        message_ref[...] = jnp.zeros(message_ref.shape, BF16)


def fetch(streams, natural, sem, *where):
    return pltpu.make_async_copy(streams.at[where], natural.at[where], sem)


def other_inputs(streams, natural, sems, first):
    groups = natural.shape[2] // GROUP
    copies = [fetch(streams, natural, sems.at[first], pl.ds(0, 1), slice(None), columns(0))]
    for g in range(1, groups):
        copies.append(fetch(streams, natural, sems.at[first + g], slice(None), slice(None), columns(g)))
    return copies


def is_last():
    return lax.axis_index("context") == lax.axis_size("context") - 1


def later_states_kernel(g, inputs, before, own_edges, streams, sems, outs, scratch):
    def states(group, refs):
        state_kernel(group, *inputs, *refs, *scratch, lambda n: None, lambda: None)

    if outs:

        @pl.when(jnp.logical_not(is_last()))
        def _():
            states(g, outs[:4])
            pack(outs[4], [outs[2][m] for m in range(outs[2].shape[0])])

    @pl.when(is_last())
    def _():
        rest = other_inputs(streams, inputs[-1], sems, 0) if g == 1 else []
        for copy in rest:
            copy.start()
        states(g - 1, before)
        for copy in rest:
            copy.wait()
        if g == 1:
            for group in range(own_edges.shape[0]):
                edge_rows(inputs[-1], own_edges, scratch[0], group)
        if outs:
            outs[4][...] = jnp.zeros(outs[4].shape, BF16)


def near_group(g, q_nat, tables_ref, kv_ref, near_ref, query_ref, taps, qa, qb):
    tokens = kv_ref.shape[0]
    chunks = tokens // CHUNK
    zero = jnp.zeros((SUB, LANES), F32)
    modes, rate, w = table_parts(tables_ref)
    p = [jnp.exp(-r) for r in rate]
    gain = [tables_ref[gain_row(modes, m)] for m in range(modes)]
    taps[0] = total(gain) + tables_ref[gain_row(modes, modes)]
    for i in range(1, CHUNK):
        gain = [a * b for a, b in zip(gain, p)]
        taps[i] = total(gain)
    h = [taps[i] for i in range(CHUNK)]
    turn_in(q_nat, qa, 0, g)

    def one_chunk(c, qs, last):
        q1, q2 = last
        window = []
        for i in range(CHUNK):
            t = c * CHUNK + i
            q = row(qs, i)
            query_ref[t] = w[0] * q + w[1] * q1 + w[2] * q2
            q1, q2 = q, q1
            window.append(kv_ref[t])
            near_ref[t] = total(h[n] * window[i - n] for n in range(i + 1))
        return q1, q2

    def two_chunks(it, last):
        c = 2 * it
        turn_in(q_nat, qb, chunk_rows(c + 1), g)
        last = one_chunk(c, qa, last)
        turn_in(q_nat, qa, chunk_rows(jnp.minimum(c + 2, chunks - 1)), g)
        return one_chunk(c + 1, qb, last)

    lax.fori_loop(0, chunks // 2, two_chunks, (zero, zero))


def merge_group(
    span, tokens, g, last, own_ref, edges_ref, got_ref, first_got, tables_ref, entering_ref, rim_ref,
    message_ref, entering_out, rim_out, next_ref, edges_out,
):
    modes, rate, w = table_parts(tables_ref)
    groups = edges_ref.shape[0]
    rank = lax.axis_index("context")
    right = (rank & span) != 0
    ahead = rank & (span - 1)
    length = 1.0 * tokens * span
    zero = jnp.zeros((SUB, LANES), F32)

    def pick(a, b):
        return [jnp.where(right, x, y) for x, y in zip(a, b)]

    def edge(group):
        rows = [edges_ref[group, i] for i in range(TAIL + HEAD)]
        return rows[:TAIL], rows[TAIL:]

    state, other = [own_ref[m] for m in range(modes)], unpack(got_ref, 0, modes)
    tail, head = edge(g)
    other_tail, other_head = other_edges(first_got, g, groups, modes, True)
    products = first_products(w, pick(head, other_head), pick(other_tail, tail))
    left_state, right_state = pick(other, state), pick(state, other)
    rows = [
        right_state[m] + jnp.exp(-length * rate[m]) * left_state[m] + first_terms(rate[m], products, length)
        for m in range(modes)
    ]
    if not last:
        for m in range(modes):
            next_ref[m] = rows[m]
    if g == 0:
        edges = []
        for group in range(groups):
            mine, theirs = edge(group), other_edges(first_got, group, groups, modes, True)
            edges.append(pick(mine[0], theirs[0]) + pick(theirs[1], mine[1]))
            for i, value in enumerate(edges[-1]):
                edges_out[group, i] = value
        rows = rows + tails_and_heads(edges, not last)
    pack(message_ref, rows)
    entering = [zero if entering_ref is None else entering_ref[m] for m in range(modes)]
    entering = enter(tokens, span, rank, rate, w, head, other, other_tail, entering)
    for m in range(modes):
        entering_out[m] = entering[m]
    for i in range(TAIL):
        old = zero if rim_ref is None else rim_ref[i]
        rim_out[i] = jnp.where(right & (ahead == 0), other_tail[i], old)


def emit_group(
    which, near_ref, query_ref, states_ref, tables_ref, head, entering, rim, out_ref, state, power, rim_ref, ta, tb, piece_done
):
    rank = lax.axis_index("context")
    modes, rate, w = table_parts(tables_ref)
    p = [jnp.exp(-r) for r in rate]
    for m in range(modes):
        power[m] = jnp.exp(-CHUNK * rate[m])
    if which.start == 0:
        for m in range(modes):
            state[m] = entering[m]
        products = first_products(w, head, rim)
        for i in range(2):
            rim_ref[i] = jnp.where(rank == 0, 0.0, products[i])
        rim_ref[2] = w[1] * rim[3] + w[2] * rim[0]
        rim_ref[3] = w[2] * rim[3]

    def one_chunk(c, turned, first):
        x = [tables_ref[gain_row(modes, m)] * (states_ref[c, m] + state[m]) for m in range(modes)]
        for i in range(CHUNK):
            t = c * CHUNK + i
            x = [a * b for a, b in zip(x, p)]
            near, query = near_ref[t], query_ref[t]
            if first and i < 2:
                x = [a + tables_ref[gain_row(modes, m)] * rim_ref[i] for m, a in enumerate(x)]
                near = near + tables_ref[gain_row(modes, modes)] * rim_ref[i]
                query = query + rim_ref[2 + i]
            mixed = (near + total(x)).astype(BF16).astype(F32)
            turned[pl.ds(i, SUB, stride=STRIDE), :] = query * mixed
        for m in range(modes):
            if first:
                held = (state[m] * p[m] + rim_ref[0]) * p[m] + rim_ref[1]
                state[m] = held * jnp.exp(-(CHUNK - 2) * tables_ref[m])
            else:
                state[m] = state[m] * power[m]

    def turn_out(turned, c):
        for j in range(SUB):
            out_ref[pl.ds(chunk_rows(c), CHUNK), pl.ds(j * LANES, LANES)] = turned[pl.ds(j * STRIDE, CHUNK), :].astype(BF16)

    begin = which.start
    one_chunk(begin, ta, begin == 0)
    one_chunk(begin + 1, tb, False)
    turn_out(ta, begin)

    def two_chunks(it, none):
        c = 2 * it
        one_chunk(c, ta, False)
        turn_out(tb, c - 1)
        one_chunk(c + 1, tb, False)
        turn_out(ta, c)
        pl.when((it & 1) == 0)(lambda: piece_done(it * 2 * CHUNK // PIECE - 1))
        return none

    lax.fori_loop(begin // 2 + 1, which.stop // 2, two_chunks, 0)
    turn_out(tb, which.stop - 1)
    piece_done(which.stop * CHUNK // PIECE - 1)


def emit_out(emit, ready, out_hbm, out_ref, ready_sems, sems):
    tokens, last = out_ref.shape[0], out_hbm.shape[1] // GROUP - 1
    copies = [
        pltpu.make_async_copy(buffer.at[rows], out_hbm.at[rows, columns(g)], ready_sems.at[i])
        for i, (rows, g, buffer) in enumerate(ready)
    ]
    for copy in copies:
        copy.start()

    def send(n):
        rows = pl.ds(pl.multiple_of(n * PIECE, PIECE), PIECE)
        return pltpu.make_async_copy(out_ref.at[rows], out_hbm.at[rows, columns(last)], sems.at[n])

    emit(out_ref, lambda n: send(n).start())
    for copy in copies + [send(n) for n in range(tokens // PIECE)]:
        copy.wait()


def is_early(span):
    return (lax.axis_index("context") & span) == 0


def is_first(span):
    rank = lax.axis_index("context")
    return is_early(span) & ((rank & (span // 2)) == 0)


def emit_known(which, g, fixed, edges_ref, entering_ref, rim_ref, out_ref, scratch, piece_done):
    entering = [entering_ref[m] for m in range(entering_ref.shape[0])]
    rim = [rim_ref[i] for i in range(TAIL)]
    head = [edges_ref[g, TAIL + i] for i in range(HEAD)]
    emit_group(which, *fixed, head, entering, rim, out_ref, *scratch, piece_done)


def emit_merged(span, g, fixed, edges_ref, entering_ref, rim_ref, merged_edges, got_ref, first_got, out_ref, scratch, piece_done):
    tokens, modes = fixed[0].shape[0], entering_ref.shape[0]
    rank = lax.axis_index("context")
    _, rate, w = table_parts(fixed[3])
    other_tail, _ = other_edges(first_got, g, edges_ref.shape[0], modes, False)
    entering = enter(
        tokens, span, rank, rate, w, [merged_edges[g, TAIL + i] for i in range(HEAD)],
        unpack(got_ref, 0, modes), other_tail, [entering_ref[m] for m in range(modes)],
    )
    begins = (rank & (span - 1)) == 0
    rim = [jnp.where(begins, other_tail[i], rim_ref[i]) for i in range(TAIL)]
    head = [edges_ref[g, TAIL + i] for i in range(HEAD)]
    emit_group(range(tokens // CHUNK), *fixed, head, entering, rim, out_ref, *scratch, piece_done)


VM = pl.BlockSpec(memory_space=pltpu.VMEM)
HB = pl.BlockSpec(memory_space=pltpu.HBM)


def call(kernel, name, operands, outs, scratch, mib, flops, in_specs=None, out_specs=None, aliases=None):
    in_specs = in_specs or [VM] * len(operands)
    operands = [
        pltpu.with_memory_space_constraint(x, pltpu.VMEM if spec is VM else pltpu.HBM) for x, spec in zip(operands, in_specs)
    ]
    return pl.pallas_call(
        kernel,
        in_specs=in_specs,
        out_specs=[VM] * len(outs) if out_specs is None else out_specs,
        out_shape=outs,
        scratch_shapes=scratch,
        input_output_aliases=aliases or {},
        compiler_params=pltpu.CompilerParams(vmem_limit_bytes=mib * 2**20),
        cost_estimate=pl.CostEstimate(flops=flops, bytes_accessed=2**20, transcendentals=0),
        name=name,
    )(*operands)


def body(streams, short_filter, decay_rate, residue, bias):
    tokens, _, channels = streams.shape
    modes = decay_rate.shape[1]
    groups = channels // GROUP
    chunks, pieces = tokens // CHUNK, tokens // PIECE
    size = lax.axis_size("context")
    vector = (SUB, LANES)
    turned = pltpu.VMEM(((SUB + 1) * STRIDE, LANES), F32)
    dma = pltpu.SemaphoreType.DMA
    work = tokens * channels

    def vectors(*shape):
        return pltpu.VMEM(shape + vector, F32)

    def message_type(count):
        return pltpu.VMEM((count // 2, 2 * SUB, LANES), BF16)

    def swap(message, span):
        return lax.ppermute(message, "context", [(i, i ^ span) for i in range(size)])

    edge = TAIL + HEAD
    state_types = [vectors(tokens), vectors(chunks, modes), vectors(modes), vectors(2 * modes + 10)]
    input_types = [
        pltpu.VMEM((modes, channels), F32), pltpu.VMEM((3, 3, channels), F32), pltpu.VMEM((modes, channels), F32),
        vectors(groups), pltpu.VMEM((3, tokens, channels), BF16),
    ]
    by_stream = streams.transpose(1, 0, 2)
    *first, first_message, own_edges, rates, taps, residues, biases, natural = call(
        first_states_kernel, "states",
        [by_stream, short_filter, decay_rate.T, residue.T, bias.reshape((groups,) + vector)],
        state_types + [message_type(modes + groups * edge), vectors(groups, edge)] + input_types,
        [turned] * 4 + [dma((4,)), dma((groups + 2,))], 4, 24 * work, in_specs=[HB] * 5,
    )
    made, message = [first], [first_message]
    def state_slot(g, after=()):
        nonlocal own_edges, natural
        held = made[-1] + ([own_edges, natural] if g == 1 else [])
        outs = state_types + [message_type(modes)] if g < groups else []
        ins = [rates, taps, residues, biases] + ([by_stream] if g == 1 else [natural])

        def kernel(*refs, g=g, count=len(held), fresh=len(outs)):
            ins, refs = refs[:5], refs[5 + count + len(after) :]
            before, outs, scratch = refs[:count], refs[count : count + fresh], refs[count + fresh :]
            if g == 1:
                later_states_kernel(g, ins[:4] + (before[5],), before[:4], before[4], ins[4], scratch[4], outs, scratch[:4])
            else:
                later_states_kernel(g, ins, before, None, None, None, outs, scratch)

        results = call(
            kernel, "states", ins + held + list(after),
            state_types + ([vectors(groups, edge), pltpu.VMEM((3, tokens, channels), BF16)] if g == 1 else []) + outs,
            [turned] * 4 + ([dma((groups,))] if g == 1 else []), 4, 24 * work,
            in_specs=[VM] * 4 + [HB if g == 1 else VM] + [VM] * (len(held) + len(after)), aliases={5 + i: i for i in range(len(held))},
        )
        made[-1] = list(results[:4])
        if g == 1:
            own_edges, natural = results[4:6]
        if outs:
            made.append(list(results[len(held) : len(held) + 4]))
            message.append(results[-1])
    for g in range(1, groups):
        state_slot(g)

    def near_all(condition, after, held):
        def kernel(*refs):
            natural, refs = refs[0], refs[1 + len(after) :]
            ins, refs = refs[: 2 * groups], refs[2 * groups + len(held) :]
            outs, scratch = refs[: 2 * groups], refs[2 * groups :]

            @pl.when(condition())
            def _():
                for g in range(groups):
                    near_group(g, natural.at[0], *ins[2 * g : 2 * g + 2], *outs[2 * g : 2 * g + 2], *scratch)

        operands = [natural] + after + sum([[made[g][3], made[g][0]] for g in range(groups)], [])
        outs = call(
            kernel, "near", operands + held, [vectors(tokens)] * (2 * groups), [vectors(CHUNK), turned, turned], 4, 24 * work,
            aliases={len(operands) + i: i for i in range(len(held))},
        )
        return list(outs)

    half = pltpu.VMEM((tokens, GROUP), BF16)
    emit_scratch = [vectors(modes), vectors(4), turned, turned]

    merged, edges = [m[2] for m in made], own_edges
    entering, rim = [None] * groups, [None] * groups
    span = 1
    while True:
        got = [swap(message[g], span) for g in range(groups)]
        if 2 * span >= size:
            break
        last, first = 4 * span >= size, entering[0] is None
        if first:
            near = near_all(lambda: is_first(size // 2), [], [])
        old_edges = edges
        for g in range(groups):
            if first and g == 1:
                state_slot(groups, [rim[0]])
                near = near_all(lambda: is_early(size // 2) & jnp.logical_not(is_first(size // 2)), [rim[0]], near)
            early = [*near[:2], made[0][1], made[0][3], own_edges] if last and g == 0 else []
            after = near[:1] if first and g == 1 else []
            operands = after + [merged[g], old_edges, got[g], got[0], made[g][3]] + ([] if first else [entering[g], rim[g]])
            count = modes + (groups * (TAIL if last else edge) if g == 0 else 0)
            outs = [message_type(count), vectors(modes), vectors(TAIL)]
            outs += [] if last else [vectors(modes)]
            outs += [vectors(groups, edge)] if g == 0 else []
            outs += [half, vectors(modes)] if early else []

            def kernel(*refs, g=g, span=span, last=last, first=first, counts=(len(early), len(outs)), skip=len(after)):
                refs = list(refs[skip:])
                ins = [refs.pop(0) for _ in range(5)] + ([None, None] if first else [refs.pop(0) for _ in range(2)])
                more, produced = ([refs.pop(0) for _ in range(n)] for n in counts)
                state_out = None if last else produced[3]
                edges_out = produced[3 if last else 4] if g == 0 else None
                merge_group(span, tokens, g, last, *ins, *produced[:3], state_out, edges_out)
                if more:

                    @pl.when(is_first(2 * span))
                    def _():
                        out_ref, state_ref = produced[-2:]
                        emit_known(
                            range(EARLY), 0, more[:4], more[4], *produced[1:3], out_ref, [state_ref] + refs, lambda n: None
                        )

            results = list(call(kernel, "merge", operands + early, outs, emit_scratch if early else [], 4, 2**20))
            message[g], entering[g], rim[g] = results[:3]
            if not last:
                merged[g] = results[3]
            if g == 0:
                edges = results[3 if last else 4]
            if early:
                begun, begun_state = results[-2:]
        span *= 2

    out_type = pltpu.HBM((tokens, channels), BF16)
    pair = [[entering[g], rim[g]] for g in range(groups)]
    def kernel(own_edges, begun, begun_state, *refs):
        ins, refs = [refs[i * 6 : i * 6 + 6] for i in range(groups)], refs[groups * 6 :]
        out_hbm, out_refs, state, scratch = refs[0], refs[1 : 1 + groups], refs[1 + groups], refs[2 + groups : 6 + groups]

        @pl.when(is_early(span))
        def _():
            @pl.when(is_first(span))
            def _():
                out_refs[0][pl.ds(0, EARLY * CHUNK), :] = begun[pl.ds(0, EARLY * CHUNK), :]
                for m in range(modes):
                    state[m] = begun_state[m]

            @pl.when(jnp.logical_not(is_first(span)))
            def _():
                emit_known(range(EARLY), 0, ins[0][:4], own_edges, *ins[0][4:], out_refs[0], [state, *scratch], lambda n: None)

            for g in range(groups - 1):
                which = range(0 if g else EARLY, chunks)
                emit_known(which, g, ins[g][:4], own_edges, *ins[g][4:], out_refs[g], [state, *scratch], lambda n: None)

            def emit(out, piece_done):
                emit_known(range(chunks), groups - 1, ins[-1][:4], own_edges, *ins[-1][4:], out, [state, *scratch], piece_done)

            done = [(pl.ds(0, tokens), g, out_refs[g]) for g in range(groups - 1)]
            emit_out(emit, done, out_hbm, out_refs[-1], *refs[6 + groups :])

    def fixed_of():
        return [[*near[2 * g : 2 * g + 2], made[g][1], made[g][3]] for g in range(groups)]

    out = call(
        kernel, "early", [own_edges, begun, begun_state] + sum([f + p for f, p in zip(fixed_of(), pair)], []),
        [out_type], [half] * groups + [vectors(modes)] + emit_scratch + [dma((groups,)), dma((pieces,))],
        4, 40 * work, out_specs=[HB],
    )[0]
    near = near_all(lambda: jnp.logical_not(is_early(span)), [entering[-1]], [])
    fixed = fixed_of()
    halves = []
    for g in range(groups):
        final = g + 1 == groups
        operands = fixed[g] + [own_edges] + pair[g] + [edges, got[g], got[0]] + (halves + [out] if final else [])

        def kernel(*refs, g=g, final=final):
            ins, refs = refs[:10], refs[10:]
            if final:
                done, (_, out_hbm, out_ref, *scratch) = refs[: groups - 1], refs[groups - 1 :]
            else:
                out_ref, *scratch = refs

            @pl.when(jnp.logical_not(is_early(span)))
            def _():
                def emit(out, piece_done):
                    emit_merged(span, g, ins[:4], *ins[4:], out, scratch[:5], piece_done)

                if final:
                    ready = [(pl.ds(0, tokens), i, x) for i, x in enumerate(done)]
                    emit_out(emit, ready, out_hbm, out_ref, *scratch[5:])
                else:
                    emit(out_ref, lambda n: None)

        if not final:
            halves += call(kernel, "late", operands, [half], [vectors(modes)] + emit_scratch, 4, 20 * work)
    return call(
        kernel, "late", operands, [out_type],
        [half, vectors(modes)] + emit_scratch + [dma((groups,)), dma((pieces,))], 4, 20 * work,
        in_specs=[VM] * (len(operands) - 1) + [HB], out_specs=[HB], aliases={len(operands) - 1: 0},
    )[0]


def solution(mesh):
    in_specs = (
        P(("dp", "context"), None, "tensor"),
        P(None, None, "tensor"),
        P("tensor", None),
        P("tensor", None),
        P("tensor"),
    )
    out_specs = P(("dp", "context"), "tensor")
    return jax.shard_map(body, mesh=mesh, in_specs=in_specs, out_specs=out_specs, check_vma=False)
```

```python
import jax
import jax.numpy as jnp
from jax import lax
from jax.experimental import pallas as pl
from jax.experimental.pallas import tpu as pltpu
from jax.sharding import PartitionSpec as P

F32 = jnp.float32
BF16 = jnp.bfloat16
LANES = 128
SUB = 8
GROUP = LANES * SUB
CHUNK = 16
PIECE = 64
STRIDE = CHUNK + 8
EARLY = 2
HEAD = 4
TAIL = 6


def rounded(first, second):
    pair = jnp.concatenate([first, second], axis=0).astype(BF16).astype(F32)
    return pair[:SUB], pair[SUB:]


def total(values):
    values = list(values)
    while len(values) > 1:
        pairs = [values[i] + values[i + 1] for i in range(0, len(values) - 1, 2)]
        values = pairs + ([values[-1]] if len(values) % 2 else [])
    return values[0]


def columns(g):
    return pl.ds(g * GROUP, GROUP)


def turn_in(source, turned, start, g):
    for j in range(SUB):
        turned[pl.ds(j * STRIDE, CHUNK), :] = source[pl.ds(start, CHUNK), pl.ds(g * GROUP + j * LANES, LANES)].astype(F32)


def turn_rows(source, turned, rows, g):
    for j in range(SUB):
        turned[pl.ds(j * STRIDE, rows), :] = source[:, pl.ds(g * GROUP + j * LANES, LANES)]


def row(turned, i):
    return turned[pl.ds(i, SUB, stride=STRIDE), :]


def chunk_rows(c):
    return pl.multiple_of(c * CHUNK, CHUNK)


def pack(message_ref, rows):
    for i in range(message_ref.shape[0]):
        message_ref[i] = jnp.concatenate(rows[2 * i : 2 * i + 2], axis=0).astype(BF16)


def unpack(message_ref, first, count):
    rows = []
    for i in range(first // 2, (first + count) // 2):
        pair = message_ref[i].astype(F32)
        rows += [pair[:SUB], pair[SUB:]]
    return rows


def first_products(w, head, tail):
    features = []
    for s, rows in ((1, (tail[1], tail[4], head[0], head[2])), (2, (tail[2], tail[5], head[1], head[3]))):
        features.append([w[3 * s] * rows[2 + t] + w[3 * s + 1] * rows[1 + t] + w[3 * s + 2] * rows[t] for t in range(2)])
    return [(features[0][t] * features[1][t]).astype(BF16).astype(F32) for t in range(2)]


def first_terms(rate, products, steps):
    return jnp.exp((1.0 - steps) * rate) * products[0] + jnp.exp((2.0 - steps) * rate) * products[1]


def enter(tokens, span, rank, rate, w, head, other, other_tail, entering):
    right = (rank & span) != 0
    ahead = rank & (span - 1)
    steps = (tokens * ahead).astype(F32)
    products = first_products(w, head, other_tail)
    result = []
    for m, r in enumerate(rate):
        missing = jnp.where(ahead > 0, first_terms(r, products, jnp.maximum(steps, 2.0)), 0.0)
        result.append(jnp.where(right, entering[m] + jnp.exp(-steps * r) * other[m] + missing, entering[m]))
    return result


def table_parts(tables_ref):
    modes = (tables_ref.shape[0] - 10) // 2
    rate = [tables_ref[m] for m in range(modes)]
    return modes, rate, [tables_ref[modes + i] for i in range(9)]


def gain_row(modes, m):
    return modes + 9 + m


def state_kernel(
    g, rate_nat, taps_nat, residue_nat, bias_nat, natural,
    kv_ref, states_ref, own_ref, tables_ref, ka, kb, va, vb, wait_piece, wait_rest,
):
    q_nat, k_nat, v_nat = (natural.at[i] for i in range(3))
    tokens, modes = natural.shape[1], rate_nat.shape[0]
    chunks = tokens // CHUNK
    rank = lax.axis_index("context")
    zero = jnp.zeros((SUB, LANES), F32)
    turn_rows(rate_nat, ka, modes, g)
    for stream in range(3):
        turn_rows(taps_nat.at[stream], (kb, va, vb)[stream], 3, g)
    p = []
    for m in range(modes):
        rate = row(ka, m)
        tables_ref[m] = rate
        p.append(jnp.exp(-rate))
    w = []
    for i in range(9):
        w.append(row((kb, va, vb)[i // 3], i % 3))
        tables_ref[modes + i] = w[i]
    wk, wv = w[3:6], w[6:9]
    wait_piece(0)
    turn_in(k_nat, ka, 0, g)
    turn_in(v_nat, va, 0, g)
    def one_chunk(c, ks, vs, acc, last):
        k1, k2, v1, v2 = last
        for m in range(modes):
            states_ref[c, m] = acc[m]
        for i in range(0, CHUNK, 2):
            products = []
            for n in (i, i + 1):
                k, v = row(ks, n), row(vs, n)
                key = wk[0] * k + wk[1] * k1 + wk[2] * k2
                value = wv[0] * v + wv[1] * v1 + wv[2] * v2
                k1, k2, v1, v2 = k, k1, v, v1
                products.append(key * value)
            for n, product in enumerate(rounded(*products)):
                if i == 0:
                    product = jnp.where((c > 0) | (rank == 0), product, 0.0)
                kv_ref[c * CHUNK + i + n] = product
                acc = [a * b + product for a, b in zip(acc, p)]
        return acc, (k1, k2, v1, v2)

    def two_chunks(it, carry):
        acc, last = carry
        c = 2 * it
        pl.when(it == PIECE // (2 * CHUNK) - 1)(lambda: wait_piece(1))
        turn_in(k_nat, kb, chunk_rows(c + 1), g)
        turn_in(v_nat, vb, chunk_rows(c + 1), g)
        acc, last = one_chunk(c, ka, va, acc, last)
        ahead = chunk_rows(jnp.minimum(c + 2, chunks - 1))
        turn_in(k_nat, ka, ahead, g)
        turn_in(v_nat, va, ahead, g)
        return one_chunk(c + 1, kb, vb, acc, last)

    acc, _ = lax.fori_loop(0, chunks // 2, two_chunks, ([zero] * modes, (zero,) * 4))
    for m in range(modes):
        own_ref[m] = acc[m]
    wait_rest()
    turn_rows(residue_nat, ka, modes, g)
    for m in range(modes):
        tables_ref[gain_row(modes, m)] = row(ka, m)
    tables_ref[gain_row(modes, modes)] = bias_nat[g]


def edge_rows(natural, edges_ref, turned, g):
    tokens = natural.shape[1]
    for stream in range(3):
        turn_in(natural.at[stream], turned, tokens - CHUNK, g)
        for i in range(2):
            edges_ref[g, 3 * i + stream] = row(turned, CHUNK - 2 + i)
        if stream:
            turn_in(natural.at[stream], turned, 0, g)
            for i in range(2):
                edges_ref[g, TAIL + 2 * i + stream - 1] = row(turned, i)


def tails_and_heads(edges, heads):
    rows = sum([e[:TAIL] for e in edges], [])
    return rows + sum([e[TAIL:] for e in edges], []) if heads else rows


def other_edges(first_got, g, groups, modes, heads):
    tail = unpack(first_got, modes + TAIL * g, TAIL)
    return tail, unpack(first_got, modes + TAIL * groups + HEAD * g, HEAD) if heads else None


def first_states_kernel(
    streams, taps_hbm, rate_hbm, residue_hbm, bias_hbm,
    kv_ref, states_ref, own_ref, tables_ref, message_ref, edges_ref, rate_nat, taps_nat, residue_nat, bias_nat, natural,
    ka, kb, va, vb, table_sems, stream_sems,
):
    _, tokens, channels = natural.shape
    groups = channels // GROUP
    keys_values = pl.ds(1, 2)
    pieces = [
        fetch(streams, natural, stream_sems.at[0], keys_values, pl.ds(0, PIECE), columns(0)),
        fetch(streams, natural, stream_sems.at[1], keys_values, pl.ds(PIECE, tokens - PIECE), columns(0)),
    ]
    rest = other_inputs(streams, natural, stream_sems, 2)
    tables = [
        pltpu.make_async_copy(src, dst, table_sems.at[i])
        for i, (src, dst) in enumerate(
            [(rate_hbm, rate_nat), (taps_hbm, taps_nat), (residue_hbm, residue_nat), (bias_hbm, bias_nat)]
        )
    ]
    for copy in tables[:2] + pieces + tables[2:]:
        copy.start()

    def wait_rest():
        for copy in tables[2:] + rest:
            copy.wait()

    @pl.when(jnp.logical_not(is_last()))
    def _():
        for copy in rest:
            copy.start()
        for copy in tables[:2]:
            copy.wait()
        state_kernel(
            0, rate_nat, taps_nat, residue_nat, bias_nat, natural,
            kv_ref, states_ref, own_ref, tables_ref, ka, kb, va, vb, lambda n: pieces[n].wait(), wait_rest,
        )
        for g in range(groups):
            edge_rows(natural, edges_ref, ka, g)
        state = [own_ref[m] for m in range(own_ref.shape[0])]
        edges = [[edges_ref[g, i] for i in range(TAIL + HEAD)] for g in range(groups)]
        pack(message_ref, state + tails_and_heads(edges, True))

    @pl.when(is_last())
    def _():
        for copy in tables + pieces:
            copy.wait()
        message_ref[...] = jnp.zeros(message_ref.shape, BF16)


def fetch(streams, natural, sem, *where):
    return pltpu.make_async_copy(streams.at[where], natural.at[where], sem)


def other_inputs(streams, natural, sems, first):
    groups = natural.shape[2] // GROUP
    copies = [fetch(streams, natural, sems.at[first], pl.ds(0, 1), slice(None), columns(0))]
    for g in range(1, groups):
        copies.append(fetch(streams, natural, sems.at[first + g], slice(None), slice(None), columns(g)))
    return copies


def is_last():
    return lax.axis_index("context") == lax.axis_size("context") - 1


def later_states_kernel(g, inputs, before, own_edges, streams, sems, outs, scratch):
    def states(group, refs):
        state_kernel(group, *inputs, *refs, *scratch, lambda n: None, lambda: None)

    if outs:

        @pl.when(jnp.logical_not(is_last()))
        def _():
            states(g, outs[:4])
            pack(outs[4], [outs[2][m] for m in range(outs[2].shape[0])])

    @pl.when(is_last())
    def _():
        rest = other_inputs(streams, inputs[-1], sems, 0) if g == 1 else []
        for copy in rest:
            copy.start()
        states(g - 1, before)
        for copy in rest:
            copy.wait()
        if g == 1:
            for group in range(own_edges.shape[0]):
                edge_rows(inputs[-1], own_edges, scratch[0], group)
        if outs:
            outs[4][...] = jnp.zeros(outs[4].shape, BF16)


def near_group(g, q_nat, tables_ref, kv_ref, near_ref, query_ref, taps, qa, qb):
    tokens = kv_ref.shape[0]
    chunks = tokens // CHUNK
    zero = jnp.zeros((SUB, LANES), F32)
    modes, rate, w = table_parts(tables_ref)
    p = [jnp.exp(-r) for r in rate]
    gain = [tables_ref[gain_row(modes, m)] for m in range(modes)]
    taps[0] = total(gain) + tables_ref[gain_row(modes, modes)]
    for i in range(1, CHUNK):
        gain = [a * b for a, b in zip(gain, p)]
        taps[i] = total(gain)
    h = [taps[i] for i in range(CHUNK)]
    turn_in(q_nat, qa, 0, g)

    def one_chunk(c, qs, last):
        q1, q2 = last
        window = []
        for i in range(CHUNK):
            t = c * CHUNK + i
            q = row(qs, i)
            query_ref[t] = w[0] * q + w[1] * q1 + w[2] * q2
            q1, q2 = q, q1
            window.append(kv_ref[t])
            near_ref[t] = total(h[n] * window[i - n] for n in range(i + 1))
        return q1, q2

    def two_chunks(it, last):
        c = 2 * it
        turn_in(q_nat, qb, chunk_rows(c + 1), g)
        last = one_chunk(c, qa, last)
        turn_in(q_nat, qa, chunk_rows(jnp.minimum(c + 2, chunks - 1)), g)
        return one_chunk(c + 1, qb, last)

    lax.fori_loop(0, chunks // 2, two_chunks, (zero, zero))


def merge_group(
    span, tokens, g, last, own_ref, edges_ref, got_ref, first_got, tables_ref, entering_ref, rim_ref,
    message_ref, entering_out, rim_out, next_ref, edges_out,
):
    modes, rate, w = table_parts(tables_ref)
    groups = edges_ref.shape[0]
    rank = lax.axis_index("context")
    right = (rank & span) != 0
    ahead = rank & (span - 1)
    length = 1.0 * tokens * span
    zero = jnp.zeros((SUB, LANES), F32)

    def pick(a, b):
        return [jnp.where(right, x, y) for x, y in zip(a, b)]

    def edge(group):
        rows = [edges_ref[group, i] for i in range(TAIL + HEAD)]
        return rows[:TAIL], rows[TAIL:]

    state, other = [own_ref[m] for m in range(modes)], unpack(got_ref, 0, modes)
    tail, head = edge(g)
    other_tail, other_head = other_edges(first_got, g, groups, modes, True)
    products = first_products(w, pick(head, other_head), pick(other_tail, tail))
    left_state, right_state = pick(other, state), pick(state, other)
    rows = [
        right_state[m] + jnp.exp(-length * rate[m]) * left_state[m] + first_terms(rate[m], products, length)
        for m in range(modes)
    ]
    if not last:
        for m in range(modes):
            next_ref[m] = rows[m]
    if g == 0:
        edges = []
        for group in range(groups):
            mine, theirs = edge(group), other_edges(first_got, group, groups, modes, True)
            edges.append(pick(mine[0], theirs[0]) + pick(theirs[1], mine[1]))
            for i, value in enumerate(edges[-1]):
                edges_out[group, i] = value
        rows = rows + tails_and_heads(edges, not last)
    pack(message_ref, rows)
    entering = [zero if entering_ref is None else entering_ref[m] for m in range(modes)]
    entering = enter(tokens, span, rank, rate, w, head, other, other_tail, entering)
    for m in range(modes):
        entering_out[m] = entering[m]
    for i in range(TAIL):
        old = zero if rim_ref is None else rim_ref[i]
        rim_out[i] = jnp.where(right & (ahead == 0), other_tail[i], old)


def emit_group(
    which, near_ref, query_ref, states_ref, tables_ref, head, entering, rim, out_ref, state, power, rim_ref, ta, tb, piece_done
):
    rank = lax.axis_index("context")
    modes, rate, w = table_parts(tables_ref)
    p = [jnp.exp(-r) for r in rate]
    for m in range(modes):
        power[m] = jnp.exp(-CHUNK * rate[m])
    if which.start == 0:
        for m in range(modes):
            state[m] = entering[m]
        products = first_products(w, head, rim)
        for i in range(2):
            rim_ref[i] = jnp.where(rank == 0, 0.0, products[i])
        rim_ref[2] = w[1] * rim[3] + w[2] * rim[0]
        rim_ref[3] = w[2] * rim[3]

    def one_chunk(c, turned, first):
        x = [tables_ref[gain_row(modes, m)] * (states_ref[c, m] + state[m]) for m in range(modes)]
        for i in range(0, CHUNK, 2):
            queries, mixed = [], []
            for n in (i, i + 1):
                t = c * CHUNK + n
                x = [a * b for a, b in zip(x, p)]
                near, query = near_ref[t], query_ref[t]
                if first and n < 2:
                    x = [a + tables_ref[gain_row(modes, m)] * rim_ref[n] for m, a in enumerate(x)]
                    near = near + tables_ref[gain_row(modes, modes)] * rim_ref[n]
                    query = query + rim_ref[2 + n]
                queries.append(query)
                mixed.append(near + total(x))
            for n, value in enumerate(rounded(*mixed)):
                turned[pl.ds(i + n, SUB, stride=STRIDE), :] = queries[n] * value
        for m in range(modes):
            if first:
                held = (state[m] * p[m] + rim_ref[0]) * p[m] + rim_ref[1]
                state[m] = held * jnp.exp(-(CHUNK - 2) * tables_ref[m])
            else:
                state[m] = state[m] * power[m]

    def turn_out(turned, c):
        for j in range(SUB):
            out_ref[pl.ds(chunk_rows(c), CHUNK), pl.ds(j * LANES, LANES)] = turned[pl.ds(j * STRIDE, CHUNK), :].astype(BF16)

    begin = which.start
    one_chunk(begin, ta, begin == 0)
    one_chunk(begin + 1, tb, False)
    turn_out(ta, begin)

    def two_chunks(it, none):
        c = 2 * it
        one_chunk(c, ta, False)
        turn_out(tb, c - 1)
        one_chunk(c + 1, tb, False)
        turn_out(ta, c)
        pl.when((it & 1) == 0)(lambda: piece_done(it * 2 * CHUNK // PIECE - 1))
        return none

    lax.fori_loop(begin // 2 + 1, which.stop // 2, two_chunks, 0)
    turn_out(tb, which.stop - 1)
    piece_done(which.stop * CHUNK // PIECE - 1)


def emit_out(emit, ready, out_hbm, out_ref, ready_sems, sems):
    tokens, last = out_ref.shape[0], out_hbm.shape[1] // GROUP - 1
    copies = [
        pltpu.make_async_copy(buffer.at[rows], out_hbm.at[rows, columns(g)], ready_sems.at[i])
        for i, (rows, g, buffer) in enumerate(ready)
    ]
    for copy in copies:
        copy.start()

    def send(n):
        rows = pl.ds(pl.multiple_of(n * PIECE, PIECE), PIECE)
        return pltpu.make_async_copy(out_ref.at[rows], out_hbm.at[rows, columns(last)], sems.at[n])

    emit(out_ref, lambda n: send(n).start())
    for copy in copies + [send(n) for n in range(tokens // PIECE)]:
        copy.wait()


def is_early(span):
    return (lax.axis_index("context") & span) == 0


def is_first(span):
    rank = lax.axis_index("context")
    return is_early(span) & ((rank & (span // 2)) == 0)


def emit_known(which, g, fixed, edges_ref, entering_ref, rim_ref, out_ref, scratch, piece_done):
    entering = [entering_ref[m] for m in range(entering_ref.shape[0])]
    rim = [rim_ref[i] for i in range(TAIL)]
    head = [edges_ref[g, TAIL + i] for i in range(HEAD)]
    emit_group(which, *fixed, head, entering, rim, out_ref, *scratch, piece_done)


def emit_merged(span, g, fixed, edges_ref, entering_ref, rim_ref, merged_edges, got_ref, first_got, out_ref, scratch, piece_done):
    tokens, modes = fixed[0].shape[0], entering_ref.shape[0]
    rank = lax.axis_index("context")
    _, rate, w = table_parts(fixed[3])
    other_tail, _ = other_edges(first_got, g, edges_ref.shape[0], modes, False)
    entering = enter(
        tokens, span, rank, rate, w, [merged_edges[g, TAIL + i] for i in range(HEAD)],
        unpack(got_ref, 0, modes), other_tail, [entering_ref[m] for m in range(modes)],
    )
    begins = (rank & (span - 1)) == 0
    rim = [jnp.where(begins, other_tail[i], rim_ref[i]) for i in range(TAIL)]
    head = [edges_ref[g, TAIL + i] for i in range(HEAD)]
    emit_group(range(tokens // CHUNK), *fixed, head, entering, rim, out_ref, *scratch, piece_done)


VM = pl.BlockSpec(memory_space=pltpu.VMEM)
HB = pl.BlockSpec(memory_space=pltpu.HBM)


def call(kernel, name, operands, outs, scratch, mib, flops, in_specs=None, out_specs=None, aliases=None):
    in_specs = in_specs or [VM] * len(operands)
    operands = [
        pltpu.with_memory_space_constraint(x, pltpu.VMEM if spec is VM else pltpu.HBM) for x, spec in zip(operands, in_specs)
    ]
    return pl.pallas_call(
        kernel,
        in_specs=in_specs,
        out_specs=[VM] * len(outs) if out_specs is None else out_specs,
        out_shape=outs,
        scratch_shapes=scratch,
        input_output_aliases=aliases or {},
        compiler_params=pltpu.CompilerParams(vmem_limit_bytes=mib * 2**20),
        cost_estimate=pl.CostEstimate(flops=flops, bytes_accessed=2**20, transcendentals=0),
        name=name,
    )(*operands)


def body(streams, short_filter, decay_rate, residue, bias):
    tokens, _, channels = streams.shape
    modes = decay_rate.shape[1]
    groups = channels // GROUP
    chunks, pieces = tokens // CHUNK, tokens // PIECE
    size = lax.axis_size("context")
    vector = (SUB, LANES)
    turned = pltpu.VMEM(((SUB + 1) * STRIDE, LANES), F32)
    dma = pltpu.SemaphoreType.DMA
    work = tokens * channels

    def vectors(*shape):
        return pltpu.VMEM(shape + vector, F32)

    def message_type(count):
        return pltpu.VMEM((count // 2, 2 * SUB, LANES), BF16)

    def swap(message, span):
        return lax.ppermute(message, "context", [(i, i ^ span) for i in range(size)])

    edge = TAIL + HEAD
    state_types = [vectors(tokens), vectors(chunks, modes), vectors(modes), vectors(2 * modes + 10)]
    input_types = [
        pltpu.VMEM((modes, channels), F32), pltpu.VMEM((3, 3, channels), F32), pltpu.VMEM((modes, channels), F32),
        vectors(groups), pltpu.VMEM((3, tokens, channels), BF16),
    ]
    by_stream = streams.transpose(1, 0, 2)
    *first, first_message, own_edges, rates, taps, residues, biases, natural = call(
        first_states_kernel, "states",
        [by_stream, short_filter, decay_rate.T, residue.T, bias.reshape((groups,) + vector)],
        state_types + [message_type(modes + groups * edge), vectors(groups, edge)] + input_types,
        [turned] * 4 + [dma((4,)), dma((groups + 2,))], 4, 24 * work, in_specs=[HB] * 5,
    )
    made, message = [first], [first_message]
    def state_slot(g, after=()):
        nonlocal own_edges, natural
        held = made[-1] + ([own_edges, natural] if g == 1 else [])
        outs = state_types + [message_type(modes)] if g < groups else []
        ins = [rates, taps, residues, biases] + ([by_stream] if g == 1 else [natural])

        def kernel(*refs, g=g, count=len(held), fresh=len(outs)):
            ins, refs = refs[:5], refs[5 + count + len(after) :]
            before, outs, scratch = refs[:count], refs[count : count + fresh], refs[count + fresh :]
            if g == 1:
                later_states_kernel(g, ins[:4] + (before[5],), before[:4], before[4], ins[4], scratch[4], outs, scratch[:4])
            else:
                later_states_kernel(g, ins, before, None, None, None, outs, scratch)

        results = call(
            kernel, "states", ins + held + list(after),
            state_types + ([vectors(groups, edge), pltpu.VMEM((3, tokens, channels), BF16)] if g == 1 else []) + outs,
            [turned] * 4 + ([dma((groups,))] if g == 1 else []), 4, 24 * work,
            in_specs=[VM] * 4 + [HB if g == 1 else VM] + [VM] * (len(held) + len(after)), aliases={5 + i: i for i in range(len(held))},
        )
        made[-1] = list(results[:4])
        if g == 1:
            own_edges, natural = results[4:6]
        if outs:
            made.append(list(results[len(held) : len(held) + 4]))
            message.append(results[-1])
    for g in range(1, groups):
        state_slot(g)

    def near_all(condition, after, held):
        def kernel(*refs):
            natural, refs = refs[0], refs[1 + len(after) :]
            ins, refs = refs[: 2 * groups], refs[2 * groups + len(held) :]
            outs, scratch = refs[: 2 * groups], refs[2 * groups :]

            @pl.when(condition())
            def _():
                for g in range(groups):
                    near_group(g, natural.at[0], *ins[2 * g : 2 * g + 2], *outs[2 * g : 2 * g + 2], *scratch)

        operands = [natural] + after + sum([[made[g][3], made[g][0]] for g in range(groups)], [])
        outs = call(
            kernel, "near", operands + held, [vectors(tokens)] * (2 * groups), [vectors(CHUNK), turned, turned], 4, 24 * work,
            aliases={len(operands) + i: i for i in range(len(held))},
        )
        return list(outs)

    half = pltpu.VMEM((tokens, GROUP), BF16)
    emit_scratch = [vectors(modes), vectors(4), turned, turned]

    merged, edges = [m[2] for m in made], own_edges
    entering, rim = [None] * groups, [None] * groups
    span = 1
    while True:
        got = [swap(message[g], span) for g in range(groups)]
        if 2 * span >= size:
            break
        last, first = 4 * span >= size, entering[0] is None
        if first:
            near = near_all(lambda: is_first(size // 2), [], [])
        old_edges = edges
        for g in range(groups):
            if first and g == 1:
                state_slot(groups, [rim[0]])
                near = near_all(lambda: is_early(size // 2) & jnp.logical_not(is_first(size // 2)), [rim[0]], near)
            early = [*near[:2], made[0][1], made[0][3], own_edges] if last and g == 0 else []
            after = near[:1] if first and g == 1 else []
            operands = after + [merged[g], old_edges, got[g], got[0], made[g][3]] + ([] if first else [entering[g], rim[g]])
            count = modes + (groups * (TAIL if last else edge) if g == 0 else 0)
            outs = [message_type(count), vectors(modes), vectors(TAIL)]
            outs += [] if last else [vectors(modes)]
            outs += [vectors(groups, edge)] if g == 0 else []
            outs += [half, vectors(modes)] if early else []

            def kernel(*refs, g=g, span=span, last=last, first=first, counts=(len(early), len(outs)), skip=len(after)):
                refs = list(refs[skip:])
                ins = [refs.pop(0) for _ in range(5)] + ([None, None] if first else [refs.pop(0) for _ in range(2)])
                more, produced = ([refs.pop(0) for _ in range(n)] for n in counts)
                state_out = None if last else produced[3]
                edges_out = produced[3 if last else 4] if g == 0 else None
                merge_group(span, tokens, g, last, *ins, *produced[:3], state_out, edges_out)
                if more:

                    @pl.when(is_first(2 * span))
                    def _():
                        out_ref, state_ref = produced[-2:]
                        emit_known(
                            range(EARLY), 0, more[:4], more[4], *produced[1:3], out_ref, [state_ref] + refs, lambda n: None
                        )

            results = list(call(kernel, "merge", operands + early, outs, emit_scratch if early else [], 4, 2**20))
            message[g], entering[g], rim[g] = results[:3]
            if not last:
                merged[g] = results[3]
            if g == 0:
                edges = results[3 if last else 4]
            if early:
                begun, begun_state = results[-2:]
        span *= 2

    out_type = pltpu.HBM((tokens, channels), BF16)
    pair = [[entering[g], rim[g]] for g in range(groups)]
    def kernel(own_edges, begun, begun_state, *refs):
        ins, refs = [refs[i * 6 : i * 6 + 6] for i in range(groups)], refs[groups * 6 :]
        out_hbm, out_refs, state, scratch = refs[0], refs[1 : 1 + groups], refs[1 + groups], refs[2 + groups : 6 + groups]

        @pl.when(is_early(span))
        def _():
            @pl.when(is_first(span))
            def _():
                out_refs[0][pl.ds(0, EARLY * CHUNK), :] = begun[pl.ds(0, EARLY * CHUNK), :]
                for m in range(modes):
                    state[m] = begun_state[m]

            @pl.when(jnp.logical_not(is_first(span)))
            def _():
                emit_known(range(EARLY), 0, ins[0][:4], own_edges, *ins[0][4:], out_refs[0], [state, *scratch], lambda n: None)

            for g in range(groups - 1):
                which = range(0 if g else EARLY, chunks)
                emit_known(which, g, ins[g][:4], own_edges, *ins[g][4:], out_refs[g], [state, *scratch], lambda n: None)

            def emit(out, piece_done):
                emit_known(range(chunks), groups - 1, ins[-1][:4], own_edges, *ins[-1][4:], out, [state, *scratch], piece_done)

            done = [(pl.ds(0, tokens), g, out_refs[g]) for g in range(groups - 1)]
            emit_out(emit, done, out_hbm, out_refs[-1], *refs[6 + groups :])

    def fixed_of():
        return [[*near[2 * g : 2 * g + 2], made[g][1], made[g][3]] for g in range(groups)]

    out = call(
        kernel, "early", [own_edges, begun, begun_state] + sum([f + p for f, p in zip(fixed_of(), pair)], []),
        [out_type], [half] * groups + [vectors(modes)] + emit_scratch + [dma((groups,)), dma((pieces,))],
        4, 40 * work, out_specs=[HB],
    )[0]
    near = near_all(lambda: jnp.logical_not(is_early(span)), [entering[-1]], [])
    fixed = fixed_of()
    halves = []
    for g in range(groups):
        final = g + 1 == groups
        operands = fixed[g] + [own_edges] + pair[g] + [edges, got[g], got[0]] + (halves + [out] if final else [])

        def kernel(*refs, g=g, final=final):
            ins, refs = refs[:10], refs[10:]
            if final:
                done, (_, out_hbm, out_ref, *scratch) = refs[: groups - 1], refs[groups - 1 :]
            else:
                out_ref, *scratch = refs

            @pl.when(jnp.logical_not(is_early(span)))
            def _():
                def emit(out, piece_done):
                    emit_merged(span, g, ins[:4], *ins[4:], out, scratch[:5], piece_done)

                if final:
                    ready = [(pl.ds(0, tokens), i, x) for i, x in enumerate(done)]
                    emit_out(emit, ready, out_hbm, out_ref, *scratch[5:])
                else:
                    emit(out_ref, lambda n: None)

        if not final:
            halves += call(kernel, "late", operands, [half], [vectors(modes)] + emit_scratch, 4, 20 * work)
    return call(
        kernel, "late", operands, [out_type],
        [half, vectors(modes)] + emit_scratch + [dma((groups,)), dma((pieces,))], 4, 20 * work,
        in_specs=[VM] * (len(operands) - 1) + [HB], out_specs=[HB], aliases={len(operands) - 1: 0},
    )[0]


def solution(mesh):
    in_specs = (
        P(("dp", "context"), None, "tensor"),
        P(None, None, "tensor"),
        P("tensor", None),
        P("tensor", None),
        P("tensor"),
    )
    out_specs = P(("dp", "context"), "tensor")
    return jax.shard_map(body, mesh=mesh, in_specs=in_specs, out_specs=out_specs, check_vma=False)
```

```python
import jax
import jax.numpy as jnp
from jax import lax
from jax.experimental import pallas as pl
from jax.experimental.pallas import tpu as pltpu
from jax.sharding import PartitionSpec as P

F32 = jnp.float32
BF16 = jnp.bfloat16
LANES = 128
SUB = 8
GROUP = LANES * SUB
CHUNK = 16
PIECE = 64
STRIDE = CHUNK + 1
EARLY = 2
HEAD = 4
TAIL = 6


def rounded(first, second):
    pair = jnp.concatenate([first, second], axis=0).astype(BF16).astype(F32)
    return pair[:SUB], pair[SUB:]


def total(values):
    values = list(values)
    while len(values) > 1:
        pairs = [values[i] + values[i + 1] for i in range(0, len(values) - 1, 2)]
        values = pairs + ([values[-1]] if len(values) % 2 else [])
    return values[0]


def columns(g):
    return pl.ds(g * GROUP, GROUP)


def turn_in(source, turned, start, g):
    for j in range(SUB):
        turned[pl.ds(j * STRIDE, CHUNK), :] = source[pl.ds(start, CHUNK), pl.ds(g * GROUP + j * LANES, LANES)].astype(F32)


def turn_rows(source, turned, rows, g):
    for j in range(SUB):
        turned[pl.ds(j * STRIDE, rows), :] = source[:, pl.ds(g * GROUP + j * LANES, LANES)]


def row(turned, i):
    return turned[pl.ds(i, SUB, stride=STRIDE), :]


def chunk_rows(c):
    return pl.multiple_of(c * CHUNK, CHUNK)


def pack(message_ref, rows):
    for i in range(message_ref.shape[0]):
        message_ref[i] = jnp.concatenate(rows[2 * i : 2 * i + 2], axis=0).astype(BF16)


def unpack(message_ref, first, count):
    rows = []
    for i in range(first // 2, (first + count) // 2):
        pair = message_ref[i].astype(F32)
        rows += [pair[:SUB], pair[SUB:]]
    return rows


def first_products(w, head, tail):
    features = []
    for s, rows in ((1, (tail[1], tail[4], head[0], head[2])), (2, (tail[2], tail[5], head[1], head[3]))):
        features.append([w[3 * s] * rows[2 + t] + w[3 * s + 1] * rows[1 + t] + w[3 * s + 2] * rows[t] for t in range(2)])
    return [(features[0][t] * features[1][t]).astype(BF16).astype(F32) for t in range(2)]


def first_terms(rate, products, steps):
    return jnp.exp((1.0 - steps) * rate) * products[0] + jnp.exp((2.0 - steps) * rate) * products[1]


def enter(tokens, span, rank, rate, w, head, other, other_tail, entering):
    right = (rank & span) != 0
    ahead = rank & (span - 1)
    steps = (tokens * ahead).astype(F32)
    products = first_products(w, head, other_tail)
    result = []
    for m, r in enumerate(rate):
        missing = jnp.where(ahead > 0, first_terms(r, products, jnp.maximum(steps, 2.0)), 0.0)
        result.append(jnp.where(right, entering[m] + jnp.exp(-steps * r) * other[m] + missing, entering[m]))
    return result


def table_parts(tables_ref):
    modes = (tables_ref.shape[0] - 10) // 2
    rate = [tables_ref[m] for m in range(modes)]
    return modes, rate, [tables_ref[modes + i] for i in range(9)]


def gain_row(modes, m):
    return modes + 9 + m


def state_kernel(
    g, rate_nat, taps_nat, residue_nat, bias_nat, natural,
    kv_ref, states_ref, own_ref, tables_ref, ka, kb, va, vb, wait_piece, wait_rest,
):
    q_nat, k_nat, v_nat = (natural.at[i] for i in range(3))
    tokens, modes = natural.shape[1], rate_nat.shape[0]
    chunks = tokens // CHUNK
    rank = lax.axis_index("context")
    zero = jnp.zeros((SUB, LANES), F32)
    turn_rows(rate_nat, ka, modes, g)
    for stream in range(3):
        turn_rows(taps_nat.at[stream], (kb, va, vb)[stream], 3, g)
    p = []
    for m in range(modes):
        rate = row(ka, m)
        tables_ref[m] = rate
        p.append(jnp.exp(-rate))
    w = []
    for i in range(9):
        w.append(row((kb, va, vb)[i // 3], i % 3))
        tables_ref[modes + i] = w[i]
    wk, wv = w[3:6], w[6:9]
    wait_piece(0)
    turn_in(k_nat, ka, 0, g)
    turn_in(v_nat, va, 0, g)
    def one_chunk(c, ks, vs, acc, last):
        k1, k2, v1, v2 = last
        for m in range(modes):
            states_ref[c, m] = acc[m]
        for i in range(0, CHUNK, 2):
            products = []
            for n in (i, i + 1):
                k, v = row(ks, n), row(vs, n)
                key = wk[0] * k + wk[1] * k1 + wk[2] * k2
                value = wv[0] * v + wv[1] * v1 + wv[2] * v2
                k1, k2, v1, v2 = k, k1, v, v1
                products.append(key * value)
            for n, product in enumerate(rounded(*products)):
                if i == 0:
                    product = jnp.where((c > 0) | (rank == 0), product, 0.0)
                kv_ref[c * CHUNK + i + n] = product
                acc = [a * b + product for a, b in zip(acc, p)]
        return acc, (k1, k2, v1, v2)

    def two_chunks(it, carry):
        acc, last = carry
        c = 2 * it
        pl.when(it == PIECE // (2 * CHUNK) - 1)(lambda: wait_piece(1))
        turn_in(k_nat, kb, chunk_rows(c + 1), g)
        turn_in(v_nat, vb, chunk_rows(c + 1), g)
        acc, last = one_chunk(c, ka, va, acc, last)
        ahead = chunk_rows(jnp.minimum(c + 2, chunks - 1))
        turn_in(k_nat, ka, ahead, g)
        turn_in(v_nat, va, ahead, g)
        return one_chunk(c + 1, kb, vb, acc, last)

    acc, _ = lax.fori_loop(0, chunks // 2, two_chunks, ([zero] * modes, (zero,) * 4))
    for m in range(modes):
        own_ref[m] = acc[m]
    wait_rest()
    turn_rows(residue_nat, ka, modes, g)
    for m in range(modes):
        tables_ref[gain_row(modes, m)] = row(ka, m)
    tables_ref[gain_row(modes, modes)] = bias_nat[g]


def edge_rows(natural, edges_ref, turned, g):
    tokens = natural.shape[1]
    for stream in range(3):
        turn_in(natural.at[stream], turned, tokens - CHUNK, g)
        for i in range(2):
            edges_ref[g, 3 * i + stream] = row(turned, CHUNK - 2 + i)
        if stream:
            turn_in(natural.at[stream], turned, 0, g)
            for i in range(2):
                edges_ref[g, TAIL + 2 * i + stream - 1] = row(turned, i)


def tails_and_heads(edges, heads):
    rows = sum([e[:TAIL] for e in edges], [])
    return rows + sum([e[TAIL:] for e in edges], []) if heads else rows


def other_edges(first_got, g, groups, modes, heads):
    tail = unpack(first_got, modes + TAIL * g, TAIL)
    return tail, unpack(first_got, modes + TAIL * groups + HEAD * g, HEAD) if heads else None


def first_states_kernel(
    streams, taps_hbm, rate_hbm, residue_hbm, bias_hbm,
    kv_ref, states_ref, own_ref, tables_ref, message_ref, edges_ref, rate_nat, taps_nat, residue_nat, bias_nat, natural,
    ka, kb, va, vb, table_sems, stream_sems,
):
    _, tokens, channels = natural.shape
    groups = channels // GROUP
    keys_values = pl.ds(1, 2)
    pieces = [
        fetch(streams, natural, stream_sems.at[0], keys_values, pl.ds(0, PIECE), columns(0)),
        fetch(streams, natural, stream_sems.at[1], keys_values, pl.ds(PIECE, tokens - PIECE), columns(0)),
    ]
    rest = other_inputs(streams, natural, stream_sems, 2)
    tables = [
        pltpu.make_async_copy(src, dst, table_sems.at[i])
        for i, (src, dst) in enumerate(
            [(rate_hbm, rate_nat), (taps_hbm, taps_nat), (residue_hbm, residue_nat), (bias_hbm, bias_nat)]
        )
    ]
    for copy in tables[:2] + pieces + tables[2:]:
        copy.start()

    def wait_rest():
        for copy in tables[2:] + rest:
            copy.wait()

    @pl.when(jnp.logical_not(is_last()))
    def _():
        for copy in rest:
            copy.start()
        for copy in tables[:2]:
            copy.wait()
        state_kernel(
            0, rate_nat, taps_nat, residue_nat, bias_nat, natural,
            kv_ref, states_ref, own_ref, tables_ref, ka, kb, va, vb, lambda n: pieces[n].wait(), wait_rest,
        )
        for g in range(groups):
            edge_rows(natural, edges_ref, ka, g)
        state = [own_ref[m] for m in range(own_ref.shape[0])]
        edges = [[edges_ref[g, i] for i in range(TAIL + HEAD)] for g in range(groups)]
        pack(message_ref, state + tails_and_heads(edges, True))

    @pl.when(is_last())
    def _():
        for copy in tables + pieces:
            copy.wait()
        message_ref[...] = jnp.zeros(message_ref.shape, BF16)


def fetch(streams, natural, sem, *where):
    return pltpu.make_async_copy(streams.at[where], natural.at[where], sem)


def other_inputs(streams, natural, sems, first):
    groups = natural.shape[2] // GROUP
    copies = [fetch(streams, natural, sems.at[first], pl.ds(0, 1), slice(None), columns(0))]
    for g in range(1, groups):
        copies.append(fetch(streams, natural, sems.at[first + g], slice(None), slice(None), columns(g)))
    return copies


def is_last():
    return lax.axis_index("context") == lax.axis_size("context") - 1


def later_states_kernel(g, inputs, before, own_edges, streams, sems, outs, scratch):
    def states(group, refs):
        state_kernel(group, *inputs, *refs, *scratch, lambda n: None, lambda: None)

    if outs:

        @pl.when(jnp.logical_not(is_last()))
        def _():
            states(g, outs[:4])
            pack(outs[4], [outs[2][m] for m in range(outs[2].shape[0])])

    @pl.when(is_last())
    def _():
        rest = other_inputs(streams, inputs[-1], sems, 0) if g == 1 else []
        for copy in rest:
            copy.start()
        states(g - 1, before)
        for copy in rest:
            copy.wait()
        if g == 1:
            for group in range(own_edges.shape[0]):
                edge_rows(inputs[-1], own_edges, scratch[0], group)
        if outs:
            outs[4][...] = jnp.zeros(outs[4].shape, BF16)


def near_group(g, q_nat, tables_ref, kv_ref, near_ref, query_ref, taps, qa, qb):
    tokens = kv_ref.shape[0]
    chunks = tokens // CHUNK
    zero = jnp.zeros((SUB, LANES), F32)
    modes, rate, w = table_parts(tables_ref)
    p = [jnp.exp(-r) for r in rate]
    gain = [tables_ref[gain_row(modes, m)] for m in range(modes)]
    taps[0] = total(gain) + tables_ref[gain_row(modes, modes)]
    for i in range(1, CHUNK):
        gain = [a * b for a, b in zip(gain, p)]
        taps[i] = total(gain)
    h = [taps[i] for i in range(CHUNK)]
    turn_in(q_nat, qa, 0, g)

    def one_chunk(c, qs, last):
        q1, q2 = last
        window = []
        for i in range(CHUNK):
            t = c * CHUNK + i
            q = row(qs, i)
            query_ref[t] = w[0] * q + w[1] * q1 + w[2] * q2
            q1, q2 = q, q1
            window.append(kv_ref[t])
            near_ref[t] = total(h[n] * window[i - n] for n in range(i + 1))
        return q1, q2

    def two_chunks(it, last):
        c = 2 * it
        turn_in(q_nat, qb, chunk_rows(c + 1), g)
        last = one_chunk(c, qa, last)
        turn_in(q_nat, qa, chunk_rows(jnp.minimum(c + 2, chunks - 1)), g)
        return one_chunk(c + 1, qb, last)

    lax.fori_loop(0, chunks // 2, two_chunks, (zero, zero))


def merge_group(
    span, tokens, g, last, own_ref, edges_ref, got_ref, first_got, tables_ref, entering_ref, rim_ref,
    message_ref, entering_out, rim_out, next_ref, edges_out,
):
    modes, rate, w = table_parts(tables_ref)
    groups = edges_ref.shape[0]
    rank = lax.axis_index("context")
    right = (rank & span) != 0
    ahead = rank & (span - 1)
    length = 1.0 * tokens * span
    zero = jnp.zeros((SUB, LANES), F32)

    def pick(a, b):
        return [jnp.where(right, x, y) for x, y in zip(a, b)]

    def edge(group):
        rows = [edges_ref[group, i] for i in range(TAIL + HEAD)]
        return rows[:TAIL], rows[TAIL:]

    state, other = [own_ref[m] for m in range(modes)], unpack(got_ref, 0, modes)
    tail, head = edge(g)
    other_tail, other_head = other_edges(first_got, g, groups, modes, True)
    products = first_products(w, pick(head, other_head), pick(other_tail, tail))
    left_state, right_state = pick(other, state), pick(state, other)
    rows = [
        right_state[m] + jnp.exp(-length * rate[m]) * left_state[m] + first_terms(rate[m], products, length)
        for m in range(modes)
    ]
    if not last:
        for m in range(modes):
            next_ref[m] = rows[m]
    if g == 0:
        edges = []
        for group in range(groups):
            mine, theirs = edge(group), other_edges(first_got, group, groups, modes, True)
            edges.append(pick(mine[0], theirs[0]) + pick(theirs[1], mine[1]))
            for i, value in enumerate(edges[-1]):
                edges_out[group, i] = value
        rows = rows + tails_and_heads(edges, not last)
    pack(message_ref, rows)
    entering = [zero if entering_ref is None else entering_ref[m] for m in range(modes)]
    entering = enter(tokens, span, rank, rate, w, head, other, other_tail, entering)
    for m in range(modes):
        entering_out[m] = entering[m]
    for i in range(TAIL):
        old = zero if rim_ref is None else rim_ref[i]
        rim_out[i] = jnp.where(right & (ahead == 0), other_tail[i], old)


def emit_group(
    which, near_ref, query_ref, states_ref, tables_ref, head, entering, rim, out_ref, state, power, rim_ref, ta, tb, piece_done
):
    rank = lax.axis_index("context")
    modes, rate, w = table_parts(tables_ref)
    p = [jnp.exp(-r) for r in rate]
    for m in range(modes):
        power[m] = jnp.exp(-CHUNK * rate[m])
    if which.start == 0:
        for m in range(modes):
            state[m] = entering[m]
        products = first_products(w, head, rim)
        for i in range(2):
            rim_ref[i] = jnp.where(rank == 0, 0.0, products[i])
        rim_ref[2] = w[1] * rim[3] + w[2] * rim[0]
        rim_ref[3] = w[2] * rim[3]

    def one_chunk(c, turned, first):
        x = [tables_ref[gain_row(modes, m)] * (states_ref[c, m] + state[m]) for m in range(modes)]
        for i in range(0, CHUNK, 2):
            queries, mixed = [], []
            for n in (i, i + 1):
                t = c * CHUNK + n
                x = [a * b for a, b in zip(x, p)]
                near, query = near_ref[t], query_ref[t]
                if first and n < 2:
                    x = [a + tables_ref[gain_row(modes, m)] * rim_ref[n] for m, a in enumerate(x)]
                    near = near + tables_ref[gain_row(modes, modes)] * rim_ref[n]
                    query = query + rim_ref[2 + n]
                queries.append(query)
                mixed.append(near + total(x))
            for n, value in enumerate(rounded(*mixed)):
                turned[pl.ds(i + n, SUB, stride=STRIDE), :] = queries[n] * value
        for m in range(modes):
            if first:
                held = (state[m] * p[m] + rim_ref[0]) * p[m] + rim_ref[1]
                state[m] = held * jnp.exp(-(CHUNK - 2) * tables_ref[m])
            else:
                state[m] = state[m] * power[m]

    def turn_out(turned, c):
        for j in range(SUB):
            out_ref[pl.ds(chunk_rows(c), CHUNK), pl.ds(j * LANES, LANES)] = turned[pl.ds(j * STRIDE, CHUNK), :].astype(BF16)

    begin = which.start
    one_chunk(begin, ta, begin == 0)
    one_chunk(begin + 1, tb, False)
    turn_out(ta, begin)

    def two_chunks(it, none):
        c = 2 * it
        one_chunk(c, ta, False)
        turn_out(tb, c - 1)
        one_chunk(c + 1, tb, False)
        turn_out(ta, c)
        pl.when((it & 1) == 0)(lambda: piece_done(it * 2 * CHUNK // PIECE - 1))
        return none

    lax.fori_loop(begin // 2 + 1, which.stop // 2, two_chunks, 0)
    turn_out(tb, which.stop - 1)
    piece_done(which.stop * CHUNK // PIECE - 1)


def emit_out(emit, ready, out_hbm, out_ref, ready_sems, sems):
    tokens, last = out_ref.shape[0], out_hbm.shape[1] // GROUP - 1
    copies = [
        pltpu.make_async_copy(buffer.at[rows], out_hbm.at[rows, columns(g)], ready_sems.at[i])
        for i, (rows, g, buffer) in enumerate(ready)
    ]
    for copy in copies:
        copy.start()

    def send(n):
        rows = pl.ds(pl.multiple_of(n * PIECE, PIECE), PIECE)
        return pltpu.make_async_copy(out_ref.at[rows], out_hbm.at[rows, columns(last)], sems.at[n])

    emit(out_ref, lambda n: send(n).start())
    for copy in copies + [send(n) for n in range(tokens // PIECE)]:
        copy.wait()


def is_early(span):
    return (lax.axis_index("context") & span) == 0


def is_first(span):
    rank = lax.axis_index("context")
    return is_early(span) & ((rank & (span // 2)) == 0)


def emit_known(which, g, fixed, edges_ref, entering_ref, rim_ref, out_ref, scratch, piece_done):
    entering = [entering_ref[m] for m in range(entering_ref.shape[0])]
    rim = [rim_ref[i] for i in range(TAIL)]
    head = [edges_ref[g, TAIL + i] for i in range(HEAD)]
    emit_group(which, *fixed, head, entering, rim, out_ref, *scratch, piece_done)


def emit_merged(span, g, fixed, edges_ref, entering_ref, rim_ref, merged_edges, got_ref, first_got, out_ref, scratch, piece_done):
    tokens, modes = fixed[0].shape[0], entering_ref.shape[0]
    rank = lax.axis_index("context")
    _, rate, w = table_parts(fixed[3])
    other_tail, _ = other_edges(first_got, g, edges_ref.shape[0], modes, False)
    entering = enter(
        tokens, span, rank, rate, w, [merged_edges[g, TAIL + i] for i in range(HEAD)],
        unpack(got_ref, 0, modes), other_tail, [entering_ref[m] for m in range(modes)],
    )
    begins = (rank & (span - 1)) == 0
    rim = [jnp.where(begins, other_tail[i], rim_ref[i]) for i in range(TAIL)]
    head = [edges_ref[g, TAIL + i] for i in range(HEAD)]
    emit_group(range(tokens // CHUNK), *fixed, head, entering, rim, out_ref, *scratch, piece_done)


VM = pl.BlockSpec(memory_space=pltpu.VMEM)
HB = pl.BlockSpec(memory_space=pltpu.HBM)


def call(kernel, name, operands, outs, scratch, mib, flops, in_specs=None, out_specs=None, aliases=None):
    in_specs = in_specs or [VM] * len(operands)
    operands = [
        pltpu.with_memory_space_constraint(x, pltpu.VMEM if spec is VM else pltpu.HBM) for x, spec in zip(operands, in_specs)
    ]
    return pl.pallas_call(
        kernel,
        in_specs=in_specs,
        out_specs=[VM] * len(outs) if out_specs is None else out_specs,
        out_shape=outs,
        scratch_shapes=scratch,
        input_output_aliases=aliases or {},
        compiler_params=pltpu.CompilerParams(vmem_limit_bytes=mib * 2**20),
        cost_estimate=pl.CostEstimate(flops=flops, bytes_accessed=2**20, transcendentals=0),
        name=name,
    )(*operands)


def body(streams, short_filter, decay_rate, residue, bias):
    tokens, _, channels = streams.shape
    modes = decay_rate.shape[1]
    groups = channels // GROUP
    chunks, pieces = tokens // CHUNK, tokens // PIECE
    size = lax.axis_size("context")
    vector = (SUB, LANES)
    turned = pltpu.VMEM(((SUB + 1) * STRIDE, LANES), F32)
    dma = pltpu.SemaphoreType.DMA
    work = tokens * channels

    def vectors(*shape):
        return pltpu.VMEM(shape + vector, F32)

    def message_type(count):
        return pltpu.VMEM((count // 2, 2 * SUB, LANES), BF16)

    def swap(message, span):
        return lax.ppermute(message, "context", [(i, i ^ span) for i in range(size)])

    edge = TAIL + HEAD
    state_types = [vectors(tokens), vectors(chunks, modes), vectors(modes), vectors(2 * modes + 10)]
    input_types = [
        pltpu.VMEM((modes, channels), F32), pltpu.VMEM((3, 3, channels), F32), pltpu.VMEM((modes, channels), F32),
        vectors(groups), pltpu.VMEM((3, tokens, channels), BF16),
    ]
    by_stream = streams.transpose(1, 0, 2)
    *first, first_message, own_edges, rates, taps, residues, biases, natural = call(
        first_states_kernel, "states",
        [by_stream, short_filter, decay_rate.T, residue.T, bias.reshape((groups,) + vector)],
        state_types + [message_type(modes + groups * edge), vectors(groups, edge)] + input_types,
        [turned] * 4 + [dma((4,)), dma((groups + 2,))], 4, 24 * work, in_specs=[HB] * 5,
    )
    made, message = [first], [first_message]
    def state_slot(g, after=()):
        nonlocal own_edges, natural
        held = made[-1] + ([own_edges, natural] if g == 1 else [])
        outs = state_types + [message_type(modes)] if g < groups else []
        ins = [rates, taps, residues, biases] + ([by_stream] if g == 1 else [natural])

        def kernel(*refs, g=g, count=len(held), fresh=len(outs)):
            ins, refs = refs[:5], refs[5 + count + len(after) :]
            before, outs, scratch = refs[:count], refs[count : count + fresh], refs[count + fresh :]
            if g == 1:
                later_states_kernel(g, ins[:4] + (before[5],), before[:4], before[4], ins[4], scratch[4], outs, scratch[:4])
            else:
                later_states_kernel(g, ins, before, None, None, None, outs, scratch)

        results = call(
            kernel, "states", ins + held + list(after),
            state_types + ([vectors(groups, edge), pltpu.VMEM((3, tokens, channels), BF16)] if g == 1 else []) + outs,
            [turned] * 4 + ([dma((groups,))] if g == 1 else []), 4, 24 * work,
            in_specs=[VM] * 4 + [HB if g == 1 else VM] + [VM] * (len(held) + len(after)), aliases={5 + i: i for i in range(len(held))},
        )
        made[-1] = list(results[:4])
        if g == 1:
            own_edges, natural = results[4:6]
        if outs:
            made.append(list(results[len(held) : len(held) + 4]))
            message.append(results[-1])
    for g in range(1, groups):
        state_slot(g)

    def near_all(condition, after, held):
        def kernel(*refs):
            natural, refs = refs[0], refs[1 + len(after) :]
            ins, refs = refs[: 2 * groups], refs[2 * groups + len(held) :]
            outs, scratch = refs[: 2 * groups], refs[2 * groups :]

            @pl.when(condition())
            def _():
                for g in range(groups):
                    near_group(g, natural.at[0], *ins[2 * g : 2 * g + 2], *outs[2 * g : 2 * g + 2], *scratch)

        operands = [natural] + after + sum([[made[g][3], made[g][0]] for g in range(groups)], [])
        outs = call(
            kernel, "near", operands + held, [vectors(tokens)] * (2 * groups), [vectors(CHUNK), turned, turned], 4, 24 * work,
            aliases={len(operands) + i: i for i in range(len(held))},
        )
        return list(outs)

    half = pltpu.VMEM((tokens, GROUP), BF16)
    emit_scratch = [vectors(modes), vectors(4), turned, turned]

    merged, edges = [m[2] for m in made], own_edges
    entering, rim = [None] * groups, [None] * groups
    span = 1
    while True:
        got = [swap(message[g], span) for g in range(groups)]
        if 2 * span >= size:
            break
        last, first = 4 * span >= size, entering[0] is None
        if first:
            near = near_all(lambda: is_first(size // 2), [], [])
        old_edges = edges
        for g in range(groups):
            if first and g == 1:
                state_slot(groups, [rim[0]])
                near = near_all(lambda: is_early(size // 2) & jnp.logical_not(is_first(size // 2)), [rim[0]], near)
            early = [*near[:2], made[0][1], made[0][3], own_edges] if last and g == 0 else []
            after = near[:1] if first and g == 1 else []
            operands = after + [merged[g], old_edges, got[g], got[0], made[g][3]] + ([] if first else [entering[g], rim[g]])
            count = modes + (groups * (TAIL if last else edge) if g == 0 else 0)
            outs = [message_type(count), vectors(modes), vectors(TAIL)]
            outs += [] if last else [vectors(modes)]
            outs += [vectors(groups, edge)] if g == 0 else []
            outs += [half, vectors(modes)] if early else []

            def kernel(*refs, g=g, span=span, last=last, first=first, counts=(len(early), len(outs)), skip=len(after)):
                refs = list(refs[skip:])
                ins = [refs.pop(0) for _ in range(5)] + ([None, None] if first else [refs.pop(0) for _ in range(2)])
                more, produced = ([refs.pop(0) for _ in range(n)] for n in counts)
                state_out = None if last else produced[3]
                edges_out = produced[3 if last else 4] if g == 0 else None
                merge_group(span, tokens, g, last, *ins, *produced[:3], state_out, edges_out)
                if more:

                    @pl.when(is_first(2 * span))
                    def _():
                        out_ref, state_ref = produced[-2:]
                        emit_known(
                            range(EARLY), 0, more[:4], more[4], *produced[1:3], out_ref, [state_ref] + refs, lambda n: None
                        )

            results = list(call(kernel, "merge", operands + early, outs, emit_scratch if early else [], 4, 2**20))
            message[g], entering[g], rim[g] = results[:3]
            if not last:
                merged[g] = results[3]
            if g == 0:
                edges = results[3 if last else 4]
            if early:
                begun, begun_state = results[-2:]
        span *= 2

    out_type = pltpu.HBM((tokens, channels), BF16)
    pair = [[entering[g], rim[g]] for g in range(groups)]
    def kernel(own_edges, begun, begun_state, *refs):
        ins, refs = [refs[i * 6 : i * 6 + 6] for i in range(groups)], refs[groups * 6 :]
        out_hbm, out_refs, state, scratch = refs[0], refs[1 : 1 + groups], refs[1 + groups], refs[2 + groups : 6 + groups]

        @pl.when(is_early(span))
        def _():
            @pl.when(is_first(span))
            def _():
                out_refs[0][pl.ds(0, EARLY * CHUNK), :] = begun[pl.ds(0, EARLY * CHUNK), :]
                for m in range(modes):
                    state[m] = begun_state[m]

            @pl.when(jnp.logical_not(is_first(span)))
            def _():
                emit_known(range(EARLY), 0, ins[0][:4], own_edges, *ins[0][4:], out_refs[0], [state, *scratch], lambda n: None)

            for g in range(groups - 1):
                which = range(0 if g else EARLY, chunks)
                emit_known(which, g, ins[g][:4], own_edges, *ins[g][4:], out_refs[g], [state, *scratch], lambda n: None)

            def emit(out, piece_done):
                emit_known(range(chunks), groups - 1, ins[-1][:4], own_edges, *ins[-1][4:], out, [state, *scratch], piece_done)

            done = [(pl.ds(0, tokens), g, out_refs[g]) for g in range(groups - 1)]
            emit_out(emit, done, out_hbm, out_refs[-1], *refs[6 + groups :])

    def fixed_of():
        return [[*near[2 * g : 2 * g + 2], made[g][1], made[g][3]] for g in range(groups)]

    out = call(
        kernel, "early", [own_edges, begun, begun_state] + sum([f + p for f, p in zip(fixed_of(), pair)], []),
        [out_type], [half] * groups + [vectors(modes)] + emit_scratch + [dma((groups,)), dma((pieces,))],
        4, 40 * work, out_specs=[HB],
    )[0]
    near = near_all(lambda: jnp.logical_not(is_early(span)), [entering[-1]], [])
    fixed = fixed_of()
    halves = []
    for g in range(groups):
        final = g + 1 == groups
        operands = fixed[g] + [own_edges] + pair[g] + [edges, got[g], got[0]] + (halves + [out] if final else [])

        def kernel(*refs, g=g, final=final):
            ins, refs = refs[:10], refs[10:]
            if final:
                done, (_, out_hbm, out_ref, *scratch) = refs[: groups - 1], refs[groups - 1 :]
            else:
                out_ref, *scratch = refs

            @pl.when(jnp.logical_not(is_early(span)))
            def _():
                def emit(out, piece_done):
                    emit_merged(span, g, ins[:4], *ins[4:], out, scratch[:5], piece_done)

                if final:
                    ready = [(pl.ds(0, tokens), i, x) for i, x in enumerate(done)]
                    emit_out(emit, ready, out_hbm, out_ref, *scratch[5:])
                else:
                    emit(out_ref, lambda n: None)

        if not final:
            halves += call(kernel, "late", operands, [half], [vectors(modes)] + emit_scratch, 4, 20 * work)
    return call(
        kernel, "late", operands, [out_type],
        [half, vectors(modes)] + emit_scratch + [dma((groups,)), dma((pieces,))], 4, 20 * work,
        in_specs=[VM] * (len(operands) - 1) + [HB], out_specs=[HB], aliases={len(operands) - 1: 0},
    )[0]


def solution(mesh):
    in_specs = (
        P(("dp", "context"), None, "tensor"),
        P(None, None, "tensor"),
        P("tensor", None),
        P("tensor", None),
        P("tensor"),
    )
    out_specs = P(("dp", "context"), "tensor")
    return jax.shard_map(body, mesh=mesh, in_specs=in_specs, out_specs=out_specs, check_vma=False)
```
